256 devices in a mesh: dp: 32 (over y, x, core), tensor: 8 (over z).
Axes of the slice: x: 4, y: 4, z: 8, core: 2. Of those that a mesh axis runs over, the one named last changes fastest.
Arguments:
- question_vectors: bfloat16 [64, 128, 8192], P('dp', None, 'tensor'), may hold values from -112 to 112
- arriving_lookup_vectors: bfloat16 [64, 128, 1024], P('dp', None, 'tensor'), may hold values from -4 to 4
- arriving_content_vectors: bfloat16 [64, 128, 1024], P('dp', None, 'tensor'), may hold values from -24 to 24
- earlier_lookup_store: bfloat16 [128, 512, 1024], P('dp', None, 'tensor'), may hold values from -6 to 6
- earlier_content_store: bfloat16 [128, 512, 1024], P('dp', None, 'tensor'), may hold values from -24 to 24
- stored_extent: int32 [128], P('dp'), may hold values from 1 to 512
- kept_parent: int32 [64], P('dp'), may hold values from 0 to 127, as said below
- final_projection_matrix: bfloat16 [8192, 8192], P('tensor', 'dp'), may hold values from -0.0625 to 0.0625
- skip_stream: bfloat16 [8192, 8192], P('dp', 'tensor'), may hold values from -3 to 3
Outputs:
- layer_out: bfloat16 [8192, 8192], P('dp', 'tensor')
The draws below stay inside these ranges and needn't reach their ends.
Inputs may be any that keep to these rules, and one draw needn't show every extreme that they name: `kept_parent`: no two values are equal. The 2 rows of one device continue trajectories cached on 2 different devices, and exactly 2 trajectories of each device survive.
All inputs are finite; a program needn't handle non-finite values.
Results may differ from the reference program's by a relative error of at most 0.018.
Values may be sent and summed in bfloat16 or wider, within the bound.
A program may use at most 128 MiB of HBM per device.

```python
import math
import jax
import jax.numpy as jnp
from jax import lax

D = 8192
HEADS = 64
KV_HEADS = 8
HEAD_DIM = 128
STRETCH = 128
CACHE = 512
ROWS_DEV = 2
SLOTS_DEV = 4
ROWS = 64
SLOTS = 128
TOKENS = 8192
N_TENSOR = 8


def key_base(key):
    return jax.random.truncated_normal(key, -4.0, 4.0, (ROWS, STRETCH, KV_HEADS * HEAD_DIM), jnp.float32)


def draw_arriving_lookup_vectors(key, part):
    base = key_base(key)
    return base.astype(jnp.bfloat16)


def draw_question_vectors(key, part):
    key = jax.random.fold_in(key, 12)
    fresh = 2.0 * jax.random.truncated_normal(key, -4.0, 4.0, (ROWS, STRETCH, HEADS * HEAD_DIM), jnp.float32)
    return fresh.astype(jnp.bfloat16)


def draw_stored_extent(key, part):
    key = jax.random.fold_in(key, 13)
    lengths = jax.random.randint(key, (SLOTS,), 1, CACHE + 1)
    return lengths.at[0].set(CACHE).astype(jnp.int32)


def draw_kept_parent(key, part):
    key = jax.random.fold_in(key, 14)
    order_key, anchor_key, offset_key, slot_key, rank_key = jax.random.split(key, 5)
    devices = SLOTS // SLOTS_DEV
    half = devices // 2
    places = jnp.arange(devices, dtype=jnp.int32)
    anchor = jax.random.randint(anchor_key, (), 0, devices).astype(jnp.int32)
    planted = jnp.stack([(anchor + 1) % devices, anchor, (anchor + half) % devices, (anchor + half + 1) % devices]).astype(jnp.int32)
    shuffled = jax.random.permutation(order_key, devices).astype(jnp.int32)
    position_of = jnp.zeros((devices,), jnp.int32).at[shuffled].set(places)
    match = places[:, None] == planted[None, :]
    planted_rank = jnp.sum(jnp.where(match, jnp.arange(4, dtype=jnp.int32)[None, :] - 4, 0), axis=1).astype(jnp.int32)
    priority = jnp.where(jnp.any(match, axis=1), planted_rank, position_of)
    cycle = jnp.argsort(priority, stable=True).astype(jnp.int32)
    where_in = jnp.zeros((devices,), jnp.int32).at[cycle].set(places)
    others = jax.random.permutation(offset_key, devices - 1).astype(jnp.int32)
    candidates = jnp.where(others == 0, 0, others + 1).astype(jnp.int32)
    offsets = jnp.concatenate([jnp.ones((1,), jnp.int32), candidates[:ROWS_DEV - 1]]).astype(jnp.int32)
    slot_keys = jax.random.split(slot_key, devices)
    slot_order = jax.vmap(lambda each_key: jax.random.permutation(each_key, SLOTS_DEV))(slot_keys).astype(jnp.int32)
    head_row = slot_order[0]
    slot_order = slot_order.at[0].set(jnp.roll(head_row, -jnp.argmax(head_row == 0)))
    tail_row = slot_order[devices - 1]
    slot_order = slot_order.at[devices - 1].set(jnp.roll(tail_row, -jnp.argmax(tail_row == SLOTS_DEV - 1)))
    rank_keys = jax.random.split(rank_key, devices)
    rank_pick = jax.vmap(lambda each_key: jax.random.permutation(each_key, ROWS_DEV))(rank_keys).astype(jnp.int32)
    sources = cycle[(where_in[:, None] + offsets[rank_pick]) % devices]
    slots = sources * SLOTS_DEV + slot_order[sources, rank_pick]
    return slots.reshape(-1).astype(jnp.int32)


def block_levels(stream_key, dims, pieces, least, high):
    loudness = 1.0
    for dim, shards_of in pieces:
        heights = jax.random.uniform(jax.random.fold_in(jax.random.fold_in(stream_key, 6), dim), (shards_of,), jnp.float32, least / len(pieces), high / len(pieces))
        loudness = loudness * jnp.repeat(jnp.exp(heights), dims[dim] // shards_of).reshape((-1,) + (1,) * (len(dims) - 1 - dim))
    return loudness


def centred(rng, shape, scale, bound, shards=(), held_as=jnp.bfloat16):
    values = jax.random.normal(rng, shape, jnp.float32) * scale
    if len(shards) > 0:
        values = block_levels(rng, shape, shards, -0.22, 0.18) * values
    return jnp.clip(values, min=-bound, max=bound).astype(held_as)


def setup_inputs(seed: int = 0) -> dict:
    arg_keys = jax.random.split(jax.random.key(seed), 10)
    return {
        "question_vectors": draw_question_vectors(jax.random.fold_in(arg_keys[9], 71), 0),
        "arriving_lookup_vectors": draw_arriving_lookup_vectors(jax.random.fold_in(arg_keys[9], 71), 0),
        "arriving_content_vectors": centred(arg_keys[2], (ROWS, STRETCH, KV_HEADS * HEAD_DIM), 4.0, 24.0, ((0, 32), (2, 8))),
        "earlier_lookup_store": centred(arg_keys[3], (SLOTS, CACHE, KV_HEADS * HEAD_DIM), 1.0, 6.0, ((0, 32), (2, 8))),
        "earlier_content_store": centred(arg_keys[4], (SLOTS, CACHE, KV_HEADS * HEAD_DIM), 4.0, 24.0, ((0, 32), (2, 8))),
        "stored_extent": draw_stored_extent(jax.random.fold_in(arg_keys[9], 71), 0),
        "kept_parent": draw_kept_parent(jax.random.fold_in(arg_keys[9], 71), 0),
        "final_projection_matrix": centred(arg_keys[7], (HEADS * HEAD_DIM, D), (HEADS * HEAD_DIM) ** -0.5, 0.0625, ((0, 8), (1, 32))),
        "skip_stream": centred(arg_keys[8], (TOKENS, D), 0.5, 3.0, ((0, 32), (1, 8))),
    }


def reference(question_vectors, arriving_lookup_vectors, arriving_content_vectors, earlier_lookup_store, earlier_content_store, stored_extent, kept_parent, final_projection_matrix, skip_stream):
    per_group = HEADS // KV_HEADS
    key_span = CACHE + STRETCH
    extent_each_line = stored_extent[kept_parent]

    def one_row(line_position):
        place_ordinal = kept_parent[line_position]
        query_all = question_vectors[line_position].astype(jnp.float32).reshape(STRETCH, KV_HEADS, per_group, HEAD_DIM)
        key_all = jnp.concatenate([earlier_lookup_store[place_ordinal], arriving_lookup_vectors[line_position]], axis=0)
        value_all = jnp.concatenate([earlier_content_store[place_ordinal], arriving_content_vectors[line_position]], axis=0)
        key_all = key_all.astype(jnp.float32).reshape(key_span, KV_HEADS, HEAD_DIM)
        value_all = value_all.astype(jnp.float32).reshape(key_span, KV_HEADS, HEAD_DIM)
        scores = jnp.einsum('cgqd,kgd->gqck', query_all, key_all) / math.sqrt(HEAD_DIM)
        position = jnp.arange(key_span)
        query_pos = jnp.arange(STRETCH)
        in_cache = position[None, :] < extent_each_line[line_position]
        in_stretch = position[None, :] - CACHE <= query_pos[:, None]
        allowed = jnp.where(position[None, :] < CACHE, in_cache, in_stretch)
        scores = jnp.where(allowed[None, None], scores, -jnp.inf)
        peak = lax.optimization_barrier(jnp.max(scores, axis=-1, keepdims=True))
        raised = jnp.exp(scores - peak)
        probs = (raised / lax.optimization_barrier(jnp.sum(raised, axis=-1, keepdims=True))).astype(jnp.bfloat16)
        mixed = jnp.einsum('gqck,kgd->cgqd', probs.astype(jnp.float32), value_all)
        return mixed.astype(jnp.bfloat16).reshape(STRETCH, HEADS * HEAD_DIM)
    attended = lax.map(one_row, jnp.arange(ROWS))
    flat = attended.reshape(ROWS * STRETCH, HEADS * HEAD_DIM)
    block = HEADS * HEAD_DIM // N_TENSOR
    total = jnp.zeros((ROWS * STRETCH, D), jnp.float32)
    for group_index in range(N_TENSOR):
        partial_sum = jnp.dot(flat[:, group_index * block:(group_index + 1) * block], final_projection_matrix[group_index * block:(group_index + 1) * block], preferred_element_type=jnp.float32)
        total = total + partial_sum.astype(jnp.bfloat16).astype(jnp.float32)
    return (skip_stream.astype(jnp.float32) + total).astype(jnp.bfloat16)
```

```python
import math

import jax
import jax.numpy as jnp
from jax import lax
from jax.experimental import pallas as pl
from jax.experimental.pallas import tpu as pltpu
from jax.sharding import PartitionSpec as P

HEAD_DIM = 128
STRETCH = 128
CACHE = 512


MESH = pl.DeviceIdType.MESH


def field(word, index):
    return jnp.bitwise_and(jnp.right_shift(jnp.int32(word), 2 * index), 3)


def packed(values):
    word = 0
    for place, value in enumerate(values):
        word |= value << (2 * place)
    if word >= 1 << 31:
        word -= 1 << 32
    return word


ORDER = [
    (0, 0), (1, 0), (3, 0), (0, 1), (0, 3), (1, 1), (1, 3), (3, 1), (3, 3),
    (2, 0), (0, 2), (2, 1), (2, 3), (1, 2), (3, 2), (2, 2),
]
EVENTS = [
    (0, 1, 0), (0, 3, 0), (1, 0, 1), (1, 0, 3), (1, 1, 0), (1, 3, 0), (0, 0, 1), (0, 0, 3),
    (0, 1, 1), (1, 1, 1), (0, 1, 3), (1, 1, 3), (0, 3, 1), (1, 3, 1), (0, 3, 3), (1, 3, 3),
    (0, 2, 0), (1, 0, 2), (1, 2, 0), (0, 0, 2), (0, 2, 1), (1, 2, 1), (0, 2, 3), (1, 2, 3),
    (1, 1, 2), (0, 1, 2), (1, 3, 2), (0, 3, 2), (0, 2, 2), (1, 2, 2),
]
ORDER_X = packed([o[0] for o in ORDER])
ORDER_Y = packed([o[1] for o in ORDER])
EVENT_TABLES = [
    (packed([e[k] for e in EVENTS[:15]]), packed([e[k] for e in EVENTS[15:]])) for k in range(3)
]


def event_field(k, index):
    low, high = EVENT_TABLES[k]
    return jnp.where(
        index < 15, field(low, jnp.minimum(index, 14)), field(high, jnp.maximum(index - 15, 0))
    )


UNITS = 32


def project_kernel(
    a_ref, w_ref, skip_ref, out_ref,
    a_buf, w_buf, p_buf, r_buf, x_buf,
    wrecv, wsend, rsem, ssem, asem, xsend, xrecv,
):
    dp = lax.axis_index("dp")
    z = lax.axis_index("tensor")
    core = lax.rem(dp, 2)
    chip = dp // 2
    x = lax.rem(chip, 4)
    y = chip // 4

    def dp_of(cx, cy, cc):
        return (lax.rem(cy + 4, 4) * 4 + lax.rem(cx + 4, 4)) * 2 + cc

    partner = (dp + 1 - 2 * core, z)

    def plane(axis, step):
        if isinstance(axis, int):
            return (dp_of(x + step, y, core) if axis == 0 else dp_of(x, y + step, core), z)
        return (
            dp_of(x + jnp.where(axis == 0, step, 0), y + jnp.where(axis == 0, 0, step), core),
            z,
        )

    barrier = pltpu.get_barrier_semaphore()
    around = [partner] + [plane(axis, step) for axis in (0, 1) for step in (1, 3)]
    around += [(dp, lax.rem(z + 1, 8)), (dp, lax.rem(z + 7, 8))]
    for other in around:
        pl.semaphore_signal(barrier, inc=1, device_id=other, device_id_type=MESH)
    pl.semaphore_wait(barrier, len(around))

    mine = [
        pltpu.make_async_remote_copy(
            src_ref=a_ref.at[pl.ds(u * 128, 128)],
            dst_ref=a_buf.at[u, pl.ds(pl.multiple_of(core * 128, 128), 128)],
            send_sem=asem.at[u],
            recv_sem=asem.at[2 + u],
            device_id=partner,
            device_id_type=MESH,
        )
        for u in range(2)
    ]
    for copy in mine:
        copy.start()

    own = y * 4 + x

    def send_half(src, block, half, axis, step):
        rows = pl.ds(pl.multiple_of(half * 512, 512), 512)
        pltpu.make_async_remote_copy(
            src_ref=src.at[rows],
            dst_ref=w_buf.at[block, rows],
            send_sem=wsend.at[axis, step // 2],
            recv_sem=wrecv.at[block, half],
            device_id=plane(axis, step),
            device_id_type=MESH,
        ).start()

    def send_quarter(block, half, axis, way):
        rows = pl.ds(pl.multiple_of(half * 512 + way * 256, 256), 256)
        pltpu.make_async_remote_copy(
            src_ref=w_buf.at[block, rows],
            dst_ref=w_buf.at[block, rows],
            send_sem=wsend.at[axis, way],
            recv_sem=wrecv.at[block, half],
            device_id=plane(axis, 1 + 2 * way),
            device_id_type=MESH,
        ).start()

    for phase in range(2):
        for half in range(2):
            for step in (1, 3):
                send_half(w_ref, own, half, half ^ phase, step)

    for u in range(2):
        a_buf[u, pl.ds(pl.multiple_of(core * 128, 128), 128), :] = a_ref[pl.ds(u * 128, 128), :]
    pltpu.make_async_copy(w_ref, w_buf.at[own], asem.at[4]).start()

    def block_at(dx, dy):
        bx = lax.rem(x - dx + 4, 4)
        by = lax.rem(y - dy + 4, 4)
        return bx, by, by * 4 + bx

    def arrival(event, carry):
        half = event_field(0, event)
        dx = event_field(1, event)
        dy = event_field(2, event)
        _, _, block = block_at(dx, dy)
        rows = pl.ds(pl.multiple_of(half * 512, 512), 512)
        landed = w_buf.at[block, rows]
        pltpu.make_async_copy(landed, landed, wrecv.at[block, half]).wait()
        near = jnp.where(half == 0, dx, dy)
        far = jnp.where(half == 0, dy, dx)
        second = 1 - half

        @pl.when(far == 0)
        def _():
            for step in (1, 3):
                send_half(w_buf.at[block], block, half, second, step)

        @pl.when((far == 0) & ((near == 1) | (near == 3)))
        def _():
            send_quarter(block, half, half, near // 2)

        @pl.when((far == 1) | (far == 3))
        def _():
            send_quarter(block, half, second, far // 2)

        return carry

    def events_by(i):
        return jnp.where(i < 1, 0, jnp.minimum(jnp.maximum(jnp.minimum(i + 3, 22), i), 30))

    def chain(i, lag, h):
        unit = i - 2 * lag
        stage = jnp.clip(unit // 2, 0, 15)
        u = lax.rem(unit + 64, 2)
        bx, by, _ = block_at(field(ORDER_X, stage), field(ORDER_Y, stage))
        goal = 2 * by + bx // 2
        d = lax.rem(goal - z + 8, 8)
        live = (unit >= 0) & (unit < UNITS)
        slot = jnp.clip(unit, 0, UNITS - 1)
        rows = pl.ds(h * 128, 128)
        if lag < 4:
            reach = 4 if h == 0 else 3
            down = jnp.where(d > reach, 1, 0)
            level = jnp.where(d > reach, d - reach - 1, reach - d)

            @pl.when(live & (d > 0) & (level == lag))
            def _():
                if lag > 0:
                    landed = r_buf.at[down, slot, rows]
                    pltpu.make_async_copy(landed, landed, rsem.at[down, slot, h]).wait()
                    p_buf[slot, rows, :] = (
                        p_buf[slot, rows, :].astype(jnp.float32)
                        + r_buf[down, slot, rows, :].astype(jnp.float32)
                    ).astype(jnp.bfloat16)
                pltpu.make_async_remote_copy(
                    src_ref=p_buf.at[slot, rows],
                    dst_ref=r_buf.at[down, slot, rows],
                    send_sem=ssem,
                    recv_sem=rsem.at[down, slot, h],
                    device_id=(dp, lax.rem(z + 1 + 6 * down, 8)),
                    device_id_type=MESH,
                ).start()
        else:
            k = lax.rem(bx, 2)

            @pl.when(live & (d == 0))
            def _():
                for way in range(2):
                    landed = r_buf.at[way, slot, rows]
                    pltpu.make_async_copy(landed, landed, rsem.at[way, slot, h]).wait()
                total = (
                    p_buf[slot, rows, :].astype(jnp.float32)
                    + r_buf[0, slot, rows, :].astype(jnp.float32)
                    + r_buf[1, slot, rows, :].astype(jnp.float32)
                )

                @pl.when(core == h)
                def _():
                    tokens = pl.ds(pl.multiple_of(u * 128, 128), 128)
                    columns = pl.ds(pl.multiple_of((2 * k + core) * 256, 256), 256)
                    out_ref[tokens, columns] = (
                        skip_ref[tokens, columns].astype(jnp.float32) + total
                    ).astype(jnp.bfloat16)

                @pl.when(core != h)
                def _():
                    p_buf[slot, rows, :] = total.astype(jnp.bfloat16)
                    pltpu.make_async_remote_copy(
                        src_ref=p_buf.at[slot, rows],
                        dst_ref=x_buf.at[k, u],
                        send_sem=xsend.at[k, u],
                        recv_sem=xrecv.at[k, u],
                        device_id=partner,
                        device_id_type=MESH,
                    ).start()

    def unit_step(i, carry):
        lax.fori_loop(events_by(i - 1), events_by(i), arrival, 0)

        @pl.when(i == 0)
        def _():
            pltpu.make_async_copy(w_ref, w_buf.at[own], asem.at[4]).wait()

        @pl.when(i < 2)
        def _():
            u = jnp.clip(i, 0, 1)
            landed = a_buf.at[u, pl.ds(pl.multiple_of((1 - core) * 128, 128), 128)]
            pltpu.make_async_copy(landed, landed, asem.at[2 + u]).wait()

        @pl.when(i < UNITS)
        def _():
            stage = jnp.clip(i // 2, 0, 15)
            _, _, block = block_at(field(ORDER_X, stage), field(ORDER_Y, stage))
            p_buf[jnp.clip(i, 0, UNITS - 1)] = jnp.dot(
                a_buf[lax.rem(i, 2)], w_buf[block], preferred_element_type=jnp.float32
            ).astype(jnp.bfloat16)

        for lag in range(5):
            for h in range(2):
                chain(i, lag, h)
        return carry

    lax.fori_loop(0, UNITS + 8, unit_step, 0)

    for k in range(2):
        for u in range(2):
            landed = x_buf.at[k, u]
            pltpu.make_async_copy(landed, landed, xrecv.at[k, u]).wait()
            tokens = pl.ds(u * 128, 128)
            columns = pl.ds(pl.multiple_of((2 * k + 1 - core) * 256, 256), 256)
            out_ref[tokens, columns] = (
                skip_ref[tokens, columns].astype(jnp.float32) + x_buf[k, u].astype(jnp.float32)
            ).astype(jnp.bfloat16)

    for u in range(2):
        mine[u].wait_send()
        for k in range(2):
            landed = x_buf.at[k, u]
            pltpu.make_async_copy(landed, landed, xsend.at[k, u]).wait()
    for axis in range(2):
        for way in range(2):
            sent = w_buf.at[pl.ds(0, 15), pl.ds(0, 256)]
            pltpu.make_async_copy(sent, sent, wsend.at[axis, way]).wait()
    sent = p_buf.at[pl.ds(0, 28)]
    pltpu.make_async_copy(sent, sent, ssem).wait()


def project(flat, weights, skip):
    vmem = pl.BlockSpec(memory_space=pltpu.VMEM)
    return pl.pallas_call(
        project_kernel,
        out_shape=jax.ShapeDtypeStruct(skip.shape, skip.dtype),
        in_specs=[vmem, vmem, vmem],
        out_specs=vmem,
        scratch_shapes=[
            pltpu.VMEM((2, 256, 1024), jnp.bfloat16),
            pltpu.VMEM((16, 1024, 256), jnp.bfloat16),
            pltpu.VMEM((UNITS, 256, 256), jnp.bfloat16),
            pltpu.VMEM((2, UNITS, 256, 256), jnp.bfloat16),
            pltpu.VMEM((2, 2, 128, 256), jnp.bfloat16),
            pltpu.SemaphoreType.DMA((16, 2)),
            pltpu.SemaphoreType.DMA((2, 2)),
            pltpu.SemaphoreType.DMA((2, UNITS, 2)),
            pltpu.SemaphoreType.DMA,
            pltpu.SemaphoreType.DMA((5,)),
            pltpu.SemaphoreType.DMA((2, 2)),
            pltpu.SemaphoreType.DMA((2, 2)),
        ],
        compiler_params=pltpu.CompilerParams(
            collective_id=1, has_side_effects=True, vmem_limit_bytes=48 * 1024 * 1024
        ),
        cost_estimate=pl.CostEstimate(
            flops=2 * 512 * 1024 * 4096, bytes_accessed=16 << 20, transcendentals=0
        ),
    )(flat, weights, skip)


def attend(
    question_vectors, arriving_lookup_vectors, arriving_content_vectors, keys_in, values_in, lengths
):
    tally_lines = question_vectors.shape[0]
    groups = arriving_lookup_vectors.shape[2] // HEAD_DIM
    head_count = question_vectors.shape[2] // HEAD_DIM
    per_group = head_count // groups
    key_span = CACHE + STRETCH
    query_all = question_vectors.reshape(tally_lines, STRETCH, groups, per_group, HEAD_DIM)
    key_all = jnp.concatenate([keys_in, arriving_lookup_vectors], axis=1).reshape(
        tally_lines, key_span, groups, HEAD_DIM
    )
    value_all = jnp.concatenate([values_in, arriving_content_vectors], axis=1).reshape(
        tally_lines, key_span, groups, HEAD_DIM
    )
    scores = jnp.einsum(
        "rcgqd,rkgd->rgqck", query_all, key_all, preferred_element_type=jnp.float32
    ) / math.sqrt(HEAD_DIM)
    position = jnp.arange(key_span)
    query_pos = jnp.arange(STRETCH)
    in_cache = position[None, None, :] < lengths[:, None, None]
    in_stretch = position[None, :] - CACHE <= query_pos[:, None]
    allowed = jnp.where(position[None, None, :] < CACHE, in_cache, in_stretch[None])
    scores = jnp.where(allowed[:, None, None], scores, -jnp.inf)
    peak = jnp.max(scores, axis=-1, keepdims=True)
    raised = jnp.exp(scores - peak)
    probs = (raised / jnp.sum(raised, axis=-1, keepdims=True)).astype(jnp.bfloat16)
    mixed = jnp.einsum("rgqck,rkgd->rcgqd", probs, value_all, preferred_element_type=jnp.float32)
    return mixed.astype(jnp.bfloat16).reshape(tally_lines, STRETCH, head_count * HEAD_DIM)


def local(
    question_vectors,
    arriving_lookup_vectors,
    arriving_content_vectors,
    earlier_lookup_store,
    earlier_content_store,
    stored_extent,
    kept_parent,
    final_projection_matrix,
    skip_stream,
):
    tally_places = earlier_lookup_store.shape[0]
    tally_lines = kept_parent.shape[0]
    dp_count = lax.axis_size("dp")
    device_rank_here = lax.axis_index("dp")
    kept_parent_shared, extent_gathered_all = (
        lax.all_gather(kept_parent, "dp", axis=0, tiled=True),
        lax.all_gather(stored_extent, "dp", axis=0, tiled=True),
    )
    sender_device = kept_parent_shared // tally_places
    device_place_shared = kept_parent_shared % tally_places
    device_lines_here = lax.dynamic_slice_in_dim(
        kept_parent_shared, device_rank_here * tally_lines, tally_lines
    )
    lengths = extent_gathered_all[device_lines_here]
    from_here = (sender_device == device_rank_here).reshape(dp_count, tally_lines)
    local_slot = device_place_shared.reshape(dp_count, tally_lines)
    picked = jnp.sum(jnp.where(from_here, local_slot, 0), axis=1)
    send_keys = earlier_lookup_store[picked]
    send_values = earlier_content_store[picked]
    recv_keys, recv_values = (
        lax.all_to_all(send_keys, "dp", split_axis=0, concat_axis=0, tiled=True),
        lax.all_to_all(send_values, "dp", split_axis=0, concat_axis=0, tiled=True),
    )
    my_sources = device_lines_here // tally_places
    keys_in = recv_keys[my_sources]
    values_in = recv_values[my_sources]
    attended = attend(
        question_vectors,
        arriving_lookup_vectors,
        arriving_content_vectors,
        keys_in,
        values_in,
        lengths,
    )
    flat = attended.reshape(tally_lines * STRETCH, attended.shape[2])
    return project(flat, final_projection_matrix, skip_stream)


def solution(mesh):
    return jax.shard_map(
        local,
        mesh=mesh,
        in_specs=(
            P("dp", None, "tensor"),
            P("dp", None, "tensor"),
            P("dp", None, "tensor"),
            P("dp", None, "tensor"),
            P("dp", None, "tensor"),
            P("dp"),
            P("dp"),
            P("tensor", "dp"),
            P("dp", "tensor"),
        ),
        out_specs=P("dp", "tensor"),
        check_vma=False,
    )
```

```python
import math

import jax
import jax.numpy as jnp
from jax import lax
from jax.experimental import pallas as pl
from jax.experimental.pallas import tpu as pltpu
from jax.sharding import PartitionSpec as P

HEAD_DIM = 128
STRETCH = 128
CACHE = 512


MESH = pl.DeviceIdType.MESH


def field(word, index):
    return jnp.bitwise_and(jnp.right_shift(jnp.int32(word), 2 * index), 3)


def packed(values):
    word = 0
    for place, value in enumerate(values):
        word |= value << (2 * place)
    if word >= 1 << 31:
        word -= 1 << 32
    return word


ORDER = [
    (0, 0), (1, 0), (3, 0), (0, 1), (0, 3), (1, 1), (1, 3), (3, 1), (3, 3),
    (2, 0), (0, 2), (2, 1), (2, 3), (1, 2), (3, 2), (2, 2),
]
EVENTS = [
    (0, 1, 0), (0, 3, 0), (1, 0, 1), (1, 0, 3), (1, 1, 0), (1, 3, 0), (0, 0, 1), (0, 0, 3),
    (0, 1, 1), (1, 1, 1), (0, 1, 3), (1, 1, 3), (0, 3, 1), (1, 3, 1), (0, 3, 3), (1, 3, 3),
    (0, 2, 0), (1, 0, 2), (1, 2, 0), (0, 0, 2), (0, 2, 1), (1, 2, 1), (0, 2, 3), (1, 2, 3),
    (1, 1, 2), (0, 1, 2), (1, 3, 2), (0, 3, 2), (0, 2, 2), (1, 2, 2),
]
ORDER_X = packed([o[0] for o in ORDER])
ORDER_Y = packed([o[1] for o in ORDER])
EVENT_TABLES = [
    (packed([e[k] for e in EVENTS[:15]]), packed([e[k] for e in EVENTS[15:]])) for k in range(3)
]


def event_field(k, index):
    low, high = EVENT_TABLES[k]
    return jnp.where(
        index < 15, field(low, jnp.minimum(index, 14)), field(high, jnp.maximum(index - 15, 0))
    )


UNITS = 32


def project_kernel(
    a_ref, w_ref, skip_ref, out_ref,
    a_buf, w_buf, p_buf, r_buf, x_buf,
    wrecv, wsend, rsem, ssem, asem, xsend, xrecv,
):
    dp = lax.axis_index("dp")
    z = lax.axis_index("tensor")
    core = lax.rem(dp, 2)
    chip = dp // 2
    x = lax.rem(chip, 4)
    y = chip // 4

    def dp_of(cx, cy, cc):
        return (lax.rem(cy + 4, 4) * 4 + lax.rem(cx + 4, 4)) * 2 + cc

    partner = (dp + 1 - 2 * core, z)

    def plane(axis, step):
        if isinstance(axis, int):
            return (dp_of(x + step, y, core) if axis == 0 else dp_of(x, y + step, core), z)
        return (
            dp_of(x + jnp.where(axis == 0, step, 0), y + jnp.where(axis == 0, 0, step), core),
            z,
        )

    barrier = pltpu.get_barrier_semaphore()
    around = [partner] + [plane(axis, step) for axis in (0, 1) for step in (1, 3)]
    around += [(dp, lax.rem(z + 1, 8)), (dp, lax.rem(z + 7, 8))]
    for other in around:
        pl.semaphore_signal(barrier, inc=1, device_id=other, device_id_type=MESH)
    pl.semaphore_wait(barrier, len(around))

    mine = [
        pltpu.make_async_remote_copy(
            src_ref=a_ref.at[pl.ds(u * 128, 128)],
            dst_ref=a_buf.at[u, pl.ds(pl.multiple_of(core * 128, 128), 128)],
            send_sem=asem.at[u],
            recv_sem=asem.at[2 + u],
            device_id=partner,
            device_id_type=MESH,
        )
        for u in range(2)
    ]
    for copy in mine:
        copy.start()

    own = y * 4 + x

    def send_half(src, block, half, axis, step):
        rows = pl.ds(pl.multiple_of(half * 512, 512), 512)
        pltpu.make_async_remote_copy(
            src_ref=src.at[rows],
            dst_ref=w_buf.at[block, rows],
            send_sem=wsend.at[axis, step // 2],
            recv_sem=wrecv.at[block, half],
            device_id=plane(axis, step),
            device_id_type=MESH,
        ).start()

    def send_quarter(block, half, axis, way):
        rows = pl.ds(pl.multiple_of(half * 512 + way * 256, 256), 256)
        pltpu.make_async_remote_copy(
            src_ref=w_buf.at[block, rows],
            dst_ref=w_buf.at[block, rows],
            send_sem=wsend.at[axis, way],
            recv_sem=wrecv.at[block, half],
            device_id=plane(axis, 1 + 2 * way),
            device_id_type=MESH,
        ).start()

    for phase in range(2):
        for half in range(2):
            for step in (1, 3):
                send_half(w_ref, own, half, half ^ phase, step)

    for u in range(2):
        a_buf[u, pl.ds(pl.multiple_of(core * 128, 128), 128), :] = a_ref[pl.ds(u * 128, 128), :]
    pltpu.make_async_copy(w_ref, w_buf.at[own], asem.at[4]).start()

    def block_at(dx, dy):
        bx = lax.rem(x - dx + 4, 4)
        by = lax.rem(y - dy + 4, 4)
        return bx, by, by * 4 + bx

    def arrival(event, carry):
        half = event_field(0, event)
        dx = event_field(1, event)
        dy = event_field(2, event)
        _, _, block = block_at(dx, dy)
        rows = pl.ds(pl.multiple_of(half * 512, 512), 512)
        landed = w_buf.at[block, rows]
        pltpu.make_async_copy(landed, landed, wrecv.at[block, half]).wait()
        near = jnp.where(half == 0, dx, dy)
        far = jnp.where(half == 0, dy, dx)
        second = 1 - half

        @pl.when(far == 0)
        def _():
            for step in (1, 3):
                send_half(w_buf.at[block], block, half, second, step)

        @pl.when((far == 0) & ((near == 1) | (near == 3)))
        def _():
            send_quarter(block, half, half, near // 2)

        @pl.when((far == 1) | (far == 3))
        def _():
            send_quarter(block, half, second, far // 2)

        return carry

    def events_by(i):
        return jnp.where(i < 1, 0, jnp.minimum(jnp.maximum(jnp.minimum(i + 3, 22), i), 30))

    def chain(i, lag, h):
        unit = i - 2 * lag
        stage = jnp.clip(unit // 2, 0, 15)
        u = lax.rem(unit + 64, 2)
        bx, by, _ = block_at(field(ORDER_X, stage), field(ORDER_Y, stage))
        goal = 2 * by + bx // 2
        d = lax.rem(goal - z + 8, 8)
        live = (unit >= 0) & (unit < UNITS)
        slot = jnp.clip(unit, 0, UNITS - 1)
        rows = pl.ds(h * 128, 128)
        if lag < 4:
            reach = 4 if h == 0 else 3
            down = jnp.where(d > reach, 1, 0)
            level = jnp.where(d > reach, d - reach - 1, reach - d)

            @pl.when(live & (d > 0) & (level == lag))
            def _():
                if lag > 0:
                    landed = r_buf.at[down, slot, rows]
                    pltpu.make_async_copy(landed, landed, rsem.at[down, slot, h]).wait()
                    p_buf[slot, rows, :] = (
                        p_buf[slot, rows, :].astype(jnp.float32)
                        + r_buf[down, slot, rows, :].astype(jnp.float32)
                    ).astype(jnp.bfloat16)
                pltpu.make_async_remote_copy(
                    src_ref=p_buf.at[slot, rows],
                    dst_ref=r_buf.at[down, slot, rows],
                    send_sem=ssem,
                    recv_sem=rsem.at[down, slot, h],
                    device_id=(dp, lax.rem(z + 1 + 6 * down, 8)),
                    device_id_type=MESH,
                ).start()
        else:
            k = lax.rem(bx, 2)

            @pl.when(live & (d == 0))
            def _():
                for way in range(2):
                    landed = r_buf.at[way, slot, rows]
                    pltpu.make_async_copy(landed, landed, rsem.at[way, slot, h]).wait()
                total = (
                    p_buf[slot, rows, :].astype(jnp.float32)
                    + r_buf[0, slot, rows, :].astype(jnp.float32)
                    + r_buf[1, slot, rows, :].astype(jnp.float32)
                )

                @pl.when(core == h)
                def _():
                    tokens = pl.ds(pl.multiple_of(u * 128, 128), 128)
                    columns = pl.ds(pl.multiple_of((2 * k + core) * 256, 256), 256)
                    out_ref[tokens, columns] = (
                        skip_ref[tokens, columns].astype(jnp.float32) + total
                    ).astype(jnp.bfloat16)

                @pl.when(core != h)
                def _():
                    p_buf[slot, rows, :] = total.astype(jnp.bfloat16)
                    pltpu.make_async_remote_copy(
                        src_ref=p_buf.at[slot, rows],
                        dst_ref=x_buf.at[k, u],
                        send_sem=xsend.at[k, u],
                        recv_sem=xrecv.at[k, u],
                        device_id=partner,
                        device_id_type=MESH,
                    ).start()

    def unit_step(i, carry):
        lax.fori_loop(events_by(i - 1), events_by(i), arrival, 0)

        @pl.when(i == 0)
        def _():
            pltpu.make_async_copy(w_ref, w_buf.at[own], asem.at[4]).wait()

        @pl.when(i < 2)
        def _():
            u = jnp.clip(i, 0, 1)
            landed = a_buf.at[u, pl.ds(pl.multiple_of((1 - core) * 128, 128), 128)]
            pltpu.make_async_copy(landed, landed, asem.at[2 + u]).wait()

        @pl.when(i < UNITS)
        def _():
            stage = jnp.clip(i // 2, 0, 15)
            _, _, block = block_at(field(ORDER_X, stage), field(ORDER_Y, stage))
            p_buf[jnp.clip(i, 0, UNITS - 1)] = jnp.dot(
                a_buf[lax.rem(i, 2)], w_buf[block], preferred_element_type=jnp.float32
            ).astype(jnp.bfloat16)

        for lag in range(5):
            for h in range(2):
                chain(i, lag, h)
        return carry

    lax.fori_loop(0, UNITS + 8, unit_step, 0)

    for k in range(2):
        for u in range(2):
            landed = x_buf.at[k, u]
            pltpu.make_async_copy(landed, landed, xrecv.at[k, u]).wait()
            tokens = pl.ds(u * 128, 128)
            columns = pl.ds(pl.multiple_of((2 * k + 1 - core) * 256, 256), 256)
            out_ref[tokens, columns] = (
                skip_ref[tokens, columns].astype(jnp.float32) + x_buf[k, u].astype(jnp.float32)
            ).astype(jnp.bfloat16)

    for u in range(2):
        mine[u].wait_send()
        for k in range(2):
            landed = x_buf.at[k, u]
            pltpu.make_async_copy(landed, landed, xsend.at[k, u]).wait()
    for axis in range(2):
        for way in range(2):
            sent = w_buf.at[pl.ds(0, 15), pl.ds(0, 256)]
            pltpu.make_async_copy(sent, sent, wsend.at[axis, way]).wait()
    sent = p_buf.at[pl.ds(0, 28)]
    pltpu.make_async_copy(sent, sent, ssem).wait()


def project(flat, weights, skip):
    vmem = pl.BlockSpec(memory_space=pltpu.VMEM)
    return pl.pallas_call(
        project_kernel,
        out_shape=jax.ShapeDtypeStruct(skip.shape, skip.dtype),
        in_specs=[vmem, vmem, vmem],
        out_specs=vmem,
        scratch_shapes=[
            pltpu.VMEM((2, 256, 1024), jnp.bfloat16),
            pltpu.VMEM((16, 1024, 256), jnp.bfloat16),
            pltpu.VMEM((UNITS, 256, 256), jnp.bfloat16),
            pltpu.VMEM((2, UNITS, 256, 256), jnp.bfloat16),
            pltpu.VMEM((2, 2, 128, 256), jnp.bfloat16),
            pltpu.SemaphoreType.DMA((16, 2)),
            pltpu.SemaphoreType.DMA((2, 2)),
            pltpu.SemaphoreType.DMA((2, UNITS, 2)),
            pltpu.SemaphoreType.DMA,
            pltpu.SemaphoreType.DMA((5,)),
            pltpu.SemaphoreType.DMA((2, 2)),
            pltpu.SemaphoreType.DMA((2, 2)),
        ],
        compiler_params=pltpu.CompilerParams(
            collective_id=1, has_side_effects=True, vmem_limit_bytes=48 * 1024 * 1024
        ),
        cost_estimate=pl.CostEstimate(
            flops=2 * 512 * 1024 * 4096, bytes_accessed=16 << 20, transcendentals=0
        ),
    )(flat, weights, skip)


def spots():
    dp = lax.axis_index("dp")
    core = lax.rem(dp, 2)
    chip = dp // 2
    return dp, lax.axis_index("tensor"), core, lax.rem(chip, 4), chip // 4


def table_kernel(mine_ref, out_ref, landing, send_sem, recv_sem):
    dp, z, _, _, _ = spots()
    barrier = pltpu.get_barrier_semaphore()

    def greet(step, carry):
        pl.semaphore_signal(
            barrier, inc=1, device_id=(lax.rem(dp + step, 32), z), device_id_type=MESH
        )
        return carry

    lax.fori_loop(1, 32, greet, 0)
    landing[dp] = mine_ref[...]
    pl.semaphore_wait(barrier, 31)

    def send(step, carry):
        pltpu.make_async_remote_copy(
            src_ref=mine_ref,
            dst_ref=landing.at[dp],
            send_sem=send_sem,
            recv_sem=recv_sem,
            device_id=(lax.rem(dp + step, 32), z),
            device_id_type=MESH,
        ).start()
        return carry

    lax.fori_loop(1, 32, send, 0)
    all_of_them = landing.at[pl.ds(0, 31)]
    pltpu.make_async_copy(all_of_them, all_of_them, recv_sem).wait()
    pltpu.make_async_copy(all_of_them, all_of_them, send_sem).wait()

    table = landing[:, 0, :]
    lane = lax.broadcasted_iota(jnp.int32, (32, 128), 1)
    line = lax.broadcasted_iota(jnp.int32, (32, 128), 0)

    def column(k):
        return jnp.sum(jnp.where(lane == k, table, 0), axis=1, keepdims=True)

    parents = [column(0), column(1)]
    rows = [
        jnp.sum(jnp.where(lane == line, parent, 0), axis=0, keepdims=True) for parent in parents
    ]
    result = jnp.zeros((32, 128), jnp.int32)
    low = jnp.full((1, 1), 9, jnp.int32)
    high = jnp.full((1, 1), -1, jnp.int32)
    for i in range(2):
        before = jnp.zeros((32, 1), jnp.int32)
        for row in rows:
            same = jnp.right_shift(row, 2) == jnp.right_shift(parents[i], 2)
            hit = same & (row < parents[i]) & (lane < 32)
            before += jnp.sum(jnp.where(hit, 1, 0), axis=1, keepdims=True)
        code = jnp.right_shift(parents[i], 2) * 2 + before
        result = jnp.where(lane == i, code, result)
        here = jnp.right_shift(parents[i], 2) == dp
        slot = jnp.bitwise_and(parents[i], 3)
        low = jnp.minimum(low, jnp.min(jnp.where(here, slot, 9), axis=0, keepdims=True))
        high = jnp.maximum(high, jnp.max(jnp.where(here, slot, -1), axis=0, keepdims=True))
        wanted = jnp.sum(
            jnp.where(line[:, :1] == dp, parents[i], 0), axis=0, keepdims=True
        )
        found = (lane >= 2) & (lane < 6) & (line * 4 + lane - 2 == wanted)
        extent = jnp.sum(
            jnp.sum(jnp.where(found, table, 0), axis=0, keepdims=True), axis=1, keepdims=True
        )
        result = jnp.where(lane == 4 + i, extent, result)
    result = jnp.where(lane == 2, low, result)
    result = jnp.where(lane == 3, high, result)
    out_ref[...] = result


def make_table(kept_parent, stored_extent):
    mine = jnp.concatenate([kept_parent, stored_extent])
    mine = jnp.broadcast_to(jnp.pad(mine, (0, 122))[None], (8, 128))
    vmem = pl.BlockSpec(memory_space=pltpu.VMEM)
    return pl.pallas_call(
        table_kernel,
        out_shape=jax.ShapeDtypeStruct((32, 128), jnp.int32),
        in_specs=[vmem],
        out_specs=vmem,
        scratch_shapes=[
            pltpu.VMEM((32, 8, 128), jnp.int32),
            pltpu.SemaphoreType.DMA,
            pltpu.SemaphoreType.DMA,
        ],
        compiler_params=pltpu.CompilerParams(collective_id=2, has_side_effects=True),
    )(mine)


def route_kernel(
    tab, k_ref, v_ref, kout, vout,
    picked, gk, gv, s1, r1, s2, r2, fin, xin,
    psend, precv, asend, arecv, fsend, frecv, s1s, s1r, s2s, s2r, xs, xr,
):
    dp, z, core, x, y = spots()
    partner = (dp + 1 - 2 * core, z)
    stores = (k_ref, v_ref)
    outs = (kout, vout)
    gathered = (gk, gv)
    first_at = (x, y)
    second_at = (y, x)

    def at(kv, which, step):
        along_x = (which == 0) == (kv == 0)
        nx = lax.rem(x + step, 4) if along_x else x
        ny = y if along_x else lax.rem(y + step, 4)
        return ((ny * 4 + nx) * 2 + core, z)

    def copy(src, dst, send, recv, target):
        return pltpu.make_async_remote_copy(
            src_ref=src, dst_ref=dst, send_sem=send, recv_sem=recv,
            device_id=target, device_id_type=MESH,
        )

    def wait(ref, sem):
        pltpu.make_async_copy(ref, ref, sem).wait()

    barrier = pltpu.get_barrier_semaphore()
    around = [partner] + [at(0, which, step) for which in range(2) for step in (1, 3)]
    for other in around:
        pl.semaphore_signal(barrier, inc=1, device_id=other, device_id_type=MESH)

    mine_rows = pl.ds(pl.multiple_of(core * 256, 256), 256)
    other_rows = pl.ds(pl.multiple_of((1 - core) * 256, 256), 256)
    for kv in range(2):
        for i in range(2):
            picked[kv, i] = stores[kv][tab[0, 2 + i]]
            gathered[kv][first_at[kv], core * 2 + i] = picked[kv, i, mine_rows, :]
    pl.semaphore_wait(barrier, len(around))
    swaps = []
    for kv in range(2):
        swaps.append(
            copy(
                picked.at[kv, pl.ds(0, 2), other_rows],
                gathered[kv].at[first_at[kv], pl.ds(pl.multiple_of(core * 2, 2), 2)],
                psend.at[kv], precv.at[kv], partner,
            )
        )
        swaps[-1].start()

    def pair(kv, place, half):
        return gathered[kv].at[place, pl.ds(2 * half, 2)]

    started = []
    for kv in range(2):
        mine = gathered[kv].at[first_at[kv], pl.ds(pl.multiple_of((1 - core) * 2, 2), 2)]
        wait(mine, precv.at[kv])
        for turn in range(2):
            for way in range(2):
                half = turn ^ way
                block = pair(kv, first_at[kv], half)
                started.append(
                    copy(
                        block, block, asend.at[kv, way, half], arecv.at[kv, way, half],
                        at(kv, 0, 1 + 2 * way),
                    )
                )
                started[-1].start()
    for kv in range(2):
        for way in range(2):
            place = lax.rem(first_at[kv] + (3 if way == 0 else 1), 4)
            block = pair(kv, place, way)
            wait(block, arecv.at[kv, way, way])
            started.append(
                copy(block, block, fsend.at[kv, way], frecv.at[kv, way], at(kv, 0, 1 + 2 * way))
            )
            started[-1].start()
    for kv in range(2):
        for way in range(2):
            place = lax.rem(first_at[kv] + (3 if way == 0 else 1), 4)
            wait(pair(kv, place, 1 - way), arecv.at[kv, way, 1 - way])
        for way in range(2):
            wait(pair(kv, lax.rem(first_at[kv] + 2, 4), way), frecv.at[kv, way])

    def candidate(kv, step, slot):
        to = lax.rem(second_at[kv] + step, 4)
        chip = to * 4 + x if kv == 0 else y * 4 + to
        code = tab[chip * 2 + slot // 2, slot % 2]
        rank = jnp.bitwise_and(code, 1)
        source_core = jnp.bitwise_and(jnp.right_shift(code, 1), 1)
        source_x = jnp.bitwise_and(jnp.right_shift(code, 2), 3)
        source_y = jnp.right_shift(code, 4)
        one, two = (source_x, source_y) if kv == 0 else (source_y, source_x)
        return gathered[kv][one, source_core * 2 + rank], two

    for kv in range(2):
        for way in range(2):
            for j in range(2):
                s1[kv, way, j] = candidate(kv, 2, 2 * way + j)[0]
            started.append(
                copy(
                    s1.at[kv, way], r1.at[kv, way], s1s.at[kv, way], s1r.at[kv, way],
                    at(kv, 1, 1 + 2 * way),
                )
            )
            started[-1].start()
    for turn in range(2):
        for kv in range(2):
            for way in range(2):
                half = 1 - way if turn == 0 else way
                if turn == 1:
                    wait(r1.at[kv, way], s1r.at[kv, way])
                for j in range(2):
                    slot = 2 * half + j
                    value, two = candidate(kv, 1 + 2 * way, slot)
                    if turn == 1:
                        value = jnp.where(two == second_at[kv], value, r1[kv, way, j])
                    s2[kv, way, slot] = value
                started.append(
                    copy(
                        s2.at[kv, way, pl.ds(2 * half, 2)], r2.at[kv, way, pl.ds(2 * half, 2)],
                        s2s.at[kv, way, half], s2r.at[kv, way, half], at(kv, 1, 1 + 2 * way),
                    )
                )
                started[-1].start()
    for kv in range(2):
        for half in range(2):
            for way in range(2):
                wait(r2.at[kv, way, pl.ds(2 * half, 2)], s2r.at[kv, way, half])
            for j in range(2):
                slot = 2 * half + j
                value, two = candidate(kv, 0, slot)
                here = second_at[kv]
                away = lax.rem(two - here + 4, 4)
                first = (away == 3) | (away == 2) if half == 0 else away == 3
                arrived = jnp.where(first, r2[kv, 0, slot], r2[kv, 1, slot])
                fin[kv, slot] = jnp.where(away == 0, value, arrived)
        theirs = fin.at[kv, pl.ds(pl.multiple_of((1 - core) * 2, 2), 2)]
        started.append(copy(theirs, xin.at[kv], xs.at[kv], xr.at[kv], partner))
        started[-1].start()
        for i in range(2):
            outs[kv][i, mine_rows, :] = fin[kv, core * 2 + i]
    for kv in range(2):
        wait(xin.at[kv], xr.at[kv])
        for i in range(2):
            outs[kv][i, other_rows, :] = xin[kv, i]
    for each in swaps + started:
        each.wait_send()


def route(table, keys, values):
    vmem = pl.BlockSpec(memory_space=pltpu.VMEM)
    item = (256, 128)
    bf16 = jnp.bfloat16
    dma = pltpu.SemaphoreType.DMA
    return pl.pallas_call(
        route_kernel,
        out_shape=[jax.ShapeDtypeStruct((2, 512, 128), bf16)] * 2,
        in_specs=[pl.BlockSpec(memory_space=pltpu.SMEM), vmem, vmem],
        out_specs=[vmem, vmem],
        scratch_shapes=[
            pltpu.VMEM((2, 2, 512, 128), bf16),
            pltpu.VMEM((4, 4) + item, bf16),
            pltpu.VMEM((4, 4) + item, bf16),
            pltpu.VMEM((2, 2, 2) + item, bf16),
            pltpu.VMEM((2, 2, 2) + item, bf16),
            pltpu.VMEM((2, 2, 4) + item, bf16),
            pltpu.VMEM((2, 2, 4) + item, bf16),
            pltpu.VMEM((2, 4) + item, bf16),
            pltpu.VMEM((2, 2) + item, bf16),
            dma((2,)), dma((2,)),
            dma((2, 2, 2)), dma((2, 2, 2)),
            dma((2, 2)), dma((2, 2)),
            dma((2, 2)), dma((2, 2)),
            dma((2, 2, 2)), dma((2, 2, 2)),
            dma((2,)), dma((2,)),
        ],
        compiler_params=pltpu.CompilerParams(
            collective_id=3, has_side_effects=True, vmem_limit_bytes=40 * 1024 * 1024
        ),
    )(table, keys, values)


def attend(
    question_vectors, arriving_lookup_vectors, arriving_content_vectors, keys_in, values_in, lengths
):
    tally_lines = question_vectors.shape[0]
    groups = arriving_lookup_vectors.shape[2] // HEAD_DIM
    head_count = question_vectors.shape[2] // HEAD_DIM
    per_group = head_count // groups
    key_span = CACHE + STRETCH
    query_all = question_vectors.reshape(tally_lines, STRETCH, groups, per_group, HEAD_DIM)
    key_all = jnp.concatenate([keys_in, arriving_lookup_vectors], axis=1).reshape(
        tally_lines, key_span, groups, HEAD_DIM
    )
    value_all = jnp.concatenate([values_in, arriving_content_vectors], axis=1).reshape(
        tally_lines, key_span, groups, HEAD_DIM
    )
    scores = jnp.einsum(
        "rcgqd,rkgd->rgqck", query_all, key_all, preferred_element_type=jnp.float32
    ) / math.sqrt(HEAD_DIM)
    position = jnp.arange(key_span)
    query_pos = jnp.arange(STRETCH)
    in_cache = position[None, None, :] < lengths[:, None, None]
    in_stretch = position[None, :] - CACHE <= query_pos[:, None]
    allowed = jnp.where(position[None, None, :] < CACHE, in_cache, in_stretch[None])
    scores = jnp.where(allowed[:, None, None], scores, -jnp.inf)
    peak = jnp.max(scores, axis=-1, keepdims=True)
    raised = jnp.exp(scores - peak)
    probs = (raised / jnp.sum(raised, axis=-1, keepdims=True)).astype(jnp.bfloat16)
    mixed = jnp.einsum("rgqck,rkgd->rcgqd", probs, value_all, preferred_element_type=jnp.float32)
    return mixed.astype(jnp.bfloat16).reshape(tally_lines, STRETCH, head_count * HEAD_DIM)


def local(
    question_vectors,
    arriving_lookup_vectors,
    arriving_content_vectors,
    earlier_lookup_store,
    earlier_content_store,
    stored_extent,
    kept_parent,
    final_projection_matrix,
    skip_stream,
):
    table = make_table(kept_parent, stored_extent)
    keys_in, values_in = route(table, earlier_lookup_store, earlier_content_store)
    lengths = table[0, 4:6]
    attended = attend(
        question_vectors,
        arriving_lookup_vectors,
        arriving_content_vectors,
        keys_in,
        values_in,
        lengths,
    )
    flat = attended.reshape(attended.shape[0] * STRETCH, attended.shape[2])
    return project(flat, final_projection_matrix, skip_stream)


def solution(mesh):
    return jax.shard_map(
        local,
        mesh=mesh,
        in_specs=(
            P("dp", None, "tensor"),
            P("dp", None, "tensor"),
            P("dp", None, "tensor"),
            P("dp", None, "tensor"),
            P("dp", None, "tensor"),
            P("dp"),
            P("dp"),
            P("tensor", "dp"),
            P("dp", "tensor"),
        ),
        out_specs=P("dp", "tensor"),
        check_vma=False,
    )
```

```python
import math

import jax
import jax.numpy as jnp
from jax import lax
from jax.experimental import pallas as pl
from jax.experimental.pallas import tpu as pltpu
from jax.sharding import PartitionSpec as P

HEAD_DIM = 128
STRETCH = 128
CACHE = 512


MESH = pl.DeviceIdType.MESH
NEAR = [(1, 0), (3, 0), (0, 1), (0, 3)]
DIAGONAL = [(1, 1), (1, 3), (3, 1), (3, 3)]
FAR = [(2, 0), (0, 2), (2, 1), (2, 3), (1, 2), (3, 2), (2, 2)]


def spots():
    dp = lax.axis_index("dp")
    core = lax.rem(dp, 2)
    chip = dp // 2
    return dp, lax.axis_index("tensor"), core, lax.rem(chip, 4), chip // 4


def beside(axis, way):
    dp, z, core, x, y = spots()
    step = 1 + 2 * way
    nx = lax.rem(x + step, 4) if axis == 0 else x
    ny = y if axis == 0 else lax.rem(y + step, 4)
    return ((ny * 4 + nx) * 2 + core, z)


def wait_for(ref, sem):
    pltpu.make_async_copy(ref, ref, sem).wait()


def project_kernel(
    a_ref, own_ref, near_ref, diagonal_ref, far_ref, skip_ref, out_ref,
    a_buf, w_buf, s_buf, r_buf, t_buf, x_buf,
    rsem, ssem, asem, lsem, xsend, xrecv,
):
    dp, z, core, x, y = spots()
    partner = (dp + 1 - 2 * core, z)
    barrier = pltpu.get_barrier_semaphore()
    around = [partner, (dp, lax.rem(z + 1, 8)), (dp, lax.rem(z + 7, 8))]
    for other in around:
        pl.semaphore_signal(barrier, inc=1, device_id=other, device_id_type=MESH)

    sources = [((0, 0), own_ref)]
    for group, ref in ((NEAR, near_ref), (DIAGONAL, diagonal_ref), (FAR, far_ref)):
        sources += [(place, ref.at[k]) for k, place in enumerate(group)]
    loads = [
        pltpu.make_async_copy(ref, w_buf.at[dy * 4 + dx], lsem.at[dy * 4 + dx])
        for (dx, dy), ref in sources
    ]
    for load in loads:
        load.start()
    pl.semaphore_wait(barrier, len(around))
    exchange = pltpu.make_async_remote_copy(
        src_ref=a_ref, dst_ref=a_buf.at[core], send_sem=asem.at[0], recv_sem=asem.at[1],
        device_id=partner, device_id_type=MESH,
    )
    exchange.start()
    a_buf[core] = a_ref[...]
    for load in loads:
        load.wait()

    def product(d, h, k):
        goal = lax.rem(z + d, 8)
        dx = lax.rem(x - 2 * lax.rem(goal, 2) - k + 4, 4)
        dy = lax.rem(y - goal // 2 + 4, 4)
        return jnp.dot(a_buf[h], w_buf[dy * 4 + dx], preferred_element_type=jnp.float32)

    def step(s, carry):
        for turn in range(2):
            h = lax.rem(core + turn, 2)
            if turn == 1:

                @pl.when(s == 0)
                def _():
                    wait_for(a_buf.at[1 - core], asem.at[1])

            for k in range(2):
                for way in range(2):
                    d = 4 - s - h if way == 0 else 4 + s + 1 - h

                    @pl.when((d > 0) & (d < 8))
                    def _():
                        value = product(d, h, k)
                        place = ((s * 2 + k) * 2 + way) * 2 + h

                        @pl.when(s == 0)
                        def _():
                            s_buf[place] = value.astype(jnp.bfloat16)

                        @pl.when(s > 0)
                        def _():
                            before = jnp.maximum(s - 1, 0)
                            wait_for(r_buf.at[before, k, way, h], rsem.at[before, k, way, h])
                            s_buf[place] = (
                                value + r_buf[before, k, way, h].astype(jnp.float32)
                            ).astype(jnp.bfloat16)

                        pltpu.make_async_remote_copy(
                            src_ref=s_buf.at[place],
                            dst_ref=r_buf.at[s, k, way, h],
                            send_sem=ssem,
                            recv_sem=rsem.at[s, k, way, h],
                            device_id=(dp, lax.rem(z + 1 + 6 * way, 8)),
                            device_id_type=MESH,
                        ).start()
        return carry

    lax.fori_loop(0, 4, step, 0)

    def total(h, k):
        for way, last in ((0, 3 - h), (1, 2 + h)):
            wait_for(r_buf.at[last, k, way, h], rsem.at[last, k, way, h])
        return (
            t_buf[h, k]
            + r_buf[3 - h, k, 0, h].astype(jnp.float32)
            + r_buf[2 + h, k, 1, h].astype(jnp.float32)
        )

    for h in range(2):
        for k in range(2):
            t_buf[h, k] = product(0, h, k)
    sent = []
    for k in range(2):
        x_buf[0, k] = total(1 - core, k).astype(jnp.bfloat16)
        sent.append(
            pltpu.make_async_remote_copy(
                src_ref=x_buf.at[0, k], dst_ref=x_buf.at[1, k],
                send_sem=xsend.at[k], recv_sem=xrecv.at[k],
                device_id=partner, device_id_type=MESH,
            )
        )
        sent[-1].start()
    for k in range(2):
        columns = pl.ds(pl.multiple_of((2 * k + core) * 256, 256), 256)
        out_ref[:, columns] = (
            skip_ref[:, columns].astype(jnp.float32) + total(core, k)
        ).astype(jnp.bfloat16)
    for k in range(2):
        sent[k].wait_recv()
        columns = pl.ds(pl.multiple_of((2 * k + 1 - core) * 256, 256), 256)
        out_ref[:, columns] = (
            skip_ref[:, columns].astype(jnp.float32) + x_buf[1, k].astype(jnp.float32)
        ).astype(jnp.bfloat16)
    exchange.wait_send()
    for k in range(2):
        sent[k].wait_send()
    wait_for(s_buf.at[pl.ds(0, 28)], ssem)


def project(flat, own, near, diagonal, far, skip):
    vmem = pl.BlockSpec(memory_space=pltpu.VMEM)
    hbm = pl.BlockSpec(memory_space=pl.ANY)
    dma = pltpu.SemaphoreType.DMA
    return pl.pallas_call(
        project_kernel,
        out_shape=jax.ShapeDtypeStruct(skip.shape, skip.dtype),
        in_specs=[vmem, hbm, hbm, hbm, hbm, vmem],
        out_specs=vmem,
        scratch_shapes=[
            pltpu.VMEM((2, 256, 1024), jnp.bfloat16),
            pltpu.VMEM((16, 1024, 256), jnp.bfloat16),
            pltpu.VMEM((32, 256, 256), jnp.bfloat16),
            pltpu.VMEM((4, 2, 2, 2, 256, 256), jnp.bfloat16),
            pltpu.VMEM((2, 2, 256, 256), jnp.float32),
            pltpu.VMEM((2, 2, 256, 256), jnp.bfloat16),
            dma((4, 2, 2, 2)),
            dma,
            dma((2,)),
            dma((16,)),
            dma((2,)),
            dma((2,)),
        ],
        compiler_params=pltpu.CompilerParams(
            collective_id=1, has_side_effects=True, vmem_limit_bytes=60 * 1024 * 1024
        ),
        cost_estimate=pl.CostEstimate(
            flops=2 * 512 * 1024 * 4096, bytes_accessed=16 << 20, transcendentals=0
        ),
    )(flat, own, near, diagonal, far, skip)


def table_kernel(mine_ref, own_ref, out_ref, near_ref, landing, send_sem, recv_sem, wsend, wrecv):
    dp, z, _, _, _ = spots()
    barrier = pltpu.get_barrier_semaphore()

    def greet(step, carry):
        pl.semaphore_signal(
            barrier, inc=1, device_id=(lax.rem(dp + step, 32), z), device_id_type=MESH
        )
        return carry

    lax.fori_loop(1, 32, greet, 0)
    landing[dp] = mine_ref[...]
    pl.semaphore_wait(barrier, 31)

    def send(step, carry):
        pltpu.make_async_remote_copy(
            src_ref=mine_ref,
            dst_ref=landing.at[dp],
            send_sem=send_sem,
            recv_sem=recv_sem,
            device_id=(lax.rem(dp + step, 32), z),
            device_id_type=MESH,
        ).start()
        return carry

    lax.fori_loop(1, 32, send, 0)
    blocks = [
        pltpu.make_async_remote_copy(
            src_ref=own_ref, dst_ref=near_ref.at[axis * 2 + way],
            send_sem=wsend.at[axis, way], recv_sem=wrecv.at[axis, way],
            device_id=beside(axis, way), device_id_type=MESH,
        )
        for axis in range(2)
        for way in range(2)
    ]
    for block in blocks:
        block.start()
    all_of_them = landing.at[pl.ds(0, 31)]
    pltpu.make_async_copy(all_of_them, all_of_them, recv_sem).wait()
    pltpu.make_async_copy(all_of_them, all_of_them, send_sem).wait()

    table = landing[:, 0, :]
    lane = lax.broadcasted_iota(jnp.int32, (32, 128), 1)
    line = lax.broadcasted_iota(jnp.int32, (32, 128), 0)

    def column(k):
        return jnp.sum(jnp.where(lane == k, table, 0), axis=1, keepdims=True)

    parents = [column(0), column(1)]
    rows = [
        jnp.sum(jnp.where(lane == line, parent, 0), axis=0, keepdims=True) for parent in parents
    ]
    result = jnp.zeros((32, 128), jnp.int32)
    low = jnp.full((1, 1), 9, jnp.int32)
    high = jnp.full((1, 1), -1, jnp.int32)
    for i in range(2):
        before = jnp.zeros((32, 1), jnp.int32)
        for row in rows:
            same = jnp.right_shift(row, 2) == jnp.right_shift(parents[i], 2)
            hit = same & (row < parents[i]) & (lane < 32)
            before += jnp.sum(jnp.where(hit, 1, 0), axis=1, keepdims=True)
        code = jnp.right_shift(parents[i], 2) * 2 + before
        result = jnp.where(lane == i, code, result)
        here = jnp.right_shift(parents[i], 2) == dp
        slot = jnp.bitwise_and(parents[i], 3)
        low = jnp.minimum(low, jnp.min(jnp.where(here, slot, 9), axis=0, keepdims=True))
        high = jnp.maximum(high, jnp.max(jnp.where(here, slot, -1), axis=0, keepdims=True))
        wanted = jnp.sum(
            jnp.where(line[:, :1] == dp, parents[i], 0), axis=0, keepdims=True
        )
        found = (lane >= 2) & (lane < 6) & (line * 4 + lane - 2 == wanted)
        extent = jnp.sum(
            jnp.sum(jnp.where(found, table, 0), axis=0, keepdims=True), axis=1, keepdims=True
        )
        result = jnp.where(lane == 4 + i, extent, result)
    result = jnp.where(lane == 2, low, result)
    result = jnp.where(lane == 3, high, result)
    out_ref[...] = result
    for block in blocks:
        block.wait()


def make_table(kept_parent, stored_extent, own):
    mine = jnp.concatenate([kept_parent, stored_extent])
    mine = jnp.broadcast_to(jnp.pad(mine, (0, 122))[None], (8, 128))
    vmem = pl.BlockSpec(memory_space=pltpu.VMEM)
    return pl.pallas_call(
        table_kernel,
        out_shape=[
            jax.ShapeDtypeStruct((32, 128), jnp.int32),
            jax.ShapeDtypeStruct((4,) + own.shape, own.dtype),
        ],
        in_specs=[vmem, pl.BlockSpec(memory_space=pl.ANY)],
        out_specs=[vmem, pl.BlockSpec(memory_space=pl.ANY)],
        scratch_shapes=[
            pltpu.VMEM((32, 8, 128), jnp.int32),
            pltpu.SemaphoreType.DMA,
            pltpu.SemaphoreType.DMA,
            pltpu.SemaphoreType.DMA((2, 2)),
            pltpu.SemaphoreType.DMA((2, 2)),
        ],
        compiler_params=pltpu.CompilerParams(collective_id=2, has_side_effects=True, vmem_limit_bytes=60 * 1024 * 1024),
    )(mine, own)


PLACES = [[0], [1], [2], [3], [], [4], [5], [6]]


def route_kernel(
    tab, k_ref, v_ref, near_ref, kout, vout, diagonal_ref, far_ref,
    picked, gk, gv, s1, r1, s2, r2, fin, xin,
    psend, precv, asend, arecv, fsend, frecv, s1s, s1r, s2s, s2r, xs, xr, dgr, far_sem, wsend,
):
    dp, z, core, x, y = spots()
    partner = (dp + 1 - 2 * core, z)
    stores = (k_ref, v_ref)
    outs = (kout, vout)
    gathered = (gk, gv)
    first_at = (x, y)
    second_at = (y, x)

    def at(kv, which, step):
        along_x = (which == 0) == (kv == 0)
        nx = lax.rem(x + step, 4) if along_x else x
        ny = y if along_x else lax.rem(y + step, 4)
        return ((ny * 4 + nx) * 2 + core, z)

    def copy(src, dst, send, recv, target):
        return pltpu.make_async_remote_copy(
            src_ref=src, dst_ref=dst, send_sem=send, recv_sem=recv,
            device_id=target, device_id_type=MESH,
        )

    def wait(ref, sem):
        pltpu.make_async_copy(ref, ref, sem).wait()

    def push(source, to, sems, first, count, axis, way):
        rows = pl.ds(first * 256, count * 256)
        refs, sem = (diagonal_ref, dgr) if sems == 0 else (far_ref, far_sem)
        group = DIAGONAL if sems == 0 else FAR
        place = group.index(to)
        pltpu.make_async_remote_copy(
            src_ref=source.at[rows], dst_ref=refs.at[place, rows],
            send_sem=wsend.at[axis, way], recv_sem=sem.at[place, first // 2],
            device_id=beside(axis, way), device_id_type=MESH,
        ).start()

    def landed(place, half):
        k = FAR.index(place)
        wait(far_ref.at[k, pl.ds(half * 512, 512)], far_sem.at[k, half])

    def weights(part):
        if part == 0:
            for half in range(2):
                for way in range(2):
                    push(near_ref.at[way], (2, 0), 1, 2 * half + way, 1, 0, way)
                    push(near_ref.at[2 + way], (0, 2), 1, 2 * (1 - half) + way, 1, 1, way)
        if part in (1, 2):
            d = 2 * part - 1
            for way in range(2):
                push(near_ref.at[part - 1], (d, 1 + 2 * way), 0, 0, 2, 1, way)
                push(near_ref.at[1 + part], (1 + 2 * way, d), 0, 2, 2, 0, way)
        if part == 3:
            landed((2, 0), 0)
            landed((0, 2), 1)
            for way in range(2):
                push(far_ref.at[0], (2, 1 + 2 * way), 1, 0, 2, 1, way)
                push(far_ref.at[1], (1 + 2 * way, 2), 1, 2, 2, 0, way)
        if part == 4:
            for k in range(4):
                dx, dy = DIAGONAL[k]
                for half in range(2):
                    wait(diagonal_ref.at[k, pl.ds(half * 512, 512)], dgr.at[k, half])
                push(diagonal_ref.at[k], (dx, 2), 1, dy // 2, 1, 1, dy // 2)
                push(diagonal_ref.at[k], (2, dy), 1, 2 + dx // 2, 1, 0, dx // 2)
        if part == 5:
            for way in range(2):
                landed((2, 1 + 2 * way), 0)
                push(far_ref.at[FAR.index((2, 1 + 2 * way))], (2, 2), 1, way, 1, 1, way)
                landed((1 + 2 * way, 2), 1)
                push(far_ref.at[FAR.index((1 + 2 * way, 2))], (2, 2), 1, 2 + way, 1, 0, way)
        if part == 6:
            landed((2, 0), 1)
            landed((0, 2), 0)
            for way in range(2):
                landed((2, 1 + 2 * way), 1)
                landed((1 + 2 * way, 2), 0)
                landed((2, 2), way)
                for axis in range(2):
                    wait(far_ref.at[pl.ds(0, 4), pl.ds(0, 11 * 64)], wsend.at[axis, way])

    def at_point(point):
        for part in PLACES[point]:
            weights(part)

    barrier = pltpu.get_barrier_semaphore()
    around = [partner] + [at(0, which, step) for which in range(2) for step in (1, 3)]
    for other in around:
        pl.semaphore_signal(barrier, inc=1, device_id=other, device_id_type=MESH)

    mine_rows = pl.ds(pl.multiple_of(core * 256, 256), 256)
    other_rows = pl.ds(pl.multiple_of((1 - core) * 256, 256), 256)
    for kv in range(2):
        for i in range(2):
            picked[kv, i] = stores[kv][tab[0, 2 + i]]
            gathered[kv][first_at[kv], core * 2 + i] = picked[kv, i, mine_rows, :]
    pl.semaphore_wait(barrier, len(around))
    at_point(0)
    swaps = []
    for kv in range(2):
        swaps.append(
            copy(
                picked.at[kv, pl.ds(0, 2), other_rows],
                gathered[kv].at[first_at[kv], pl.ds(pl.multiple_of(core * 2, 2), 2)],
                psend.at[kv], precv.at[kv], partner,
            )
        )
        swaps[-1].start()

    def pair(kv, place, half):
        return gathered[kv].at[place, pl.ds(2 * half, 2)]

    started = []
    for kv in range(2):
        mine = gathered[kv].at[first_at[kv], pl.ds(pl.multiple_of((1 - core) * 2, 2), 2)]
        wait(mine, precv.at[kv])
        for turn in range(2):
            for way in range(2):
                half = turn ^ way
                block = pair(kv, first_at[kv], half)
                started.append(
                    copy(
                        block, block, asend.at[kv, way, half], arecv.at[kv, way, half],
                        at(kv, 0, 1 + 2 * way),
                    )
                )
                started[-1].start()
    at_point(1)
    for kv in range(2):
        for way in range(2):
            place = lax.rem(first_at[kv] + (3 if way == 0 else 1), 4)
            block = pair(kv, place, way)
            wait(block, arecv.at[kv, way, way])
            started.append(
                copy(block, block, fsend.at[kv, way], frecv.at[kv, way], at(kv, 0, 1 + 2 * way))
            )
            started[-1].start()
    at_point(2)
    for kv in range(2):
        for way in range(2):
            place = lax.rem(first_at[kv] + (3 if way == 0 else 1), 4)
            wait(pair(kv, place, 1 - way), arecv.at[kv, way, 1 - way])
        for way in range(2):
            wait(pair(kv, lax.rem(first_at[kv] + 2, 4), way), frecv.at[kv, way])

    def candidate(kv, step, slot):
        to = lax.rem(second_at[kv] + step, 4)
        chip = to * 4 + x if kv == 0 else y * 4 + to
        code = tab[chip * 2 + slot // 2, slot % 2]
        rank = jnp.bitwise_and(code, 1)
        source_core = jnp.bitwise_and(jnp.right_shift(code, 1), 1)
        source_x = jnp.bitwise_and(jnp.right_shift(code, 2), 3)
        source_y = jnp.right_shift(code, 4)
        one, two = (source_x, source_y) if kv == 0 else (source_y, source_x)
        return gathered[kv][one, source_core * 2 + rank], two

    for kv in range(2):
        for way in range(2):
            for j in range(2):
                s1[kv, way, j] = candidate(kv, 2, 2 * way + j)[0]
            started.append(
                copy(
                    s1.at[kv, way], r1.at[kv, way], s1s.at[kv, way], s1r.at[kv, way],
                    at(kv, 1, 1 + 2 * way),
                )
            )
            started[-1].start()
    at_point(3)
    for turn in range(2):
        if turn == 1:
            at_point(4)
        for kv in range(2):
            for way in range(2):
                half = 1 - way if turn == 0 else way
                if turn == 1:
                    wait(r1.at[kv, way], s1r.at[kv, way])
                for j in range(2):
                    slot = 2 * half + j
                    value, two = candidate(kv, 1 + 2 * way, slot)
                    if turn == 1:
                        value = jnp.where(two == second_at[kv], value, r1[kv, way, j])
                    s2[kv, way, slot] = value
                started.append(
                    copy(
                        s2.at[kv, way, pl.ds(2 * half, 2)], r2.at[kv, way, pl.ds(2 * half, 2)],
                        s2s.at[kv, way, half], s2r.at[kv, way, half], at(kv, 1, 1 + 2 * way),
                    )
                )
                started[-1].start()
    at_point(5)
    for kv in range(2):
        for half in range(2):
            for way in range(2):
                wait(r2.at[kv, way, pl.ds(2 * half, 2)], s2r.at[kv, way, half])
            for j in range(2):
                slot = 2 * half + j
                value, two = candidate(kv, 0, slot)
                here = second_at[kv]
                away = lax.rem(two - here + 4, 4)
                first = (away == 3) | (away == 2) if half == 0 else away == 3
                arrived = jnp.where(first, r2[kv, 0, slot], r2[kv, 1, slot])
                fin[kv, slot] = jnp.where(away == 0, value, arrived)
        theirs = fin.at[kv, pl.ds(pl.multiple_of((1 - core) * 2, 2), 2)]
        started.append(copy(theirs, xin.at[kv], xs.at[kv], xr.at[kv], partner))
        started[-1].start()
        for i in range(2):
            outs[kv][i, mine_rows, :] = fin[kv, core * 2 + i]
    at_point(6)
    for kv in range(2):
        wait(xin.at[kv], xr.at[kv])
        for i in range(2):
            outs[kv][i, other_rows, :] = xin[kv, i]
    at_point(7)
    for each in swaps + started:
        each.wait_send()


def route(table, keys, values, near):
    vmem = pl.BlockSpec(memory_space=pltpu.VMEM)
    item = (256, 128)
    hbm = pl.BlockSpec(memory_space=pl.ANY)
    bf16 = jnp.bfloat16
    dma = pltpu.SemaphoreType.DMA
    return pl.pallas_call(
        route_kernel,
        out_shape=[jax.ShapeDtypeStruct((2, 512, 128), bf16)] * 2
        + [jax.ShapeDtypeStruct((count,) + near.shape[1:], bf16) for count in (4, 7)],
        in_specs=[pl.BlockSpec(memory_space=pltpu.SMEM), vmem, vmem, hbm],
        out_specs=[vmem, vmem, hbm, hbm],
        scratch_shapes=[
            pltpu.VMEM((2, 2, 512, 128), bf16),
            pltpu.VMEM((4, 4) + item, bf16),
            pltpu.VMEM((4, 4) + item, bf16),
            pltpu.VMEM((2, 2, 2) + item, bf16),
            pltpu.VMEM((2, 2, 2) + item, bf16),
            pltpu.VMEM((2, 2, 4) + item, bf16),
            pltpu.VMEM((2, 2, 4) + item, bf16),
            pltpu.VMEM((2, 4) + item, bf16),
            pltpu.VMEM((2, 2) + item, bf16),
            dma((2,)), dma((2,)),
            dma((2, 2, 2)), dma((2, 2, 2)),
            dma((2, 2)), dma((2, 2)),
            dma((2, 2)), dma((2, 2)),
            dma((2, 2, 2)), dma((2, 2, 2)),
            dma((2,)), dma((2,)),
            dma((4, 2)), dma((7, 2)), dma((2, 2)),
        ],
        compiler_params=pltpu.CompilerParams(
            collective_id=3, has_side_effects=True, vmem_limit_bytes=60 * 1024 * 1024
        ),
    )(table, keys, values, near)


def attend(
    question_vectors, arriving_lookup_vectors, arriving_content_vectors, keys_in, values_in, lengths
):
    tally_lines = question_vectors.shape[0]
    groups = arriving_lookup_vectors.shape[2] // HEAD_DIM
    head_count = question_vectors.shape[2] // HEAD_DIM
    per_group = head_count // groups
    key_span = CACHE + STRETCH
    query_all = question_vectors.reshape(tally_lines, STRETCH, groups, per_group, HEAD_DIM)
    key_all = jnp.concatenate([keys_in, arriving_lookup_vectors], axis=1).reshape(
        tally_lines, key_span, groups, HEAD_DIM
    )
    value_all = jnp.concatenate([values_in, arriving_content_vectors], axis=1).reshape(
        tally_lines, key_span, groups, HEAD_DIM
    )
    scores = jnp.einsum(
        "rcgqd,rkgd->rgqck", query_all, key_all, preferred_element_type=jnp.float32
    ) / math.sqrt(HEAD_DIM)
    position = jnp.arange(key_span)
    query_pos = jnp.arange(STRETCH)
    in_cache = position[None, None, :] < lengths[:, None, None]
    in_stretch = position[None, :] - CACHE <= query_pos[:, None]
    allowed = jnp.where(position[None, None, :] < CACHE, in_cache, in_stretch[None])
    scores = jnp.where(allowed[:, None, None], scores, -jnp.inf)
    peak = jnp.max(scores, axis=-1, keepdims=True)
    raised = jnp.exp(scores - peak)
    probs = (raised / jnp.sum(raised, axis=-1, keepdims=True)).astype(jnp.bfloat16)
    mixed = jnp.einsum("rgqck,rkgd->rcgqd", probs, value_all, preferred_element_type=jnp.float32)
    return mixed.astype(jnp.bfloat16).reshape(tally_lines, STRETCH, head_count * HEAD_DIM)


def local(
    question_vectors,
    arriving_lookup_vectors,
    arriving_content_vectors,
    earlier_lookup_store,
    earlier_content_store,
    stored_extent,
    kept_parent,
    final_projection_matrix,
    skip_stream,
):
    table, near = make_table(kept_parent, stored_extent, final_projection_matrix)
    keys_in, values_in, diagonal, far = route(
        table, earlier_lookup_store, earlier_content_store, near
    )
    lengths = table[0, 4:6]
    attended = attend(
        question_vectors,
        arriving_lookup_vectors,
        arriving_content_vectors,
        keys_in,
        values_in,
        lengths,
    )
    flat = attended.reshape(attended.shape[0] * STRETCH, attended.shape[2])
    return project(flat, final_projection_matrix, near, diagonal, far, skip_stream)


def solution(mesh):
    return jax.shard_map(
        local,
        mesh=mesh,
        in_specs=(
            P("dp", None, "tensor"),
            P("dp", None, "tensor"),
            P("dp", None, "tensor"),
            P("dp", None, "tensor"),
            P("dp", None, "tensor"),
            P("dp"),
            P("dp"),
            P("tensor", "dp"),
            P("dp", "tensor"),
        ),
        out_specs=P("dp", "tensor"),
        check_vma=False,
    )
```

```python
import math

import jax
import jax.numpy as jnp
from jax import lax
from jax.experimental import pallas as pl
from jax.experimental.pallas import tpu as pltpu
from jax.sharding import PartitionSpec as P

HEAD_DIM = 128
STRETCH = 128
CACHE = 512
MESH = pl.DeviceIdType.MESH


def spots():
    dp = lax.axis_index("dp")
    core = lax.rem(dp, 2)
    chip = dp // 2
    return dp, lax.axis_index("tensor"), core, lax.rem(chip, 4), chip // 4


def beside(axis, way):
    dp, z, core, x, y = spots()
    step = 1 + 2 * way
    nx = lax.rem(x + step, 4) if axis == 0 else x
    ny = y if axis == 0 else lax.rem(y + step, 4)
    return ((ny * 4 + nx) * 2 + core, z)


def remote(src, dst, send, recv, target):
    return pltpu.make_async_remote_copy(
        src_ref=src, dst_ref=dst, send_sem=send, recv_sem=recv,
        device_id=target, device_id_type=MESH,
    )


def wait_for(ref, sem):
    pltpu.make_async_copy(ref, ref, sem).wait()


def row_table(table, dp):
    lane = lax.broadcasted_iota(jnp.int32, (32, 128), 1)
    line = lax.broadcasted_iota(jnp.int32, (32, 128), 0)

    def column(k):
        return jnp.sum(jnp.where(lane == k, table, 0), axis=1, keepdims=True)

    parents = [column(0), column(1)]
    rows = [
        jnp.sum(jnp.where(lane == line, parent, 0), axis=0, keepdims=True) for parent in parents
    ]
    result = jnp.zeros((32, 128), jnp.int32)
    low = jnp.full((1, 1), 9, jnp.int32)
    high = jnp.full((1, 1), -1, jnp.int32)
    for i in range(2):
        before = jnp.zeros((32, 1), jnp.int32)
        for row in rows:
            same = jnp.right_shift(row, 2) == jnp.right_shift(parents[i], 2)
            hit = same & (row < parents[i]) & (lane < 32)
            before += jnp.sum(jnp.where(hit, 1, 0), axis=1, keepdims=True)
        code = jnp.right_shift(parents[i], 2) * 2 + before
        result = jnp.where(lane == i, code, result)
        here = jnp.right_shift(parents[i], 2) == dp
        slot = jnp.bitwise_and(parents[i], 3)
        low = jnp.minimum(low, jnp.min(jnp.where(here, slot, 9), axis=0, keepdims=True))
        high = jnp.maximum(high, jnp.max(jnp.where(here, slot, -1), axis=0, keepdims=True))
        wanted = jnp.sum(jnp.where(line[:, :1] == dp, parents[i], 0), axis=0, keepdims=True)
        found = (lane >= 2) & (lane < 6) & (line * 4 + lane - 2 == wanted)
        extent = jnp.sum(
            jnp.sum(jnp.where(found, table, 0), axis=0, keepdims=True), axis=1, keepdims=True
        )
        result = jnp.where(lane == 4 + i, extent, result)
    result = jnp.where(lane == 2, jnp.minimum(low, 3), result)
    return jnp.where(lane == 3, jnp.maximum(high, 0), result)


NEAR = [(1, 0), (3, 0), (0, 1), (0, 3)]
DIAGONAL = [(1, 1), (1, 3), (3, 1), (3, 3)]
FAR = [(2, 0), (0, 2), (2, 1), (2, 3), (1, 2), (3, 2), (2, 2)]
PLACES = {"gather": [1], "forward": [2], "select": [0], "relay": [4], "own": [3], "row0": [5]}


def layer_kernel(
    mine_ref, q_ref, new_k_ref, new_v_ref, k_ref, v_ref, own_ref, skip_ref, out_ref,
    landing, tab_vmem, tab, w_buf,
    picked, gk, gv, s1, r1, s2, r2, fin, xin, all_k, all_v,
    a_buf, s_buf, r_buf, t_buf, x_buf,
    tsem, nsem, wsem, wsend,
    psend, precv, asend, arecv, fsend, frecv, s1s, s1r, s2s, s2r, xs, xr,
    rsem, ssem, esem, xsend, xrecv,
):
    dp, z, core, x, y = spots()
    partner = (dp + 1 - 2 * core, z)
    barrier = pltpu.get_barrier_semaphore()

    def greet(step, carry):
        pl.semaphore_signal(
            barrier, inc=1, device_id=(lax.rem(dp + step, 32), z), device_id_type=MESH
        )
        return carry

    lax.fori_loop(1, 32, greet, 0)
    for step in (1, 7):
        pl.semaphore_signal(
            barrier, inc=1, device_id=(dp, lax.rem(z + step, 8)), device_id_type=MESH
        )
    landing[dp] = mine_ref[...]
    w_buf[0] = own_ref[...]
    pl.semaphore_wait(barrier, 33)

    def share(step, carry):
        remote(
            mine_ref, landing.at[dp], tsem.at[0], tsem.at[1], (lax.rem(dp + step, 32), z)
        ).start()
        return carry

    lax.fori_loop(1, 32, share, 0)

    def slot_of(place):
        return place[1] * 4 + place[0]

    def sem_of(place, half):
        return wsem.at[(DIAGONAL + FAR).index(place), half]

    def push(source, to, first, count, axis, way):
        rows = pl.ds(first * 256, count * 256)
        remote(
            w_buf.at[slot_of(source), rows], w_buf.at[slot_of(to), rows],
            wsend.at[axis, way], sem_of(to, first // 2), beside(axis, way),
        ).start()

    def landed(place, half):
        wait_for(w_buf.at[slot_of(place), pl.ds(half * 512, 512)], sem_of(place, half))

    def weights(part):
        if part == 0:
            for half in range(2):
                for way in range(2):
                    push(NEAR[way], (2, 0), 2 * half + way, 1, 0, way)
                    push(NEAR[2 + way], (0, 2), 2 * (1 - half) + way, 1, 1, way)
        if part in (1, 2):
            d = 2 * part - 1
            for way in range(2):
                push(NEAR[part - 1], (d, 1 + 2 * way), 0, 2, 1, way)
                push(NEAR[part + 1], (1 + 2 * way, d), 2, 2, 0, way)
        if part == 3:
            landed((2, 0), 0)
            landed((0, 2), 1)
            for way in range(2):
                push((2, 0), (2, 1 + 2 * way), 0, 2, 1, way)
                push((0, 2), (1 + 2 * way, 2), 2, 2, 0, way)
        if part == 4:
            for dx, dy in DIAGONAL:
                for half in range(2):
                    landed((dx, dy), half)
                push((dx, dy), (dx, 2), dy // 2, 1, 1, dy // 2)
                push((dx, dy), (2, dy), 2 + dx // 2, 1, 0, dx // 2)
        if part == 5:
            for way in range(2):
                landed((2, 1 + 2 * way), 0)
                push((2, 1 + 2 * way), (2, 2), way, 1, 1, way)
                landed((1 + 2 * way, 2), 1)
                push((1 + 2 * way, 2), (2, 2), 2 + way, 1, 0, way)
        if part == 6:
            landed((2, 0), 1)
            landed((0, 2), 0)
            for way in range(2):
                landed((2, 1 + 2 * way), 1)
                landed((1 + 2 * way, 2), 0)
                landed((2, 2), way)

    def at_point(point):
        for part in PLACES.get(point, []):
            weights(part)

    for axis in range(2):
        for way in range(2):
            remote(
                w_buf.at[0], w_buf.at[slot_of(NEAR[axis * 2 + way])],
                wsend.at[axis, way], nsem.at[axis, way], beside(axis, way),
            ).start()

    all_of_them = landing.at[pl.ds(0, 31)]
    wait_for(all_of_them, tsem.at[1])
    tab_vmem[...] = row_table(landing[:, 0, :], dp)
    to_scalar = pltpu.make_async_copy(tab_vmem, tab, tsem.at[2])
    to_scalar.start()
    to_scalar.wait()

    stores = (k_ref, v_ref)
    gathered = (gk, gv)
    first_at = (x, y)
    second_at = (y, x)
    started = []

    def send(*args):
        started.append(remote(*args))
        started[-1].start()

    def at(kv, which, way):
        return beside(kv ^ which, way)

    mine_rows = pl.ds(pl.multiple_of(core * 256, 256), 256)
    other_rows = pl.ds(pl.multiple_of((1 - core) * 256, 256), 256)
    my_two = pl.ds(pl.multiple_of(core * 2, 2), 2)
    other_two = pl.ds(pl.multiple_of((1 - core) * 2, 2), 2)
    for kv in range(2):
        for i in range(2):
            picked[kv, i] = stores[kv][jnp.bitwise_and(tab[0, 2 + i], 3)]
            gathered[kv][first_at[kv], core * 2 + i] = picked[kv, i, mine_rows, :]
        send(
            picked.at[kv, pl.ds(0, 2), other_rows], gathered[kv].at[first_at[kv], my_two],
            psend.at[kv], precv.at[kv], partner,
        )

    def pair(kv, place, half):
        return gathered[kv].at[place, pl.ds(2 * half, 2)]

    for kv in range(2):
        wait_for(gathered[kv].at[first_at[kv], other_two], precv.at[kv])
        for turn in range(2):
            for way in range(2):
                half = turn ^ way
                block = pair(kv, first_at[kv], half)
                send(block, block, asend.at[kv, way, half], arecv.at[kv, way, half], at(kv, 0, way))
    for axis in range(2):
        for way in range(2):
            wait_for(w_buf.at[slot_of(NEAR[axis * 2 + way])], nsem.at[axis, way])
    at_point("gather")
    for kv in range(2):
        for way in range(2):
            block = pair(kv, lax.rem(first_at[kv] + (3 if way == 0 else 1), 4), way)
            wait_for(block, arecv.at[kv, way, way])
            send(block, block, fsend.at[kv, way], frecv.at[kv, way], at(kv, 0, way))
    at_point("forward")
    for kv in range(2):
        for way in range(2):
            place = lax.rem(first_at[kv] + (3 if way == 0 else 1), 4)
            wait_for(pair(kv, place, 1 - way), arecv.at[kv, way, 1 - way])
        for way in range(2):
            wait_for(pair(kv, lax.rem(first_at[kv] + 2, 4), way), frecv.at[kv, way])

    def candidate(kv, step, slot):
        to = lax.rem(second_at[kv] + step, 4)
        chip = to * 4 + x if kv == 0 else y * 4 + to
        code = tab[chip * 2 + slot // 2, slot % 2]
        rank = jnp.bitwise_and(code, 1)
        source_core = jnp.bitwise_and(jnp.right_shift(code, 1), 1)
        source_x = jnp.bitwise_and(jnp.right_shift(code, 2), 3)
        source_y = jnp.bitwise_and(jnp.right_shift(code, 4), 3)
        one, two = (source_x, source_y) if kv == 0 else (source_y, source_x)
        return gathered[kv][one, source_core * 2 + rank], two

    for kv in range(2):
        for way in range(2):
            for j in range(2):
                s1[kv, way, j] = candidate(kv, 2, 2 * way + j)[0]
            send(s1.at[kv, way], r1.at[kv, way], s1s.at[kv, way], s1r.at[kv, way], at(kv, 1, way))
    at_point("select")
    for turn in range(2):
        for kv in range(2):
            for way in range(2):
                half = 1 - way if turn == 0 else way
                if turn == 1:
                    wait_for(r1.at[kv, way], s1r.at[kv, way])
                for j in range(2):
                    slot = 2 * half + j
                    value, two = candidate(kv, 1 + 2 * way, slot)
                    if turn == 1:
                        value = jnp.where(two == second_at[kv], value, r1[kv, way, j])
                    s2[kv, way, slot] = value
                two_slots = pl.ds(2 * half, 2)
                send(
                    s2.at[kv, way, two_slots], r2.at[kv, way, two_slots],
                    s2s.at[kv, way, half], s2r.at[kv, way, half], at(kv, 1, way),
                )
        at_point("relay" if turn == 0 else "own")
    whole = (all_k, all_v)
    for kv in range(2):
        for half in range(2):
            for way in range(2):
                wait_for(r2.at[kv, way, pl.ds(2 * half, 2)], s2r.at[kv, way, half])
            for j in range(2):
                slot = 2 * half + j
                value, two = candidate(kv, 0, slot)
                away = lax.rem(two - second_at[kv] + 4, 4)
                first = (away == 3) | (away == 2) if half == 0 else away == 3
                arrived = jnp.where(first, r2[kv, 0, slot], r2[kv, 1, slot])
                fin[kv, slot] = jnp.where(away == 0, value, arrived)
        send(fin.at[kv, other_two], xin.at[kv], xs.at[kv], xr.at[kv], partner)
        for i in range(2):
            whole[kv][i, mine_rows, :] = fin[kv, core * 2 + i]
            whole[kv][i, pl.ds(CACHE, STRETCH), :] = (new_k_ref, new_v_ref)[kv][i]
    for kv in range(2):
        wait_for(xin.at[kv], xr.at[kv])
        for i in range(2):
            whole[kv][i, other_rows, :] = xin[kv, i]

    scale = 1.0 / math.sqrt(HEAD_DIM)
    span = CACHE + STRETCH
    exchange = []
    for i in range(2):
        position = lax.broadcasted_iota(jnp.int32, (2 * STRETCH, span), 1)
        token = lax.rem(lax.broadcasted_iota(jnp.int32, (2 * STRETCH, span), 0), STRETCH)
        bound = jnp.where(position < CACHE, tab[0, 4 + i], token + CACHE + 1)
        penalty = jnp.where(position < bound, 0.0, -1e30)
        tokens = pl.ds(i * STRETCH, STRETCH)

        def heads(c, carry):
            both = pl.ds(pl.multiple_of(c * 256, 256), 256)
            q = q_ref[i, :, both]
            q = jnp.concatenate([q[:, :HEAD_DIM], q[:, HEAD_DIM:]], axis=0)
            scores = lax.dot_general(
                q, all_k[i], (((1,), (1,)), ((), ())), preferred_element_type=jnp.float32
            )
            scores = scores * scale + penalty
            raised = jnp.exp(scores - jnp.max(scores, axis=1, keepdims=True))
            total = jnp.sum(raised, axis=1, keepdims=True)
            mixed = jnp.dot(
                raised.astype(jnp.bfloat16), all_v[i], preferred_element_type=jnp.float32
            )
            mixed = (mixed / total).astype(jnp.bfloat16)
            a_buf[core, tokens, both] = jnp.concatenate(
                [mixed[:STRETCH], mixed[STRETCH:]], axis=1
            )
            return carry

        lax.fori_loop(0, 4, heads, 0)
        exchange.append(
            remote(
                a_buf.at[core, tokens], a_buf.at[core, tokens],
                esem.at[0, i], esem.at[1, i], partner,
            )
        )
        exchange[-1].start()
        at_point("row%d" % i)
    weights(6)

    def product(d, h, k):
        goal = lax.rem(z + d, 8)
        dx = lax.rem(x - 2 * lax.rem(goal, 2) - k + 4, 4)
        dy = lax.rem(y - goal // 2 + 4, 4)
        return jnp.dot(a_buf[h], w_buf[dy * 4 + dx], preferred_element_type=jnp.float32)

    def step(s, carry):
        for turn in range(2):
            h = lax.rem(core + turn, 2)
            if turn == 1:

                @pl.when(s == 0)
                def _():
                    for i in range(2):
                        rows = pl.ds(i * STRETCH, STRETCH)
                        wait_for(a_buf.at[1 - core, rows], esem.at[1, i])

            for k in range(2):
                for way in range(2):
                    d = 4 - s - h if way == 0 else 4 + s + 1 - h

                    @pl.when((d > 0) & (d < 8))
                    def _():
                        value = product(d, h, k)
                        place = ((s * 2 + k) * 2 + way) * 2 + h

                        @pl.when(s == 0)
                        def _():
                            s_buf[place] = value.astype(jnp.bfloat16)

                        @pl.when(s > 0)
                        def _():
                            before = jnp.maximum(s - 1, 0)
                            wait_for(r_buf.at[before, k, way, h], rsem.at[before, k, way, h])
                            s_buf[place] = (
                                value + r_buf[before, k, way, h].astype(jnp.float32)
                            ).astype(jnp.bfloat16)

                        remote(
                            s_buf.at[place], r_buf.at[s, k, way, h],
                            ssem, rsem.at[s, k, way, h], (dp, lax.rem(z + 1 + 6 * way, 8)),
                        ).start()
        return carry

    lax.fori_loop(0, 4, step, 0)

    def total_of(h, k):
        for way, last in ((0, 3 - h), (1, 2 + h)):
            wait_for(r_buf.at[last, k, way, h], rsem.at[last, k, way, h])
        return (
            t_buf[h, k]
            + r_buf[3 - h, k, 0, h].astype(jnp.float32)
            + r_buf[2 + h, k, 1, h].astype(jnp.float32)
        )

    for h in range(2):
        for k in range(2):
            t_buf[h, k] = product(0, h, k)
    last = []
    for k in range(2):
        x_buf[0, k] = total_of(1 - core, k).astype(jnp.bfloat16)
        last.append(remote(x_buf.at[0, k], x_buf.at[1, k], xsend.at[k], xrecv.at[k], partner))
        last[-1].start()
    for k in range(2):
        columns = pl.ds(pl.multiple_of((2 * k + core) * 256, 256), 256)
        out_ref[:, columns] = (
            skip_ref[:, columns].astype(jnp.float32) + total_of(core, k)
        ).astype(jnp.bfloat16)
    for k in range(2):
        last[k].wait_recv()
        columns = pl.ds(pl.multiple_of((2 * k + 1 - core) * 256, 256), 256)
        out_ref[:, columns] = (
            skip_ref[:, columns].astype(jnp.float32) + x_buf[1, k].astype(jnp.float32)
        ).astype(jnp.bfloat16)
    for each in started + exchange + last:
        each.wait_send()
    wait_for(s_buf.at[pl.ds(0, 28)], ssem)
    wait_for(all_of_them, tsem.at[0])
    for axis in range(2):
        for way in range(2):
            wait_for(w_buf.at[pl.ds(0, 15), pl.ds(0, 256)], wsend.at[axis, way])


def local(
    question_vectors,
    arriving_lookup_vectors,
    arriving_content_vectors,
    earlier_lookup_store,
    earlier_content_store,
    stored_extent,
    kept_parent,
    final_projection_matrix,
    skip_stream,
):
    mine = jnp.concatenate([kept_parent, stored_extent])
    mine = jnp.broadcast_to(jnp.pad(mine, (0, 122))[None], (8, 128))
    vmem = pl.BlockSpec(memory_space=pltpu.VMEM)
    dma = pltpu.SemaphoreType.DMA
    bf16 = jnp.bfloat16
    item = (256, 128)
    return pl.pallas_call(
        layer_kernel,
        out_shape=jax.ShapeDtypeStruct(skip_stream.shape, skip_stream.dtype),
        in_specs=[vmem] * 8,
        out_specs=vmem,
        scratch_shapes=[
            pltpu.VMEM((32, 8, 128), jnp.int32),
            pltpu.VMEM((32, 128), jnp.int32),
            pltpu.SMEM((32, 128), jnp.int32),
            pltpu.VMEM((16, 1024, 256), bf16),
            pltpu.VMEM((2, 2, 512, 128), bf16),
            pltpu.VMEM((4, 4) + item, bf16),
            pltpu.VMEM((4, 4) + item, bf16),
            pltpu.VMEM((2, 2, 2) + item, bf16),
            pltpu.VMEM((2, 2, 2) + item, bf16),
            pltpu.VMEM((2, 2, 4) + item, bf16),
            pltpu.VMEM((2, 2, 4) + item, bf16),
            pltpu.VMEM((2, 4) + item, bf16),
            pltpu.VMEM((2, 2) + item, bf16),
            pltpu.VMEM((2, CACHE + STRETCH, HEAD_DIM), bf16),
            pltpu.VMEM((2, CACHE + STRETCH, HEAD_DIM), bf16),
            pltpu.VMEM((2, 256, 1024), bf16),
            pltpu.VMEM((32, 256, 256), bf16),
            pltpu.VMEM((4, 2, 2, 2, 256, 256), bf16),
            pltpu.VMEM((2, 2, 256, 256), jnp.float32),
            pltpu.VMEM((2, 2, 256, 256), bf16),
            dma((3,)), dma((2, 2)), dma((11, 2)), dma((2, 2)),
            dma((2,)), dma((2,)),
            dma((2, 2, 2)), dma((2, 2, 2)),
            dma((2, 2)), dma((2, 2)),
            dma((2, 2)), dma((2, 2)),
            dma((2, 2, 2)), dma((2, 2, 2)),
            dma((2,)), dma((2,)),
            dma((4, 2, 2, 2)), dma, dma((2, 2)), dma((2,)), dma((2,)),
        ],
        compiler_params=pltpu.CompilerParams(
            collective_id=1, has_side_effects=True, vmem_limit_bytes=56 * 1024 * 1024
        ),
        cost_estimate=pl.CostEstimate(
            flops=10 << 30, bytes_accessed=8 << 20, transcendentals=2 << 20
        ),
    )(
        mine,
        question_vectors,
        arriving_lookup_vectors,
        arriving_content_vectors,
        earlier_lookup_store,
        earlier_content_store,
        final_projection_matrix,
        skip_stream,
    )


def solution(mesh):
    return jax.shard_map(
        local,
        mesh=mesh,
        in_specs=(
            P("dp", None, "tensor"),
            P("dp", None, "tensor"),
            P("dp", None, "tensor"),
            P("dp", None, "tensor"),
            P("dp", None, "tensor"),
            P("dp"),
            P("dp"),
            P("tensor", "dp"),
            P("dp", "tensor"),
        ),
        out_specs=P("dp", "tensor"),
        check_vma=False,
    )
```

```python
import math

import jax
import jax.numpy as jnp
from jax import lax
from jax.experimental import pallas as pl
from jax.experimental.pallas import tpu as pltpu
from jax.sharding import PartitionSpec as P

HEAD_DIM = 128
STRETCH = 128
CACHE = 512
MESH = pl.DeviceIdType.MESH


def spots():
    dp = lax.axis_index("dp")
    core = lax.rem(dp, 2)
    chip = dp // 2
    return dp, lax.axis_index("tensor"), core, lax.rem(chip, 4), chip // 4


def beside(axis, way):
    dp, z, core, x, y = spots()
    step = 1 + 2 * way
    nx = lax.rem(x + step, 4) if axis == 0 else x
    ny = y if axis == 0 else lax.rem(y + step, 4)
    return ((ny * 4 + nx) * 2 + core, z)


def remote(src, dst, send, recv, target):
    return pltpu.make_async_remote_copy(
        src_ref=src, dst_ref=dst, send_sem=send, recv_sem=recv,
        device_id=target, device_id_type=MESH,
    )


def wait_for(ref, sem):
    pltpu.make_async_copy(ref, ref, sem).wait()


def row_table(table, dp):
    lane = lax.broadcasted_iota(jnp.int32, (32, 128), 1)
    line = lax.broadcasted_iota(jnp.int32, (32, 128), 0)

    def column(k):
        return jnp.sum(jnp.where(lane == k, table, 0), axis=1, keepdims=True)

    parents = [column(0), column(1)]
    rows = [
        jnp.sum(jnp.where(lane == line, parent, 0), axis=0, keepdims=True) for parent in parents
    ]
    result = jnp.zeros((32, 128), jnp.int32)
    low = jnp.full((1, 1), 9, jnp.int32)
    high = jnp.full((1, 1), -1, jnp.int32)
    for i in range(2):
        before = jnp.zeros((32, 1), jnp.int32)
        for row in rows:
            same = jnp.right_shift(row, 2) == jnp.right_shift(parents[i], 2)
            hit = same & (row < parents[i]) & (lane < 32)
            before += jnp.sum(jnp.where(hit, 1, 0), axis=1, keepdims=True)
        code = jnp.right_shift(parents[i], 2) * 2 + before
        result = jnp.where(lane == i, code, result)
        here = jnp.right_shift(parents[i], 2) == dp
        slot = jnp.bitwise_and(parents[i], 3)
        low = jnp.minimum(low, jnp.min(jnp.where(here, slot, 9), axis=0, keepdims=True))
        high = jnp.maximum(high, jnp.max(jnp.where(here, slot, -1), axis=0, keepdims=True))
        wanted = jnp.sum(jnp.where(line[:, :1] == dp, parents[i], 0), axis=0, keepdims=True)
        found = (lane >= 2) & (lane < 6) & (line * 4 + lane - 2 == wanted)
        extent = jnp.sum(
            jnp.sum(jnp.where(found, table, 0), axis=0, keepdims=True), axis=1, keepdims=True
        )
        result = jnp.where(lane == 4 + i, extent, result)
    result = jnp.where(lane == 2, jnp.minimum(low, 3), result)
    return jnp.where(lane == 3, jnp.maximum(high, 0), result)


NEAR = [(1, 0), (3, 0), (0, 1), (0, 3)]
DIAGONAL = [(1, 1), (1, 3), (3, 1), (3, 3)]
FAR = [(2, 0), (0, 2), (2, 1), (2, 3), (1, 2), (3, 2), (2, 2)]
PLACES = {
    "start": ["own"],
    "gather": [],
    "forward": ["side 0"],
    "select": ["own b", "far b"],
    "relay": [],
    "own": ["side 1"],
    "swap": ["odd"],
    "row0": ["own a", "even"],
    "row1": [],
}


def layer_kernel(
    mine_ref, q_ref, new_k_ref, new_v_ref, k_ref, v_ref, own_ref, skip_ref, out_ref,
    landing, tab_vmem, tab, w_buf,
    picked, gk, gv, s1, r1, s2, r2, fin, xin, all_k, all_v,
    a_buf, s_buf, r_buf, t_buf, x_buf,
    tsem, wsem, wsend,
    psend, precv, asend, arecv, fsend, frecv, s1s, s1r, s2s, s2r, xs, xr,
    rsem, ssem, esem, xsend, xrecv,
):
    dp, z, core, x, y = spots()
    partner = (dp + 1 - 2 * core, z)
    barrier = pltpu.get_barrier_semaphore()

    def greet(step, carry):
        pl.semaphore_signal(
            barrier, inc=1, device_id=(lax.rem(dp + step, 32), z), device_id_type=MESH
        )
        return carry

    lax.fori_loop(1, 32, greet, 0)
    for step in (1, 7):
        pl.semaphore_signal(
            barrier, inc=1, device_id=(dp, lax.rem(z + step, 8)), device_id_type=MESH
        )
    landing[dp] = mine_ref[...]
    w_buf[0] = own_ref[...]
    pl.semaphore_wait(barrier, 33)

    def share(step, carry):
        remote(
            mine_ref, landing.at[dp], tsem.at[0], tsem.at[1], (lax.rem(dp + step, 32), z)
        ).start()
        return carry

    lax.fori_loop(1, 32, share, 0)

    def slot_of(place):
        return place[1] * 4 + place[0]

    def sem_of(place, half):
        return wsem.at[(NEAR + DIAGONAL + FAR).index(place), half]

    def push(source, to, first, count, axis, way):
        rows = pl.ds(first * 256, count * 256)
        remote(
            w_buf.at[slot_of(source), rows], w_buf.at[slot_of(to), rows],
            wsend.at[axis, way], sem_of(to, first // 2), beside(axis, way),
        ).start()

    def landed(place, half):
        wait_for(w_buf.at[slot_of(place), pl.ds(half * 512, 512)], sem_of(place, half))

    def weights(part):
        if part == "own":
            for way in range(2):
                push((0, 0), (1 + 2 * way, 0), 0, 2, 0, way)
                push((0, 0), (0, 1 + 2 * way), 2, 2, 1, way)
        if part == "own b":
            for way in range(2):
                push((0, 0), (1 + 2 * way, 0), 2, 2, 0, way)
        if part in ("side 0", "side 1"):
            d = 1 if part == "side 0" else 3
            landed((d, 0), 0)
            landed((0, d), 1)
            for way in range(2):
                push((d, 0), (d, 1 + 2 * way), 0, 2, 1, way)
                push((0, d), (1 + 2 * way, d), 2, 2, 0, way)
            if d == 3:
                push((0, 3), (0, 2), 3, 1, 1, 1)
        if part == "far b":
            push((0, 1), (0, 2), 2, 1, 1, 0)
        if part == "odd":
            landed((0, 2), 1)
            for way in range(2):
                push((0, 2), (1 + 2 * way, 2), 2, 2, 0, way)
            for dx, dy in DIAGONAL:
                landed((dx, dy), 0)
                push((dx, dy), (dx, 2), dy // 2, 1, 1, dy // 2)
        if part == "own a":
            for way in range(2):
                push((0, 0), (0, 1 + 2 * way), 0, 2, 1, way)
        if part == "even":
            for way in range(2):
                landed((1 + 2 * way, 0), 1)
                for half in range(2):
                    push((1 + 2 * way, 0), (2, 0), 2 * half + way, 1, 0, way)
        if part == "odd done":
            for dx, dy in DIAGONAL:
                landed((dx, dy), 1)
                push((dx, dy), (2, dy), 2 + dx // 2, 1, 0, dx // 2)
            for dx in (1, 3):
                landed((dx, 2), 1)
                push((dx, 2), (2, 2), 2 + dx // 2, 1, 0, dx // 2)
                landed((dx, 2), 0)
        if part == "even 1":
            landed((2, 0), 0)
            for way in range(2):
                push((2, 0), (2, 1 + 2 * way), 0, 2, 1, way)
            for way in range(2):
                landed((0, 1 + 2 * way), 0)
                push((0, 1 + 2 * way), (0, 2), way, 1, 1, way)
        if part == "even 2":
            for way in range(2):
                landed((2, 1 + 2 * way), 0)
                push((2, 1 + 2 * way), (2, 2), way, 1, 1, way)
        if part == "even done":
            landed((2, 0), 1)
            landed((0, 2), 0)
            for way in range(2):
                landed((2, 1 + 2 * way), 1)
                landed((2, 2), way)

    def at_point(point):
        for part in PLACES[point]:
            weights(part)

    at_point("start")
    all_of_them = landing.at[pl.ds(0, 31)]
    wait_for(all_of_them, tsem.at[1])
    tab_vmem[...] = row_table(landing[:, 0, :], dp)
    to_scalar = pltpu.make_async_copy(tab_vmem, tab, tsem.at[2])
    to_scalar.start()
    to_scalar.wait()

    stores = (k_ref, v_ref)
    gathered = (gk, gv)
    first_at = (x, y)
    second_at = (y, x)
    started = []

    def send(*args):
        started.append(remote(*args))
        started[-1].start()

    def at(kv, which, way):
        return beside(kv ^ which, way)

    mine_rows = pl.ds(pl.multiple_of(core * 256, 256), 256)
    other_rows = pl.ds(pl.multiple_of((1 - core) * 256, 256), 256)
    my_two = pl.ds(pl.multiple_of(core * 2, 2), 2)
    other_two = pl.ds(pl.multiple_of((1 - core) * 2, 2), 2)
    for kv in range(2):
        for i in range(2):
            picked[kv, i] = stores[kv][jnp.bitwise_and(tab[0, 2 + i], 3)]
            gathered[kv][first_at[kv], core * 2 + i] = picked[kv, i, mine_rows, :]
        send(
            picked.at[kv, pl.ds(0, 2), other_rows], gathered[kv].at[first_at[kv], my_two],
            psend.at[kv], precv.at[kv], partner,
        )

    def pair(kv, place, half):
        return gathered[kv].at[place, pl.ds(2 * half, 2)]

    for kv in range(2):
        wait_for(gathered[kv].at[first_at[kv], other_two], precv.at[kv])
        for turn in range(2):
            for way in range(2):
                half = turn ^ way
                block = pair(kv, first_at[kv], half)
                send(block, block, asend.at[kv, way, half], arecv.at[kv, way, half], at(kv, 0, way))
    at_point("gather")
    for kv in range(2):
        for way in range(2):
            block = pair(kv, lax.rem(first_at[kv] + (3 if way == 0 else 1), 4), way)
            wait_for(block, arecv.at[kv, way, way])
            send(block, block, fsend.at[kv, way], frecv.at[kv, way], at(kv, 0, way))
    at_point("forward")
    for kv in range(2):
        for way in range(2):
            place = lax.rem(first_at[kv] + (3 if way == 0 else 1), 4)
            wait_for(pair(kv, place, 1 - way), arecv.at[kv, way, 1 - way])
        for way in range(2):
            wait_for(pair(kv, lax.rem(first_at[kv] + 2, 4), way), frecv.at[kv, way])

    def candidate(kv, step, slot):
        to = lax.rem(second_at[kv] + step, 4)
        chip = to * 4 + x if kv == 0 else y * 4 + to
        code = tab[chip * 2 + slot // 2, slot % 2]
        rank = jnp.bitwise_and(code, 1)
        source_core = jnp.bitwise_and(jnp.right_shift(code, 1), 1)
        source_x = jnp.bitwise_and(jnp.right_shift(code, 2), 3)
        source_y = jnp.bitwise_and(jnp.right_shift(code, 4), 3)
        one, two = (source_x, source_y) if kv == 0 else (source_y, source_x)
        return gathered[kv][one, source_core * 2 + rank], two

    for kv in range(2):
        for way in range(2):
            for j in range(2):
                s1[kv, way, j] = candidate(kv, 2, 2 * way + j)[0]
            send(s1.at[kv, way], r1.at[kv, way], s1s.at[kv, way], s1r.at[kv, way], at(kv, 1, way))
    at_point("select")
    for turn in range(2):
        for kv in range(2):
            for way in range(2):
                half = 1 - way if turn == 0 else way
                if turn == 1:
                    wait_for(r1.at[kv, way], s1r.at[kv, way])
                for j in range(2):
                    slot = 2 * half + j
                    value, two = candidate(kv, 1 + 2 * way, slot)
                    if turn == 1:
                        value = jnp.where(two == second_at[kv], value, r1[kv, way, j])
                    s2[kv, way, slot] = value
                two_slots = pl.ds(2 * half, 2)
                send(
                    s2.at[kv, way, two_slots], r2.at[kv, way, two_slots],
                    s2s.at[kv, way, half], s2r.at[kv, way, half], at(kv, 1, way),
                )
        at_point("relay" if turn == 0 else "own")
    whole = (all_k, all_v)
    for kv in range(2):
        for half in range(2):
            for way in range(2):
                wait_for(r2.at[kv, way, pl.ds(2 * half, 2)], s2r.at[kv, way, half])
            for j in range(2):
                slot = 2 * half + j
                value, two = candidate(kv, 0, slot)
                away = lax.rem(two - second_at[kv] + 4, 4)
                first = (away == 3) | (away == 2) if half == 0 else away == 3
                arrived = jnp.where(first, r2[kv, 0, slot], r2[kv, 1, slot])
                fin[kv, slot] = jnp.where(away == 0, value, arrived)
        send(fin.at[kv, other_two], xin.at[kv], xs.at[kv], xr.at[kv], partner)
        for i in range(2):
            whole[kv][i, mine_rows, :] = fin[kv, core * 2 + i]
            whole[kv][i, pl.ds(CACHE, STRETCH), :] = (new_k_ref, new_v_ref)[kv][i]
    at_point("swap")
    for kv in range(2):
        wait_for(xin.at[kv], xr.at[kv])
        for i in range(2):
            whole[kv][i, other_rows, :] = xin[kv, i]

    scale = 1.0 / math.sqrt(HEAD_DIM)
    span = CACHE + STRETCH
    exchange = []
    for i in range(2):
        position = lax.broadcasted_iota(jnp.int32, (2 * STRETCH, span), 1)
        token = lax.rem(lax.broadcasted_iota(jnp.int32, (2 * STRETCH, span), 0), STRETCH)
        bound = jnp.where(position < CACHE, tab[0, 4 + i], token + CACHE + 1)
        penalty = jnp.where(position < bound, 0.0, -1e30)
        tokens = pl.ds(i * STRETCH, STRETCH)

        def heads(c, carry):
            both = pl.ds(pl.multiple_of(c * 256, 256), 256)
            q = q_ref[i, :, both]
            q = jnp.concatenate([q[:, :HEAD_DIM], q[:, HEAD_DIM:]], axis=0)
            scores = lax.dot_general(
                q, all_k[i], (((1,), (1,)), ((), ())), preferred_element_type=jnp.float32
            )
            scores = scores * scale + penalty
            raised = jnp.exp(scores - jnp.max(scores, axis=1, keepdims=True))
            total = jnp.sum(raised, axis=1, keepdims=True)
            mixed = jnp.dot(
                raised.astype(jnp.bfloat16), all_v[i], preferred_element_type=jnp.float32
            )
            mixed = (mixed / total).astype(jnp.bfloat16)
            a_buf[core, tokens, both] = jnp.concatenate(
                [mixed[:STRETCH], mixed[STRETCH:]], axis=1
            )
            return carry

        lax.fori_loop(0, 4, heads, 0)
        exchange.append(
            remote(
                a_buf.at[core, tokens], a_buf.at[core, tokens],
                esem.at[0, i], esem.at[1, i], partner,
            )
        )
        exchange[-1].start()
        at_point("row%d" % i)
    weights("odd done")

    def product(d, h, k):
        goal = lax.rem(z + d, 8)
        dx = lax.rem(x - 2 * lax.rem(goal, 2) - k + 4, 4)
        dy = lax.rem(y - goal // 2 + 4, 4)
        return jnp.dot(a_buf[h], w_buf[dy * 4 + dx], preferred_element_type=jnp.float32)

    def columns_of(round_):
        return lax.rem(x + 1 + round_, 2)

    def final(round_):
        k = columns_of(round_)

        def total_of(h):
            value = product(0, h, k)
            for way, end in ((0, 3 - h), (1, 2 + h)):
                for u in range(2):
                    rows = pl.ds(u * 128, 128)
                    wait_for(
                        r_buf.at[end, round_, way, h, rows], rsem.at[end, round_, way, h, u]
                    )
                value += r_buf[end, round_, way, h].astype(jnp.float32)
            return value

        x_buf[0, round_] = total_of(1 - core).astype(jnp.bfloat16)
        remote(
            x_buf.at[0, round_], x_buf.at[1, round_], xsend.at[round_], xrecv.at[round_], partner
        ).start()
        columns = pl.ds(pl.multiple_of((2 * k + core) * 256, 256), 256)
        out_ref[:, columns] = (
            skip_ref[:, columns].astype(jnp.float32) + total_of(core)
        ).astype(jnp.bfloat16)

    def step(i, carry):
        round_ = i // 4
        s = lax.rem(i, 4)
        k = columns_of(round_)
        for when, part in ((1, "even 1"), (3, "even 2"), (4, "even done")):

            @pl.when(i == when)
            def _():
                weights(part)

        @pl.when(i == 6)
        def _():
            final(0)

        for turn in range(2):
            h = lax.rem(core + turn, 2)
            if turn == 1:

                @pl.when(i == 0)
                def _():
                    for row in range(2):
                        rows = pl.ds(row * STRETCH, STRETCH)
                        wait_for(a_buf.at[1 - core, rows], esem.at[1, row])

            for way in range(2):
                d = 4 - s - h if way == 0 else 4 + s + 1 - h

                @pl.when((d > 0) & (d < 8))
                def _():
                    place = ((s * 2 + round_) * 2 + way) * 2 + h
                    t_buf[...] = product(d, h, k)
                    for u in range(2):
                        rows = pl.ds(u * 128, 128)

                        @pl.when(s == 0)
                        def _():
                            s_buf[place, rows, :] = t_buf[rows, :].astype(jnp.bfloat16)

                        @pl.when(s > 0)
                        def _():
                            before = jnp.maximum(s - 1, 0)
                            wait_for(
                                r_buf.at[before, round_, way, h, rows],
                                rsem.at[before, round_, way, h, u],
                            )
                            s_buf[place, rows, :] = (
                                t_buf[rows, :]
                                + r_buf[before, round_, way, h, rows, :].astype(jnp.float32)
                            ).astype(jnp.bfloat16)

                        remote(
                            s_buf.at[place, rows], r_buf.at[s, round_, way, h, rows],
                            ssem, rsem.at[s, round_, way, h, u],
                            (dp, lax.rem(z + 1 + 6 * way, 8)),
                        ).start()
        return carry

    lax.fori_loop(0, 8, step, 0)
    final(1)
    for round_ in range(2):
        k = columns_of(round_)
        wait_for(x_buf.at[1, round_], xrecv.at[round_])
        columns = pl.ds(pl.multiple_of((2 * k + 1 - core) * 256, 256), 256)
        out_ref[:, columns] = (
            skip_ref[:, columns].astype(jnp.float32) + x_buf[1, round_].astype(jnp.float32)
        ).astype(jnp.bfloat16)
        wait_for(x_buf.at[0, round_], xsend.at[round_])
    for each in started + exchange:
        each.wait_send()
    wait_for(s_buf.at[pl.ds(0, 28)], ssem)
    wait_for(all_of_them, tsem.at[0])
    for axis in range(2):
        for way in range(2):
            wait_for(w_buf.at[pl.ds(0, 15), pl.ds(0, 256)], wsend.at[axis, way])


def local(
    question_vectors,
    arriving_lookup_vectors,
    arriving_content_vectors,
    earlier_lookup_store,
    earlier_content_store,
    stored_extent,
    kept_parent,
    final_projection_matrix,
    skip_stream,
):
    mine = jnp.concatenate([kept_parent, stored_extent])
    mine = jnp.broadcast_to(jnp.pad(mine, (0, 122))[None], (8, 128))
    vmem = pl.BlockSpec(memory_space=pltpu.VMEM)
    dma = pltpu.SemaphoreType.DMA
    bf16 = jnp.bfloat16
    item = (256, 128)
    return pl.pallas_call(
        layer_kernel,
        out_shape=jax.ShapeDtypeStruct(skip_stream.shape, skip_stream.dtype),
        in_specs=[vmem] * 8,
        out_specs=vmem,
        scratch_shapes=[
            pltpu.VMEM((32, 8, 128), jnp.int32),
            pltpu.VMEM((32, 128), jnp.int32),
            pltpu.SMEM((32, 128), jnp.int32),
            pltpu.VMEM((16, 1024, 256), bf16),
            pltpu.VMEM((2, 2, 512, 128), bf16),
            pltpu.VMEM((4, 4) + item, bf16),
            pltpu.VMEM((4, 4) + item, bf16),
            pltpu.VMEM((2, 2, 2) + item, bf16),
            pltpu.VMEM((2, 2, 2) + item, bf16),
            pltpu.VMEM((2, 2, 4) + item, bf16),
            pltpu.VMEM((2, 2, 4) + item, bf16),
            pltpu.VMEM((2, 4) + item, bf16),
            pltpu.VMEM((2, 2) + item, bf16),
            pltpu.VMEM((2, CACHE + STRETCH, HEAD_DIM), bf16),
            pltpu.VMEM((2, CACHE + STRETCH, HEAD_DIM), bf16),
            pltpu.VMEM((2, 256, 1024), bf16),
            pltpu.VMEM((32, 256, 256), bf16),
            pltpu.VMEM((4, 2, 2, 2, 256, 256), bf16),
            pltpu.VMEM((256, 256), jnp.float32),
            pltpu.VMEM((2, 2, 256, 256), bf16),
            dma((3,)), dma((15, 2)), dma((2, 2)),
            dma((2,)), dma((2,)),
            dma((2, 2, 2)), dma((2, 2, 2)),
            dma((2, 2)), dma((2, 2)),
            dma((2, 2)), dma((2, 2)),
            dma((2, 2, 2)), dma((2, 2, 2)),
            dma((2,)), dma((2,)),
            dma((4, 2, 2, 2, 2)), dma, dma((2, 2)), dma((2,)), dma((2,)),
        ],
        compiler_params=pltpu.CompilerParams(
            collective_id=1, has_side_effects=True, vmem_limit_bytes=56 * 1024 * 1024
        ),
        cost_estimate=pl.CostEstimate(
            flops=10 << 30, bytes_accessed=8 << 20, transcendentals=2 << 20
        ),
    )(
        mine,
        question_vectors,
        arriving_lookup_vectors,
        arriving_content_vectors,
        earlier_lookup_store,
        earlier_content_store,
        final_projection_matrix,
        skip_stream,
    )


def solution(mesh):
    return jax.shard_map(
        local,
        mesh=mesh,
        in_specs=(
            P("dp", None, "tensor"),
            P("dp", None, "tensor"),
            P("dp", None, "tensor"),
            P("dp", None, "tensor"),
            P("dp", None, "tensor"),
            P("dp"),
            P("dp"),
            P("tensor", "dp"),
            P("dp", "tensor"),
        ),
        out_specs=P("dp", "tensor"),
        check_vma=False,
    )
```

```python
import math

import jax
import jax.numpy as jnp
from jax import lax
from jax.experimental import pallas as pl
from jax.experimental.pallas import tpu as pltpu
from jax.sharding import PartitionSpec as P

HEAD_DIM = 128
STRETCH = 128
CACHE = 512
MESH = pl.DeviceIdType.MESH


def spots():
    dp = lax.axis_index("dp")
    core = lax.rem(dp, 2)
    chip = dp // 2
    return dp, lax.axis_index("tensor"), core, lax.rem(chip, 4), chip // 4


def beside(axis, way):
    dp, z, core, x, y = spots()
    step = 1 + 2 * way
    nx = lax.rem(x + step, 4) if axis == 0 else x
    ny = y if axis == 0 else lax.rem(y + step, 4)
    return ((ny * 4 + nx) * 2 + core, z)


def remote(src, dst, send, recv, target):
    return pltpu.make_async_remote_copy(
        src_ref=src, dst_ref=dst, send_sem=send, recv_sem=recv,
        device_id=target, device_id_type=MESH,
    )


def wait_for(ref, sem):
    pltpu.make_async_copy(ref, ref, sem).wait()


def row_table(table, dp):
    lane = lax.broadcasted_iota(jnp.int32, (32, 128), 1)
    line = lax.broadcasted_iota(jnp.int32, (32, 128), 0)

    def column(k):
        return jnp.sum(jnp.where(lane == k, table, 0), axis=1, keepdims=True)

    parents = [column(0), column(1)]
    rows = [
        jnp.sum(jnp.where(lane == line, parent, 0), axis=0, keepdims=True) for parent in parents
    ]
    result = jnp.zeros((32, 128), jnp.int32)
    low = jnp.full((1, 1), 9, jnp.int32)
    high = jnp.full((1, 1), -1, jnp.int32)
    for i in range(2):
        before = jnp.zeros((32, 1), jnp.int32)
        for row in rows:
            same = jnp.right_shift(row, 2) == jnp.right_shift(parents[i], 2)
            hit = same & (row < parents[i]) & (lane < 32)
            before += jnp.sum(jnp.where(hit, 1, 0), axis=1, keepdims=True)
        code = jnp.right_shift(parents[i], 2) * 2 + before
        result = jnp.where(lane == i, code, result)
        here = jnp.right_shift(parents[i], 2) == dp
        slot = jnp.bitwise_and(parents[i], 3)
        low = jnp.minimum(low, jnp.min(jnp.where(here, slot, 9), axis=0, keepdims=True))
        high = jnp.maximum(high, jnp.max(jnp.where(here, slot, -1), axis=0, keepdims=True))
        wanted = jnp.sum(jnp.where(line[:, :1] == dp, parents[i], 0), axis=0, keepdims=True)
        found = (lane >= 2) & (lane < 6) & (line * 4 + lane - 2 == wanted)
        extent = jnp.sum(
            jnp.sum(jnp.where(found, table, 0), axis=0, keepdims=True), axis=1, keepdims=True
        )
        result = jnp.where(lane == 4 + i, extent, result)
    result = jnp.where(lane == 2, jnp.minimum(low, 3), result)
    return jnp.where(lane == 3, jnp.maximum(high, 0), result)


NEAR = [(1, 0), (3, 0), (0, 1), (0, 3)]
DIAGONAL = [(1, 1), (1, 3), (3, 1), (3, 3)]
FAR = [(2, 0), (0, 2), (2, 1), (2, 3), (1, 2), (3, 2), (2, 2)]
PLACES = {'start': [('own a', 0), ('own b', 0)], 'gather': [], 'forward': [('side', 0)], 'select': [('far', 0)], 'relay': [], 'own': [('diagonal', 0), ('far side', 0), ('own a', 1)], 'swap': [('corner', 0)], 'row0': [('own b', 1)], 'row1': [('done', 0)]}
SERVICES = {
    (0, 1): ("side", 1),
    (1, 0): ("far", 1),
    (2, 0): ("diagonal", 1),
    (2, 1): ("far side", 1),
    (3, 1): ("corner", 1),
    (4, 0): ("done", 1),
}


def layer_kernel(
    parent_ref, extent_ref, q_hbm, new_k_hbm, new_v_hbm, k_hbm, v_hbm, own_ref, skip_hbm, out_ref,
    landing, tab_vmem, tab, w_buf, q_ref, new_k_ref, new_v_ref, k_ref, v_ref, skip_ref,
    picked, gk, gv, s1, r1, s2, r2, fin, xin, all_k, all_v,
    a_buf, s_buf, r_buf, t_buf, x_buf,
    tsem, lsem, wsem, wsend,
    psend, precv, asend, arecv, fsend, frecv, s1s, s1r, s2s, s2r, xs, xr,
    rsem, ssem, esem, xsend, xrecv,
):
    dp, z, core, x, y = spots()
    chip = dp // 2
    partner = (dp + 1 - 2 * core, z)
    barrier = pltpu.get_barrier_semaphore()

    def slot_of(place):
        return place[1] * 4 + place[0]

    def sem_of(place, half, part):
        return wsem.at[(NEAR + DIAGONAL + FAR).index(place), half, part]

    def push(source, to, first, count, axis, way, part):
        rows = pl.ds(first * 256, count * 256)
        remote(
            w_buf.at[part, slot_of(source), rows], w_buf.at[part, slot_of(to), rows],
            wsend.at[axis, way], sem_of(to, first // 2, part), beside(axis, way),
        ).start()

    def landed(place, half, part):
        wait_for(
            w_buf.at[part, slot_of(place), pl.ds(half * 512, 512)], sem_of(place, half, part)
        )

    def weights(stage, part):
        if stage == "own a":
            for way in range(2):
                push((0, 0), (1 + 2 * way, 0), 0, 2, 0, way, part)
                push((0, 0), (0, 1 + 2 * way), 2, 2, 1, way, part)
        if stage == "own b":
            for way in range(2):
                push((0, 0), (1 + 2 * way, 0), 2, 2, 0, way, part)
                push((0, 0), (0, 1 + 2 * way), 0, 2, 1, way, part)
        if stage == "side":
            for d in (1, 3):
                landed((d, 0), 0, part)
                landed((0, d), 1, part)
                for way in range(2):
                    push((d, 0), (d, 1 + 2 * way), 0, 2, 1, way, part)
                    push((0, d), (1 + 2 * way, d), 2, 2, 0, way, part)
        if stage == "far":
            for way in range(2):
                near = 1 + 2 * way
                landed((near, 0), 1, part)
                landed((0, near), 0, part)
                push((near, 0), (2, 0), way, 1, 0, way, part)
                push((0, near), (0, 2), 2 + way, 1, 1, way, part)
                push((near, 0), (2, 0), 2 + way, 1, 0, way, part)
                push((0, near), (0, 2), way, 1, 1, way, part)
        if stage == "diagonal":
            for dx, dy in DIAGONAL:
                for half in range(2):
                    landed((dx, dy), half, part)
                push((dx, dy), (dx, 2), dy // 2, 1, 1, dy // 2, part)
                push((dx, dy), (2, dy), 2 + dx // 2, 1, 0, dx // 2, part)
        if stage == "far side":
            landed((2, 0), 0, part)
            landed((0, 2), 1, part)
            for way in range(2):
                push((2, 0), (2, 1 + 2 * way), 0, 2, 1, way, part)
                push((0, 2), (1 + 2 * way, 2), 2, 2, 0, way, part)
        if stage == "corner":
            for way in range(2):
                side = 1 + 2 * way
                landed((2, side), 0, part)
                push((2, side), (2, 2), way, 1, 1, way, part)
                landed((side, 2), 1, part)
                push((side, 2), (2, 2), 2 + way, 1, 0, way, part)
        if stage == "done":
            landed((2, 0), 1, part)
            landed((0, 2), 0, part)
            for way in range(2):
                side = 1 + 2 * way
                landed((2, side), 1, part)
                landed((side, 2), 0, part)
                landed((2, 2), way, part)

    def at_point(point):
        for stage, part in PLACES[point]:
            weights(stage, part)

    def same_core(step):
        return (lax.rem(dp + 2 * step, 32), z)

    def greet(step, carry):
        pl.semaphore_signal(barrier, inc=1, device_id=same_core(step), device_id_type=MESH)
        return carry

    lax.fori_loop(1, 16, greet, 0)
    for other in (partner, (dp, lax.rem(z + 1, 8)), (dp, lax.rem(z + 7, 8))):
        pl.semaphore_signal(barrier, inc=1, device_id=other, device_id_type=MESH)
    loads = [
        pltpu.make_async_copy(source, target, lsem.at[n])
        for n, (source, target) in enumerate(
            [
                (k_hbm, k_ref), (v_hbm, v_ref),
                (own_ref.at[:, pl.ds(0, 128)], w_buf.at[0, 0]),
                (own_ref.at[:, pl.ds(128, 128)], w_buf.at[1, 0]), (q_hbm, q_ref),
                (new_k_hbm, new_k_ref), (new_v_hbm, new_v_ref), (skip_hbm, skip_ref),
            ]
        )
    ]
    for load in loads:
        load.start()
    lane = lax.broadcasted_iota(jnp.int32, (8, 128), 1)
    numbers = jnp.zeros((8, 128), jnp.int32)
    for n in range(6):
        number = parent_ref[n] if n < 2 else extent_ref[n - 2]
        numbers = jnp.where(lane == n, number, numbers)
    landing[dp] = numbers
    loads[2].wait()
    loads[3].wait()
    pl.semaphore_wait(barrier, 18)

    beside_me = remote(landing.at[dp], landing.at[dp], tsem.at[3], tsem.at[4], partner)
    beside_me.start()
    beside_me.wait_recv()
    both_cores = landing.at[pl.ds(pl.multiple_of(chip * 2, 2), 2)]

    def share(step, carry):
        remote(both_cores, both_cores, tsem.at[0], tsem.at[1], same_core(step)).start()
        return carry

    lax.fori_loop(1, 16, share, 0)
    at_point("start")

    all_of_them = landing.at[pl.ds(0, 30)]
    wait_for(all_of_them, tsem.at[1])
    tab_vmem[...] = row_table(landing[:, 0, :], dp)
    to_scalar = pltpu.make_async_copy(tab_vmem, tab, tsem.at[2])
    to_scalar.start()
    to_scalar.wait()
    for load in loads[:2]:
        load.wait()

    stores = (k_ref, v_ref)
    gathered = (gk, gv)
    first_at = (x, y)
    second_at = (y, x)
    started = []

    def send(*args):
        started.append(remote(*args))
        started[-1].start()

    def at(kv, which, way):
        return beside(kv ^ which, way)

    mine_rows = pl.ds(pl.multiple_of(core * 256, 256), 256)
    other_rows = pl.ds(pl.multiple_of((1 - core) * 256, 256), 256)
    my_two = pl.ds(pl.multiple_of(core * 2, 2), 2)
    other_two = pl.ds(pl.multiple_of((1 - core) * 2, 2), 2)
    for kv in range(2):
        for i in range(2):
            picked[kv, i] = stores[kv][jnp.bitwise_and(tab[0, 2 + i], 3)]
            gathered[kv][first_at[kv], core * 2 + i] = picked[kv, i, mine_rows, :]
        send(
            picked.at[kv, pl.ds(0, 2), other_rows], gathered[kv].at[first_at[kv], my_two],
            psend.at[kv], precv.at[kv], partner,
        )

    def pair(kv, place, half):
        return gathered[kv].at[place, pl.ds(2 * half, 2)]

    for kv in range(2):
        wait_for(gathered[kv].at[first_at[kv], other_two], precv.at[kv])
        for turn in range(2):
            for way in range(2):
                half = turn ^ way
                block = pair(kv, first_at[kv], half)
                send(block, block, asend.at[kv, way, half], arecv.at[kv, way, half], at(kv, 0, way))
    at_point("gather")
    for kv in range(2):
        for way in range(2):
            block = pair(kv, lax.rem(first_at[kv] + (3 if way == 0 else 1), 4), way)
            wait_for(block, arecv.at[kv, way, way])
            send(block, block, fsend.at[kv, way], frecv.at[kv, way], at(kv, 0, way))
    at_point("forward")
    for kv in range(2):
        for way in range(2):
            place = lax.rem(first_at[kv] + (3 if way == 0 else 1), 4)
            wait_for(pair(kv, place, 1 - way), arecv.at[kv, way, 1 - way])
        for way in range(2):
            wait_for(pair(kv, lax.rem(first_at[kv] + 2, 4), way), frecv.at[kv, way])

    def candidate(kv, step, slot):
        to = lax.rem(second_at[kv] + step, 4)
        chip = to * 4 + x if kv == 0 else y * 4 + to
        code = tab[chip * 2 + slot // 2, slot % 2]
        rank = jnp.bitwise_and(code, 1)
        source_core = jnp.bitwise_and(jnp.right_shift(code, 1), 1)
        source_x = jnp.bitwise_and(jnp.right_shift(code, 2), 3)
        source_y = jnp.bitwise_and(jnp.right_shift(code, 4), 3)
        one, two = (source_x, source_y) if kv == 0 else (source_y, source_x)
        return gathered[kv][one, source_core * 2 + rank], two

    for kv in range(2):
        for way in range(2):
            for j in range(2):
                s1[kv, way, j] = candidate(kv, 2, 2 * way + j)[0]
            send(s1.at[kv, way], r1.at[kv, way], s1s.at[kv, way], s1r.at[kv, way], at(kv, 1, way))
    at_point("select")
    for turn in range(2):
        for kv in range(2):
            for way in range(2):
                half = 1 - way if turn == 0 else way
                if turn == 1:
                    wait_for(r1.at[kv, way], s1r.at[kv, way])
                for j in range(2):
                    slot = 2 * half + j
                    value, two = candidate(kv, 1 + 2 * way, slot)
                    if turn == 1:
                        value = jnp.where(two == second_at[kv], value, r1[kv, way, j])
                    s2[kv, way, slot] = value
                two_slots = pl.ds(2 * half, 2)
                send(
                    s2.at[kv, way, two_slots], r2.at[kv, way, two_slots],
                    s2s.at[kv, way, half], s2r.at[kv, way, half], at(kv, 1, way),
                )
        at_point("relay" if turn == 0 else "own")
    whole = (all_k, all_v)
    for load in loads[4:]:
        load.wait()
    for kv in range(2):
        for half in range(2):
            for way in range(2):
                wait_for(r2.at[kv, way, pl.ds(2 * half, 2)], s2r.at[kv, way, half])
            for j in range(2):
                slot = 2 * half + j
                value, two = candidate(kv, 0, slot)
                away = lax.rem(two - second_at[kv] + 4, 4)
                first = (away == 3) | (away == 2) if half == 0 else away == 3
                arrived = jnp.where(first, r2[kv, 0, slot], r2[kv, 1, slot])
                fin[kv, slot] = jnp.where(away == 0, value, arrived)
        send(fin.at[kv, other_two], xin.at[kv], xs.at[kv], xr.at[kv], partner)
        for i in range(2):
            whole[kv][i, mine_rows, :] = fin[kv, core * 2 + i]
            whole[kv][i, pl.ds(CACHE, STRETCH), :] = (new_k_ref, new_v_ref)[kv][i]
    at_point("swap")
    for kv in range(2):
        wait_for(xin.at[kv], xr.at[kv])
        for i in range(2):
            whole[kv][i, other_rows, :] = xin[kv, i]

    scale = 1.0 / math.sqrt(HEAD_DIM)
    span = CACHE + STRETCH
    exchange = []
    for i in range(2):
        position = lax.broadcasted_iota(jnp.int32, (2 * STRETCH, span), 1)
        token = lax.rem(lax.broadcasted_iota(jnp.int32, (2 * STRETCH, span), 0), STRETCH)
        bound = jnp.where(position < CACHE, tab[0, 4 + i], token + CACHE + 1)
        penalty = jnp.where(position < bound, 0.0, -1e30)
        tokens = pl.ds(i * STRETCH, STRETCH)

        def heads(c, carry):
            both = pl.ds(pl.multiple_of(c * 256, 256), 256)
            q = q_ref[i, :, both]
            q = jnp.concatenate([q[:, :HEAD_DIM], q[:, HEAD_DIM:]], axis=0)
            scores = lax.dot_general(
                q, all_k[i], (((1,), (1,)), ((), ())), preferred_element_type=jnp.float32
            )
            scores = scores * scale + penalty
            raised = jnp.exp(scores - jnp.max(scores, axis=1, keepdims=True))
            total = jnp.sum(raised, axis=1, keepdims=True)
            mixed = jnp.dot(
                raised.astype(jnp.bfloat16), all_v[i], preferred_element_type=jnp.float32
            )
            mixed = (mixed / total).astype(jnp.bfloat16)
            a_buf[core, tokens, both] = jnp.concatenate(
                [mixed[:STRETCH], mixed[STRETCH:]], axis=1
            )
            return carry

        lax.fori_loop(0, 4, heads, 0)
        exchange.append(
            remote(
                a_buf.at[core, tokens], a_buf.at[core, tokens],
                esem.at[0, i], esem.at[1, i], partner,
            )
        )
        exchange[-1].start()
        at_point("row%d" % i)

    def product(d, h, part):
        goal = lax.rem(z + d, 8)
        dy = lax.rem(y - goal // 2 + 4, 4)
        columns = []
        for k in range(2):
            dx = lax.rem(x - 2 * lax.rem(goal, 2) - k + 4, 4)
            columns.append(w_buf[part, dy * 4 + dx])
        return jnp.dot(
            a_buf[h], jnp.concatenate(columns, axis=1), preferred_element_type=jnp.float32
        )

    def finish(round_, owner, value):
        for k in range(2):
            columns = pl.ds(pl.multiple_of((2 * k + owner) * 256 + round_ * 128, 128), 128)
            out_ref[:, columns] = (
                skip_ref[:, columns].astype(jnp.float32)
                + value[:, k * 128 : k * 128 + 128].astype(jnp.float32)
            ).astype(jnp.bfloat16)

    def final(round_):
        def total_of(h):
            value = product(0, h, round_)
            for way, end in ((0, 3 - h), (1, 2 + h)):
                for u in range(2):
                    rows = pl.ds(u * 128, 128)
                    wait_for(
                        r_buf.at[end, round_, way, h, rows], rsem.at[end, round_, way, h, u]
                    )
                value += r_buf[end, round_, way, h].astype(jnp.float32)
            return value

        x_buf[0, round_] = total_of(1 - core).astype(jnp.bfloat16)
        remote(
            x_buf.at[0, round_], x_buf.at[1, round_], xsend.at[round_], xrecv.at[round_], partner
        ).start()
        finish(round_, core, total_of(core))

    def step(i, carry):
        round_ = i // 4
        s = lax.rem(i, 4)
        @pl.when(i == 6)
        def _():
            final(0)

        for turn in range(2):
            h = lax.rem(core + turn, 2)
            for (when, where), (stage, part) in SERVICES.items():
                if where == turn:

                    @pl.when(i == when)
                    def _():
                        weights(stage, part)

            if turn == 1:

                @pl.when(i == 0)
                def _():
                    for row in range(2):
                        rows = pl.ds(row * STRETCH, STRETCH)
                        wait_for(a_buf.at[1 - core, rows], esem.at[1, row])

            for way in range(2):
                d = 4 - s - h if way == 0 else 4 + s + 1 - h

                @pl.when((d > 0) & (d < 8))
                def _():
                    place = ((s * 2 + round_) * 2 + way) * 2 + h
                    t_buf[...] = product(d, h, round_)
                    for u in range(2):
                        rows = pl.ds(u * 128, 128)

                        @pl.when(s == 0)
                        def _():
                            s_buf[place, rows, :] = t_buf[rows, :].astype(jnp.bfloat16)

                        @pl.when(s > 0)
                        def _():
                            before = jnp.maximum(s - 1, 0)
                            wait_for(
                                r_buf.at[before, round_, way, h, rows],
                                rsem.at[before, round_, way, h, u],
                            )
                            s_buf[place, rows, :] = (
                                t_buf[rows, :]
                                + r_buf[before, round_, way, h, rows, :].astype(jnp.float32)
                            ).astype(jnp.bfloat16)

                        remote(
                            s_buf.at[place, rows], r_buf.at[s, round_, way, h, rows],
                            ssem, rsem.at[s, round_, way, h, u],
                            (dp, lax.rem(z + 1 + 6 * way, 8)),
                        ).start()
        return carry

    lax.fori_loop(0, 8, step, 0)
    final(1)
    for round_ in range(2):
        wait_for(x_buf.at[1, round_], xrecv.at[round_])
        finish(round_, 1 - core, x_buf[1, round_])
        wait_for(x_buf.at[0, round_], xsend.at[round_])
    for each in started + exchange:
        each.wait_send()
    wait_for(s_buf.at[pl.ds(0, 28)], ssem)
    wait_for(all_of_them, tsem.at[0])
    beside_me.wait_send()
    for axis in range(2):
        for way in range(2):
            wait_for(w_buf.at[0, pl.ds(0, 15), pl.ds(0, 512)], wsend.at[axis, way])


def local(
    question_vectors,
    arriving_lookup_vectors,
    arriving_content_vectors,
    earlier_lookup_store,
    earlier_content_store,
    stored_extent,
    kept_parent,
    final_projection_matrix,
    skip_stream,
):
    vmem = pl.BlockSpec(memory_space=pltpu.VMEM)
    dma = pltpu.SemaphoreType.DMA
    bf16 = jnp.bfloat16
    item = (256, 128)
    return pl.pallas_call(
        layer_kernel,
        out_shape=jax.ShapeDtypeStruct(skip_stream.shape, skip_stream.dtype),
        in_specs=[pl.BlockSpec(memory_space=pltpu.SMEM)] * 2
        + [pl.BlockSpec(memory_space=pl.ANY)] * 7,
        out_specs=vmem,
        scratch_shapes=[
            pltpu.VMEM((32, 8, 128), jnp.int32),
            pltpu.VMEM((32, 128), jnp.int32),
            pltpu.SMEM((32, 128), jnp.int32),
            pltpu.VMEM((2, 16, 1024, 128), bf16),
            pltpu.VMEM(question_vectors.shape, bf16),
            pltpu.VMEM(arriving_lookup_vectors.shape, bf16),
            pltpu.VMEM(arriving_content_vectors.shape, bf16),
            pltpu.VMEM(earlier_lookup_store.shape, bf16),
            pltpu.VMEM(earlier_content_store.shape, bf16),
            pltpu.VMEM(skip_stream.shape, bf16),
            pltpu.VMEM((2, 2, 512, 128), bf16),
            pltpu.VMEM((4, 4) + item, bf16),
            pltpu.VMEM((4, 4) + item, bf16),
            pltpu.VMEM((2, 2, 2) + item, bf16),
            pltpu.VMEM((2, 2, 2) + item, bf16),
            pltpu.VMEM((2, 2, 4) + item, bf16),
            pltpu.VMEM((2, 2, 4) + item, bf16),
            pltpu.VMEM((2, 4) + item, bf16),
            pltpu.VMEM((2, 2) + item, bf16),
            pltpu.VMEM((2, CACHE + STRETCH, HEAD_DIM), bf16),
            pltpu.VMEM((2, CACHE + STRETCH, HEAD_DIM), bf16),
            pltpu.VMEM((2, 256, 1024), bf16),
            pltpu.VMEM((32, 256, 256), bf16),
            pltpu.VMEM((4, 2, 2, 2, 256, 256), bf16),
            pltpu.VMEM((256, 256), jnp.float32),
            pltpu.VMEM((2, 2, 256, 256), bf16),
            dma((5,)), dma((8,)), dma((15, 2, 2)), dma((2, 2)),
            dma((2,)), dma((2,)),
            dma((2, 2, 2)), dma((2, 2, 2)),
            dma((2, 2)), dma((2, 2)),
            dma((2, 2)), dma((2, 2)),
            dma((2, 2, 2)), dma((2, 2, 2)),
            dma((2,)), dma((2,)),
            dma((4, 2, 2, 2, 2)), dma, dma((2, 2)), dma((2,)), dma((2,)),
        ],
        compiler_params=pltpu.CompilerParams(
            collective_id=1, has_side_effects=True, vmem_limit_bytes=60 * 1024 * 1024
        ),
        cost_estimate=pl.CostEstimate(
            flops=10 << 30, bytes_accessed=8 << 20, transcendentals=2 << 20
        ),
    )(
        kept_parent,
        stored_extent,
        question_vectors,
        arriving_lookup_vectors,
        arriving_content_vectors,
        earlier_lookup_store,
        earlier_content_store,
        final_projection_matrix,
        skip_stream,
    )


def solution(mesh):
    return jax.shard_map(
        local,
        mesh=mesh,
        in_specs=(
            P("dp", None, "tensor"),
            P("dp", None, "tensor"),
            P("dp", None, "tensor"),
            P("dp", None, "tensor"),
            P("dp", None, "tensor"),
            P("dp"),
            P("dp"),
            P("tensor", "dp"),
            P("dp", "tensor"),
        ),
        out_specs=P("dp", "tensor"),
        check_vma=False,
    )
```

```python
import math

import jax
import jax.numpy as jnp
from jax import lax
from jax.experimental import pallas as pl
from jax.experimental.pallas import tpu as pltpu
from jax.sharding import PartitionSpec as P

HEAD_DIM = 128
STRETCH = 128
CACHE = 512
MESH = pl.DeviceIdType.MESH


def spots():
    dp = lax.axis_index("dp")
    core = lax.rem(dp, 2)
    chip = dp // 2
    return dp, lax.axis_index("tensor"), core, lax.rem(chip, 4), chip // 4


def beside(axis, way):
    dp, z, core, x, y = spots()
    step = 1 + 2 * way
    nx = lax.rem(x + step, 4) if axis == 0 else x
    ny = y if axis == 0 else lax.rem(y + step, 4)
    return ((ny * 4 + nx) * 2 + core, z)


def remote(src, dst, send, recv, target):
    return pltpu.make_async_remote_copy(
        src_ref=src, dst_ref=dst, send_sem=send, recv_sem=recv,
        device_id=target, device_id_type=MESH,
    )


def wait_for(ref, sem):
    pltpu.make_async_copy(ref, ref, sem).wait()


def row_table(table, dp):
    lane = lax.broadcasted_iota(jnp.int32, (32, 128), 1)
    line = lax.broadcasted_iota(jnp.int32, (32, 128), 0)

    def column(k):
        return jnp.sum(jnp.where(lane == k, table, 0), axis=1, keepdims=True)

    parents = [column(0), column(1)]
    rows = [
        jnp.sum(jnp.where(lane == line, parent, 0), axis=0, keepdims=True) for parent in parents
    ]
    result = jnp.zeros((32, 128), jnp.int32)
    low = jnp.full((1, 1), 9, jnp.int32)
    high = jnp.full((1, 1), -1, jnp.int32)
    for i in range(2):
        before = jnp.zeros((32, 1), jnp.int32)
        for row in rows:
            same = jnp.right_shift(row, 2) == jnp.right_shift(parents[i], 2)
            hit = same & (row < parents[i]) & (lane < 32)
            before += jnp.sum(jnp.where(hit, 1, 0), axis=1, keepdims=True)
        code = jnp.right_shift(parents[i], 2) * 2 + before
        result = jnp.where(lane == i, code, result)
        here = jnp.right_shift(parents[i], 2) == dp
        slot = jnp.bitwise_and(parents[i], 3)
        low = jnp.minimum(low, jnp.min(jnp.where(here, slot, 9), axis=0, keepdims=True))
        high = jnp.maximum(high, jnp.max(jnp.where(here, slot, -1), axis=0, keepdims=True))
        wanted = jnp.sum(jnp.where(line[:, :1] == dp, parents[i], 0), axis=0, keepdims=True)
        found = (lane >= 2) & (lane < 6) & (line * 4 + lane - 2 == wanted)
        extent = jnp.sum(
            jnp.sum(jnp.where(found, table, 0), axis=0, keepdims=True), axis=1, keepdims=True
        )
        result = jnp.where(lane == 4 + i, extent, result)
    result = jnp.where(lane == 2, jnp.minimum(low, 3), result)
    return jnp.where(lane == 3, jnp.maximum(high, 0), result)


NEAR = [(1, 0), (3, 0), (0, 1), (0, 3)]
DIAGONAL = [(1, 1), (1, 3), (3, 1), (3, 3)]
FAR = [(2, 0), (0, 2), (2, 1), (2, 3), (1, 2), (3, 2), (2, 2)]
PLACES = {'start': [('own a', 0), ('own b', 0)], 'gather': [], 'forward': [('far', 0)], 'select': [('side', 0)], 'relay': [], 'own': [('far side', 0), ('diagonal', 0)], 'swap': [('corner', 0)], 'row0': [('own a', 1), ('own b', 1)], 'row1': [('done', 0)]}
SERVICES = {
    (0, 1): ("side", 1),
    (1, 0): ("far", 1),
    (2, 0): ("diagonal", 1),
    (2, 1): ("far side", 1),
    (3, 1): ("corner", 1),
    (4, 0): ("done", 1),
}


def layer_kernel(
    parent_ref, extent_ref, q_hbm, new_k_hbm, new_v_hbm, k_hbm, v_hbm, own_ref, skip_hbm, out_ref,
    landing, tab_vmem, tab, w_buf, q_ref, new_k_ref, new_v_ref, k_ref, v_ref, skip_ref,
    picked, gk, gv, s1, r1, s2, r2, fin, xin, all_k, all_v,
    a_buf, s_buf, r_buf, t_buf, x_buf,
    tsem, lsem, wsem, wsend,
    psend, precv, asend, arecv, fsend, frecv, s1s, s1r, s2s, s2r, xs, xr,
    rsem, ssem, esem, xsend, xrecv,
):
    dp, z, core, x, y = spots()
    chip = dp // 2
    partner = (dp + 1 - 2 * core, z)
    barrier = pltpu.get_barrier_semaphore()

    def slot_of(place):
        return place[1] * 4 + place[0]

    def sem_of(place, half, part):
        return wsem.at[(NEAR + DIAGONAL + FAR).index(place), half, part]

    def push(source, to, first, count, axis, way, part):
        rows = pl.ds(first * 256, count * 256)
        remote(
            w_buf.at[part, slot_of(source), rows], w_buf.at[part, slot_of(to), rows],
            wsend.at[axis, way], sem_of(to, first // 2, part), beside(axis, way),
        ).start()

    def landed(place, half, part):
        wait_for(
            w_buf.at[part, slot_of(place), pl.ds(half * 512, 512)], sem_of(place, half, part)
        )

    def weights(stage, part):
        if stage == "own a":
            for way in range(2):
                push((0, 0), (1 + 2 * way, 0), 0, 2, 0, way, part)
                push((0, 0), (0, 1 + 2 * way), 2, 2, 1, way, part)
        if stage == "own b":
            for way in range(2):
                push((0, 0), (1 + 2 * way, 0), 2, 2, 0, way, part)
                push((0, 0), (0, 1 + 2 * way), 0, 2, 1, way, part)
        if stage == "side":
            for d in (1, 3):
                if part == 1:
                    landed((d, 0), 0, part)
                    landed((0, d), 1, part)
                for way in range(2):
                    push((d, 0), (d, 1 + 2 * way), 0, 2, 1, way, part)
                    push((0, d), (1 + 2 * way, d), 2, 2, 0, way, part)
        if stage == "far":
            for way in range(2):
                near = 1 + 2 * way
                if part == 0:
                    landed((near, 0), 0, part)
                    landed((0, near), 1, part)
                landed((near, 0), 1, part)
                landed((0, near), 0, part)
                push((near, 0), (2, 0), way, 1, 0, way, part)
                push((0, near), (0, 2), 2 + way, 1, 1, way, part)
                push((near, 0), (2, 0), 2 + way, 1, 0, way, part)
                push((0, near), (0, 2), way, 1, 1, way, part)
        if stage == "diagonal":
            for dx, dy in DIAGONAL:
                for half in range(2):
                    landed((dx, dy), half, part)
                push((dx, dy), (dx, 2), dy // 2, 1, 1, dy // 2, part)
                push((dx, dy), (2, dy), 2 + dx // 2, 1, 0, dx // 2, part)
        if stage == "far side":
            landed((2, 0), 0, part)
            landed((0, 2), 1, part)
            for way in range(2):
                push((2, 0), (2, 1 + 2 * way), 0, 2, 1, way, part)
                push((0, 2), (1 + 2 * way, 2), 2, 2, 0, way, part)
        if stage == "corner":
            for way in range(2):
                side = 1 + 2 * way
                landed((2, side), 0, part)
                push((2, side), (2, 2), way, 1, 1, way, part)
                landed((side, 2), 1, part)
                push((side, 2), (2, 2), 2 + way, 1, 0, way, part)
        if stage == "done":
            landed((2, 0), 1, part)
            landed((0, 2), 0, part)
            for way in range(2):
                side = 1 + 2 * way
                landed((2, side), 1, part)
                landed((side, 2), 0, part)
                landed((2, 2), way, part)

    def at_point(point):
        for stage, part in PLACES[point]:
            weights(stage, part)

    def same_core(step):
        return (lax.rem(dp + 2 * step, 32), z)

    def greet(step, carry):
        pl.semaphore_signal(barrier, inc=1, device_id=same_core(step), device_id_type=MESH)
        return carry

    lax.fori_loop(1, 16, greet, 0)
    for other in (partner, (dp, lax.rem(z + 1, 8)), (dp, lax.rem(z + 7, 8))):
        pl.semaphore_signal(barrier, inc=1, device_id=other, device_id_type=MESH)
    loads = [
        pltpu.make_async_copy(source, target, lsem.at[n])
        for n, (source, target) in enumerate(
            [
                (k_hbm, k_ref), (v_hbm, v_ref),
                (own_ref.at[:, pl.ds(0, 128)], w_buf.at[0, 0]),
                (own_ref.at[:, pl.ds(128, 128)], w_buf.at[1, 0]), (q_hbm, q_ref),
                (new_k_hbm, new_k_ref), (new_v_hbm, new_v_ref), (skip_hbm, skip_ref),
            ]
        )
    ]
    for load in loads:
        load.start()
    lane = lax.broadcasted_iota(jnp.int32, (8, 128), 1)
    numbers = jnp.zeros((8, 128), jnp.int32)
    for n in range(6):
        number = parent_ref[n] if n < 2 else extent_ref[n - 2]
        numbers = jnp.where(lane == n, number, numbers)
    landing[dp] = numbers
    loads[2].wait()
    loads[3].wait()
    pl.semaphore_wait(barrier, 18)

    beside_me = remote(landing.at[dp], landing.at[dp], tsem.at[3], tsem.at[4], partner)
    beside_me.start()
    beside_me.wait_recv()
    both_cores = landing.at[pl.ds(pl.multiple_of(chip * 2, 2), 2)]

    def share(step, carry):
        remote(both_cores, both_cores, tsem.at[0], tsem.at[1], same_core(step)).start()
        return carry

    lax.fori_loop(1, 16, share, 0)
    at_point("start")

    all_of_them = landing.at[pl.ds(0, 30)]
    wait_for(all_of_them, tsem.at[1])
    tab_vmem[...] = row_table(landing[:, 0, :], dp)
    to_scalar = pltpu.make_async_copy(tab_vmem, tab, tsem.at[2])
    to_scalar.start()
    to_scalar.wait()
    for load in loads[:2]:
        load.wait()

    stores = (k_ref, v_ref)
    gathered = (gk, gv)
    first_at = (x, y)
    second_at = (y, x)
    started = []

    def send(*args):
        started.append(remote(*args))
        started[-1].start()

    def at(kv, which, way):
        return beside(kv ^ which, way)

    mine_rows = pl.ds(pl.multiple_of(core * 256, 256), 256)
    other_rows = pl.ds(pl.multiple_of((1 - core) * 256, 256), 256)
    my_two = pl.ds(pl.multiple_of(core * 2, 2), 2)
    other_two = pl.ds(pl.multiple_of((1 - core) * 2, 2), 2)
    for kv in range(2):
        for i in range(2):
            picked[kv, i] = stores[kv][jnp.bitwise_and(tab[0, 2 + i], 3)]
            gathered[kv][first_at[kv], core * 2 + i] = picked[kv, i, mine_rows, :]
        send(
            picked.at[kv, pl.ds(0, 2), other_rows], gathered[kv].at[first_at[kv], my_two],
            psend.at[kv], precv.at[kv], partner,
        )

    def pair(kv, place, half):
        return gathered[kv].at[place, pl.ds(2 * half, 2)]

    for kv in range(2):
        wait_for(gathered[kv].at[first_at[kv], other_two], precv.at[kv])
        for turn in range(2):
            for way in range(2):
                half = turn ^ way
                block = pair(kv, first_at[kv], half)
                send(block, block, asend.at[kv, way, half], arecv.at[kv, way, half], at(kv, 0, way))
    at_point("gather")
    for kv in range(2):
        for way in range(2):
            block = pair(kv, lax.rem(first_at[kv] + (3 if way == 0 else 1), 4), way)
            wait_for(block, arecv.at[kv, way, way])
            send(block, block, fsend.at[kv, way], frecv.at[kv, way], at(kv, 0, way))
    at_point("forward")
    for kv in range(2):
        for way in range(2):
            place = lax.rem(first_at[kv] + (3 if way == 0 else 1), 4)
            wait_for(pair(kv, place, 1 - way), arecv.at[kv, way, 1 - way])
        for way in range(2):
            wait_for(pair(kv, lax.rem(first_at[kv] + 2, 4), way), frecv.at[kv, way])

    def candidate(kv, step, slot):
        to = lax.rem(second_at[kv] + step, 4)
        chip = to * 4 + x if kv == 0 else y * 4 + to
        code = tab[chip * 2 + slot // 2, slot % 2]
        rank = jnp.bitwise_and(code, 1)
        source_core = jnp.bitwise_and(jnp.right_shift(code, 1), 1)
        source_x = jnp.bitwise_and(jnp.right_shift(code, 2), 3)
        source_y = jnp.bitwise_and(jnp.right_shift(code, 4), 3)
        one, two = (source_x, source_y) if kv == 0 else (source_y, source_x)
        return gathered[kv][one, source_core * 2 + rank], two

    for kv in range(2):
        for way in range(2):
            for j in range(2):
                s1[kv, way, j] = candidate(kv, 2, 2 * way + j)[0]
            send(s1.at[kv, way], r1.at[kv, way], s1s.at[kv, way], s1r.at[kv, way], at(kv, 1, way))
    at_point("select")
    for turn in range(2):
        for kv in range(2):
            for way in range(2):
                half = 1 - way if turn == 0 else way
                if turn == 1:
                    wait_for(r1.at[kv, way], s1r.at[kv, way])
                for j in range(2):
                    slot = 2 * half + j
                    value, two = candidate(kv, 1 + 2 * way, slot)
                    if turn == 1:
                        value = jnp.where(two == second_at[kv], value, r1[kv, way, j])
                    s2[kv, way, slot] = value
                two_slots = pl.ds(2 * half, 2)
                send(
                    s2.at[kv, way, two_slots], r2.at[kv, way, two_slots],
                    s2s.at[kv, way, half], s2r.at[kv, way, half], at(kv, 1, way),
                )
        at_point("relay" if turn == 0 else "own")
    whole = (all_k, all_v)
    for load in loads[4:]:
        load.wait()
    for kv in range(2):
        for half in range(2):
            for way in range(2):
                wait_for(r2.at[kv, way, pl.ds(2 * half, 2)], s2r.at[kv, way, half])
            for j in range(2):
                slot = 2 * half + j
                value, two = candidate(kv, 0, slot)
                away = lax.rem(two - second_at[kv] + 4, 4)
                first = (away == 3) | (away == 2) if half == 0 else away == 3
                arrived = jnp.where(first, r2[kv, 0, slot], r2[kv, 1, slot])
                fin[kv, slot] = jnp.where(away == 0, value, arrived)
        send(fin.at[kv, other_two], xin.at[kv], xs.at[kv], xr.at[kv], partner)
        for i in range(2):
            whole[kv][i, mine_rows, :] = fin[kv, core * 2 + i]
            whole[kv][i, pl.ds(CACHE, STRETCH), :] = (new_k_ref, new_v_ref)[kv][i]
    at_point("swap")
    for kv in range(2):
        wait_for(xin.at[kv], xr.at[kv])
        for i in range(2):
            whole[kv][i, other_rows, :] = xin[kv, i]

    scale = 1.0 / math.sqrt(HEAD_DIM)
    span = CACHE + STRETCH
    exchange = []
    for i in range(2):
        position = lax.broadcasted_iota(jnp.int32, (2 * STRETCH, span), 1)
        token = lax.rem(lax.broadcasted_iota(jnp.int32, (2 * STRETCH, span), 0), STRETCH)
        bound = jnp.where(position < CACHE, tab[0, 4 + i], token + CACHE + 1)
        penalty = jnp.where(position < bound, 0.0, -1e30)
        tokens = pl.ds(i * STRETCH, STRETCH)

        def heads(c, carry):
            both = pl.ds(pl.multiple_of(c * 256, 256), 256)
            q = q_ref[i, :, both]
            q = jnp.concatenate([q[:, :HEAD_DIM], q[:, HEAD_DIM:]], axis=0)
            scores = lax.dot_general(
                q, all_k[i], (((1,), (1,)), ((), ())), preferred_element_type=jnp.float32
            )
            scores = scores * scale + penalty
            raised = jnp.exp(scores - jnp.max(scores, axis=1, keepdims=True))
            total = jnp.sum(raised, axis=1, keepdims=True)
            mixed = jnp.dot(
                raised.astype(jnp.bfloat16), all_v[i], preferred_element_type=jnp.float32
            )
            mixed = (mixed / total).astype(jnp.bfloat16)
            a_buf[core, tokens, both] = jnp.concatenate(
                [mixed[:STRETCH], mixed[STRETCH:]], axis=1
            )
            return carry

        lax.fori_loop(0, 4, heads, 0)
        exchange.append(
            remote(
                a_buf.at[core, tokens], a_buf.at[core, tokens],
                esem.at[0, i], esem.at[1, i], partner,
            )
        )
        exchange[-1].start()
        at_point("row%d" % i)

    def product(d, h, part):
        goal = lax.rem(z + d, 8)
        dy = lax.rem(y - goal // 2 + 4, 4)
        columns = []
        for k in range(2):
            dx = lax.rem(x - 2 * lax.rem(goal, 2) - k + 4, 4)
            columns.append(w_buf[part, dy * 4 + dx])
        return jnp.dot(
            a_buf[h], jnp.concatenate(columns, axis=1), preferred_element_type=jnp.float32
        )

    def finish(round_, owner, value):
        for k in range(2):
            columns = pl.ds(pl.multiple_of((2 * k + owner) * 256 + round_ * 128, 128), 128)
            out_ref[:, columns] = (
                skip_ref[:, columns].astype(jnp.float32)
                + value[:, k * 128 : k * 128 + 128].astype(jnp.float32)
            ).astype(jnp.bfloat16)

    def final(round_):
        def total_of(h):
            value = product(0, h, round_)
            for way, end in ((0, 3 - h), (1, 2 + h)):
                for u in range(2):
                    rows = pl.ds(u * 128, 128)
                    wait_for(
                        r_buf.at[end, round_, way, h, rows], rsem.at[end, round_, way, h, u]
                    )
                value += r_buf[end, round_, way, h].astype(jnp.float32)
            return value

        x_buf[0, round_] = total_of(1 - core).astype(jnp.bfloat16)
        remote(
            x_buf.at[0, round_], x_buf.at[1, round_], xsend.at[round_], xrecv.at[round_], partner
        ).start()
        finish(round_, core, total_of(core))

    def step(i, carry):
        round_ = i // 4
        s = lax.rem(i, 4)
        @pl.when(i == 6)
        def _():
            final(0)

        for turn in range(2):
            h = lax.rem(core + turn, 2)
            for (when, where), (stage, part) in SERVICES.items():
                if where == turn:

                    @pl.when(i == when)
                    def _():
                        weights(stage, part)

            if turn == 1:

                @pl.when(i == 0)
                def _():
                    for row in range(2):
                        rows = pl.ds(row * STRETCH, STRETCH)
                        wait_for(a_buf.at[1 - core, rows], esem.at[1, row])

            for way in range(2):
                d = 4 - s - h if way == 0 else 4 + s + 1 - h

                @pl.when((d > 0) & (d < 8))
                def _():
                    place = ((s * 2 + round_) * 2 + way) * 2 + h
                    t_buf[...] = product(d, h, round_)
                    for u in range(2):
                        rows = pl.ds(u * 128, 128)

                        @pl.when(s == 0)
                        def _():
                            s_buf[place, rows, :] = t_buf[rows, :].astype(jnp.bfloat16)

                        @pl.when(s > 0)
                        def _():
                            before = jnp.maximum(s - 1, 0)
                            wait_for(
                                r_buf.at[before, round_, way, h, rows],
                                rsem.at[before, round_, way, h, u],
                            )
                            s_buf[place, rows, :] = (
                                t_buf[rows, :]
                                + r_buf[before, round_, way, h, rows, :].astype(jnp.float32)
                            ).astype(jnp.bfloat16)

                        remote(
                            s_buf.at[place, rows], r_buf.at[s, round_, way, h, rows],
                            ssem, rsem.at[s, round_, way, h, u],
                            (dp, lax.rem(z + 1 + 6 * way, 8)),
                        ).start()
        return carry

    lax.fori_loop(0, 8, step, 0)
    final(1)
    for round_ in range(2):
        wait_for(x_buf.at[1, round_], xrecv.at[round_])
        finish(round_, 1 - core, x_buf[1, round_])
        wait_for(x_buf.at[0, round_], xsend.at[round_])
    for each in started + exchange:
        each.wait_send()
    wait_for(s_buf.at[pl.ds(0, 28)], ssem)
    wait_for(all_of_them, tsem.at[0])
    beside_me.wait_send()
    for axis in range(2):
        for way in range(2):
            wait_for(w_buf.at[0, pl.ds(0, 15), pl.ds(0, 512)], wsend.at[axis, way])


def local(
    question_vectors,
    arriving_lookup_vectors,
    arriving_content_vectors,
    earlier_lookup_store,
    earlier_content_store,
    stored_extent,
    kept_parent,
    final_projection_matrix,
    skip_stream,
):
    vmem = pl.BlockSpec(memory_space=pltpu.VMEM)
    dma = pltpu.SemaphoreType.DMA
    bf16 = jnp.bfloat16
    item = (256, 128)
    return pl.pallas_call(
        layer_kernel,
        out_shape=jax.ShapeDtypeStruct(skip_stream.shape, skip_stream.dtype),
        in_specs=[pl.BlockSpec(memory_space=pltpu.SMEM)] * 2
        + [pl.BlockSpec(memory_space=pl.ANY)] * 7,
        out_specs=vmem,
        scratch_shapes=[
            pltpu.VMEM((32, 8, 128), jnp.int32),
            pltpu.VMEM((32, 128), jnp.int32),
            pltpu.SMEM((32, 128), jnp.int32),
            pltpu.VMEM((2, 16, 1024, 128), bf16),
            pltpu.VMEM(question_vectors.shape, bf16),
            pltpu.VMEM(arriving_lookup_vectors.shape, bf16),
            pltpu.VMEM(arriving_content_vectors.shape, bf16),
            pltpu.VMEM(earlier_lookup_store.shape, bf16),
            pltpu.VMEM(earlier_content_store.shape, bf16),
            pltpu.VMEM(skip_stream.shape, bf16),
            pltpu.VMEM((2, 2, 512, 128), bf16),
            pltpu.VMEM((4, 4) + item, bf16),
            pltpu.VMEM((4, 4) + item, bf16),
            pltpu.VMEM((2, 2, 2) + item, bf16),
            pltpu.VMEM((2, 2, 2) + item, bf16),
            pltpu.VMEM((2, 2, 4) + item, bf16),
            pltpu.VMEM((2, 2, 4) + item, bf16),
            pltpu.VMEM((2, 4) + item, bf16),
            pltpu.VMEM((2, 2) + item, bf16),
            pltpu.VMEM((2, CACHE + STRETCH, HEAD_DIM), bf16),
            pltpu.VMEM((2, CACHE + STRETCH, HEAD_DIM), bf16),
            pltpu.VMEM((2, 256, 1024), bf16),
            pltpu.VMEM((32, 256, 256), bf16),
            pltpu.VMEM((4, 2, 2, 2, 256, 256), bf16),
            pltpu.VMEM((256, 256), jnp.float32),
            pltpu.VMEM((2, 2, 256, 256), bf16),
            dma((5,)), dma((8,)), dma((15, 2, 2)), dma((2, 2)),
            dma((2,)), dma((2,)),
            dma((2, 2, 2)), dma((2, 2, 2)),
            dma((2, 2)), dma((2, 2)),
            dma((2, 2)), dma((2, 2)),
            dma((2, 2, 2)), dma((2, 2, 2)),
            dma((2,)), dma((2,)),
            dma((4, 2, 2, 2, 2)), dma, dma((2, 2)), dma((2,)), dma((2,)),
        ],
        compiler_params=pltpu.CompilerParams(
            collective_id=1, has_side_effects=True, vmem_limit_bytes=60 * 1024 * 1024
        ),
        cost_estimate=pl.CostEstimate(
            flops=10 << 30, bytes_accessed=8 << 20, transcendentals=2 << 20
        ),
    )(
        kept_parent,
        stored_extent,
        question_vectors,
        arriving_lookup_vectors,
        arriving_content_vectors,
        earlier_lookup_store,
        earlier_content_store,
        final_projection_matrix,
        skip_stream,
    )


def solution(mesh):
    return jax.shard_map(
        local,
        mesh=mesh,
        in_specs=(
            P("dp", None, "tensor"),
            P("dp", None, "tensor"),
            P("dp", None, "tensor"),
            P("dp", None, "tensor"),
            P("dp", None, "tensor"),
            P("dp"),
            P("dp"),
            P("tensor", "dp"),
            P("dp", "tensor"),
        ),
        out_specs=P("dp", "tensor"),
        check_vma=False,
    )
```

```python
import math

import jax
import jax.numpy as jnp
from jax import lax
from jax.experimental import pallas as pl
from jax.experimental.pallas import tpu as pltpu
from jax.sharding import PartitionSpec as P

HEAD_DIM = 128
STRETCH = 128
CACHE = 512
MESH = pl.DeviceIdType.MESH


def spots():
    dp = lax.axis_index("dp")
    core = lax.rem(dp, 2)
    chip = dp // 2
    return dp, lax.axis_index("tensor"), core, lax.rem(chip, 4), chip // 4


def beside(axis, way):
    dp, z, core, x, y = spots()
    step = 1 + 2 * way
    nx = lax.rem(x + step, 4) if axis == 0 else x
    ny = y if axis == 0 else lax.rem(y + step, 4)
    return ((ny * 4 + nx) * 2 + core, z)


def remote(src, dst, send, recv, target):
    return pltpu.make_async_remote_copy(
        src_ref=src, dst_ref=dst, send_sem=send, recv_sem=recv,
        device_id=target, device_id_type=MESH,
    )


def wait_for(ref, sem):
    pltpu.make_async_copy(ref, ref, sem).wait()


def row_table(table, dp):
    lane = lax.broadcasted_iota(jnp.int32, (32, 128), 1)
    line = lax.broadcasted_iota(jnp.int32, (32, 128), 0)

    def column(k):
        return jnp.sum(jnp.where(lane == k, table, 0), axis=1, keepdims=True)

    parents = [column(0), column(1)]
    rows = [
        jnp.sum(jnp.where(lane == line, parent, 0), axis=0, keepdims=True) for parent in parents
    ]
    result = jnp.zeros((32, 128), jnp.int32)
    low = jnp.full((1, 1), 9, jnp.int32)
    high = jnp.full((1, 1), -1, jnp.int32)
    for i in range(2):
        before = jnp.zeros((32, 1), jnp.int32)
        for row in rows:
            same = jnp.right_shift(row, 2) == jnp.right_shift(parents[i], 2)
            hit = same & (row < parents[i]) & (lane < 32)
            before += jnp.sum(jnp.where(hit, 1, 0), axis=1, keepdims=True)
        code = jnp.right_shift(parents[i], 2) * 2 + before
        result = jnp.where(lane == i, code, result)
        here = jnp.right_shift(parents[i], 2) == dp
        slot = jnp.bitwise_and(parents[i], 3)
        low = jnp.minimum(low, jnp.min(jnp.where(here, slot, 9), axis=0, keepdims=True))
        high = jnp.maximum(high, jnp.max(jnp.where(here, slot, -1), axis=0, keepdims=True))
        wanted = jnp.sum(jnp.where(line[:, :1] == dp, parents[i], 0), axis=0, keepdims=True)
        found = (lane >= 2) & (lane < 6) & (line * 4 + lane - 2 == wanted)
        extent = jnp.sum(
            jnp.sum(jnp.where(found, table, 0), axis=0, keepdims=True), axis=1, keepdims=True
        )
        result = jnp.where(lane == 4 + i, extent, result)
    result = jnp.where(lane == 2, jnp.minimum(low, 3), result)
    return jnp.where(lane == 3, jnp.maximum(high, 0), result)


NEAR = [(1, 0), (3, 0), (0, 1), (0, 3)]
DIAGONAL = [(1, 1), (1, 3), (3, 1), (3, 3)]
FAR = [(2, 0), (0, 2), (2, 1), (2, 3), (1, 2), (3, 2), (2, 2)]
PLACES = {'start': [('own a', 0), ('own b', 0)], 'gather': [], 'forward': [('far', 0)], 'select': [('side', 0)], 'relay': [], 'own': [('far side', 0), ('diagonal', 0)], 'swap': [('corner', 0)], 'row0': [('own a', 1), ('own b', 1)], 'row1': [('done', 0)]}
SERVICES = {
    (0, 1): ("side", 1),
    (1, 0): ("far", 1),
    (2, 0): ("diagonal", 1),
    (2, 1): ("far side", 1),
    (3, 1): ("corner", 1),
    (4, 0): ("done", 1),
}


def layer_kernel(
    parent_hbm, extent_hbm, q_hbm, new_k_hbm, new_v_hbm, k_hbm, v_hbm, own_ref, skip_hbm, out_hbm,
    landing, tab_vmem, tab, w_buf, q_ref, new_k_ref, new_v_ref, k_ref, v_ref, skip_ref, parent_ref, extent_ref, out_ref, osem,
    picked, gk, gv, s1, r1, s2, r2, fin, xin, all_k, all_v,
    a_buf, s_buf, r_buf, t_buf, x_buf,
    tsem, lsem, wsem, wsend,
    psend, precv, asend, arecv, fsend, frecv, s1s, s1r, s2s, s2r, xs, xr,
    rsem, ssem, esem, xsend, xrecv,
):
    dp, z, core, x, y = spots()
    chip = dp // 2
    partner = (dp + 1 - 2 * core, z)
    barrier = pltpu.get_barrier_semaphore()

    def slot_of(place):
        return place[1] * 4 + place[0]

    def sem_of(place, half, part):
        return wsem.at[(NEAR + DIAGONAL + FAR).index(place), half, part]

    def push(source, to, first, count, axis, way, part):
        rows = pl.ds(first * 256, count * 256)
        remote(
            w_buf.at[part, slot_of(source), rows], w_buf.at[part, slot_of(to), rows],
            wsend.at[axis, way], sem_of(to, first // 2, part), beside(axis, way),
        ).start()

    def landed(place, half, part):
        wait_for(
            w_buf.at[part, slot_of(place), pl.ds(half * 512, 512)], sem_of(place, half, part)
        )

    def weights(stage, part):
        if stage == "own a":
            for way in range(2):
                push((0, 0), (1 + 2 * way, 0), 0, 2, 0, way, part)
                push((0, 0), (0, 1 + 2 * way), 2, 2, 1, way, part)
        if stage == "own b":
            for way in range(2):
                push((0, 0), (1 + 2 * way, 0), 2, 2, 0, way, part)
                push((0, 0), (0, 1 + 2 * way), 0, 2, 1, way, part)
        if stage == "side":
            for d in (1, 3):
                if part == 1:
                    landed((d, 0), 0, part)
                    landed((0, d), 1, part)
                for way in range(2):
                    push((d, 0), (d, 1 + 2 * way), 0, 2, 1, way, part)
                    push((0, d), (1 + 2 * way, d), 2, 2, 0, way, part)
        if stage == "far":
            for way in range(2):
                near = 1 + 2 * way
                if part == 0:
                    landed((near, 0), 0, part)
                    landed((0, near), 1, part)
                landed((near, 0), 1, part)
                landed((0, near), 0, part)
                push((near, 0), (2, 0), way, 1, 0, way, part)
                push((0, near), (0, 2), 2 + way, 1, 1, way, part)
                push((near, 0), (2, 0), 2 + way, 1, 0, way, part)
                push((0, near), (0, 2), way, 1, 1, way, part)
        if stage == "diagonal":
            for dx, dy in DIAGONAL:
                for half in range(2):
                    landed((dx, dy), half, part)
                push((dx, dy), (dx, 2), dy // 2, 1, 1, dy // 2, part)
                push((dx, dy), (2, dy), 2 + dx // 2, 1, 0, dx // 2, part)
        if stage == "far side":
            landed((2, 0), 0, part)
            landed((0, 2), 1, part)
            for way in range(2):
                push((2, 0), (2, 1 + 2 * way), 0, 2, 1, way, part)
                push((0, 2), (1 + 2 * way, 2), 2, 2, 0, way, part)
        if stage == "corner":
            for way in range(2):
                side = 1 + 2 * way
                landed((2, side), 0, part)
                push((2, side), (2, 2), way, 1, 1, way, part)
                landed((side, 2), 1, part)
                push((side, 2), (2, 2), 2 + way, 1, 0, way, part)
        if stage == "done":
            landed((2, 0), 1, part)
            landed((0, 2), 0, part)
            for way in range(2):
                side = 1 + 2 * way
                landed((2, side), 1, part)
                landed((side, 2), 0, part)
                landed((2, 2), way, part)

    def at_point(point):
        for stage, part in PLACES[point]:
            weights(stage, part)

    def same_core(step):
        return (lax.rem(dp + 2 * step, 32), z)

    def greet(step, carry):
        pl.semaphore_signal(barrier, inc=1, device_id=same_core(step), device_id_type=MESH)
        return carry

    lax.fori_loop(1, 16, greet, 0)
    for other in (partner, (dp, lax.rem(z + 1, 8)), (dp, lax.rem(z + 7, 8))):
        pl.semaphore_signal(barrier, inc=1, device_id=other, device_id_type=MESH)
    numbers_in = [
        pltpu.make_async_copy(parent_hbm, parent_ref, lsem.at[8]),
        pltpu.make_async_copy(extent_hbm, extent_ref, lsem.at[9]),
    ]
    for load in numbers_in:
        load.start()
    loads = [
        pltpu.make_async_copy(source, target, lsem.at[n])
        for n, (source, target) in enumerate(
            [
                (k_hbm, k_ref), (v_hbm, v_ref),
                (own_ref.at[:, pl.ds(0, 128)], w_buf.at[0, 0]),
                (own_ref.at[:, pl.ds(128, 128)], w_buf.at[1, 0]), (q_hbm, q_ref),
                (new_k_hbm, new_k_ref), (new_v_hbm, new_v_ref), (skip_hbm, skip_ref),
            ]
        )
    ]
    for load in loads:
        load.start()
    for load in numbers_in:
        load.wait()
    lane = lax.broadcasted_iota(jnp.int32, (8, 128), 1)
    numbers = jnp.zeros((8, 128), jnp.int32)
    for n in range(6):
        number = parent_ref[n] if n < 2 else extent_ref[n - 2]
        numbers = jnp.where(lane == n, number, numbers)
    landing[dp] = numbers
    loads[2].wait()
    loads[3].wait()
    pl.semaphore_wait(barrier, 18)

    beside_me = remote(landing.at[dp], landing.at[dp], tsem.at[3], tsem.at[4], partner)
    beside_me.start()
    beside_me.wait_recv()
    both_cores = landing.at[pl.ds(pl.multiple_of(chip * 2, 2), 2)]

    def share(step, carry):
        remote(both_cores, both_cores, tsem.at[0], tsem.at[1], same_core(step)).start()
        return carry

    lax.fori_loop(1, 16, share, 0)
    at_point("start")

    all_of_them = landing.at[pl.ds(0, 30)]
    wait_for(all_of_them, tsem.at[1])
    tab_vmem[...] = row_table(landing[:, 0, :], dp)
    to_scalar = pltpu.make_async_copy(tab_vmem, tab, tsem.at[2])
    to_scalar.start()
    to_scalar.wait()
    for load in loads[:2]:
        load.wait()

    stores = (k_ref, v_ref)
    gathered = (gk, gv)
    first_at = (x, y)
    second_at = (y, x)
    started = []

    def send(*args):
        started.append(remote(*args))
        started[-1].start()

    def at(kv, which, way):
        return beside(kv ^ which, way)

    mine_rows = pl.ds(pl.multiple_of(core * 256, 256), 256)
    other_rows = pl.ds(pl.multiple_of((1 - core) * 256, 256), 256)
    my_two = pl.ds(pl.multiple_of(core * 2, 2), 2)
    other_two = pl.ds(pl.multiple_of((1 - core) * 2, 2), 2)
    for kv in range(2):
        for i in range(2):
            picked[kv, i] = stores[kv][jnp.bitwise_and(tab[0, 2 + i], 3)]
            gathered[kv][first_at[kv], core * 2 + i] = picked[kv, i, mine_rows, :]
        send(
            picked.at[kv, pl.ds(0, 2), other_rows], gathered[kv].at[first_at[kv], my_two],
            psend.at[kv], precv.at[kv], partner,
        )

    def pair(kv, place, half):
        return gathered[kv].at[place, pl.ds(2 * half, 2)]

    for kv in range(2):
        wait_for(gathered[kv].at[first_at[kv], other_two], precv.at[kv])
        for turn in range(2):
            for way in range(2):
                half = turn ^ way
                block = pair(kv, first_at[kv], half)
                send(block, block, asend.at[kv, way, half], arecv.at[kv, way, half], at(kv, 0, way))
    at_point("gather")
    for kv in range(2):
        for way in range(2):
            block = pair(kv, lax.rem(first_at[kv] + (3 if way == 0 else 1), 4), way)
            wait_for(block, arecv.at[kv, way, way])
            send(block, block, fsend.at[kv, way], frecv.at[kv, way], at(kv, 0, way))
    at_point("forward")
    for kv in range(2):
        for way in range(2):
            place = lax.rem(first_at[kv] + (3 if way == 0 else 1), 4)
            wait_for(pair(kv, place, 1 - way), arecv.at[kv, way, 1 - way])
        for way in range(2):
            wait_for(pair(kv, lax.rem(first_at[kv] + 2, 4), way), frecv.at[kv, way])

    def candidate(kv, step, slot):
        to = lax.rem(second_at[kv] + step, 4)
        chip = to * 4 + x if kv == 0 else y * 4 + to
        code = tab[chip * 2 + slot // 2, slot % 2]
        rank = jnp.bitwise_and(code, 1)
        source_core = jnp.bitwise_and(jnp.right_shift(code, 1), 1)
        source_x = jnp.bitwise_and(jnp.right_shift(code, 2), 3)
        source_y = jnp.bitwise_and(jnp.right_shift(code, 4), 3)
        one, two = (source_x, source_y) if kv == 0 else (source_y, source_x)
        return gathered[kv][one, source_core * 2 + rank], two

    for kv in range(2):
        for way in range(2):
            for j in range(2):
                s1[kv, way, j] = candidate(kv, 2, 2 * way + j)[0]
            send(s1.at[kv, way], r1.at[kv, way], s1s.at[kv, way], s1r.at[kv, way], at(kv, 1, way))
    at_point("select")
    for turn in range(2):
        for kv in range(2):
            for way in range(2):
                half = 1 - way if turn == 0 else way
                if turn == 1:
                    wait_for(r1.at[kv, way], s1r.at[kv, way])
                for j in range(2):
                    slot = 2 * half + j
                    value, two = candidate(kv, 1 + 2 * way, slot)
                    if turn == 1:
                        value = jnp.where(two == second_at[kv], value, r1[kv, way, j])
                    s2[kv, way, slot] = value
                two_slots = pl.ds(2 * half, 2)
                send(
                    s2.at[kv, way, two_slots], r2.at[kv, way, two_slots],
                    s2s.at[kv, way, half], s2r.at[kv, way, half], at(kv, 1, way),
                )
        at_point("relay" if turn == 0 else "own")
    whole = (all_k, all_v)
    for load in loads[4:]:
        load.wait()
    for kv in range(2):
        for half in range(2):
            for way in range(2):
                wait_for(r2.at[kv, way, pl.ds(2 * half, 2)], s2r.at[kv, way, half])
            for j in range(2):
                slot = 2 * half + j
                value, two = candidate(kv, 0, slot)
                away = lax.rem(two - second_at[kv] + 4, 4)
                first = (away == 3) | (away == 2) if half == 0 else away == 3
                arrived = jnp.where(first, r2[kv, 0, slot], r2[kv, 1, slot])
                fin[kv, slot] = jnp.where(away == 0, value, arrived)
        send(fin.at[kv, other_two], xin.at[kv], xs.at[kv], xr.at[kv], partner)
        for i in range(2):
            whole[kv][i, mine_rows, :] = fin[kv, core * 2 + i]
            whole[kv][i, pl.ds(CACHE, STRETCH), :] = (new_k_ref, new_v_ref)[kv][i]
    at_point("swap")
    for kv in range(2):
        wait_for(xin.at[kv], xr.at[kv])
        for i in range(2):
            whole[kv][i, other_rows, :] = xin[kv, i]

    scale = 1.0 / math.sqrt(HEAD_DIM)
    span = CACHE + STRETCH
    exchange = []
    for i in range(2):
        position = lax.broadcasted_iota(jnp.int32, (2 * STRETCH, span), 1)
        token = lax.rem(lax.broadcasted_iota(jnp.int32, (2 * STRETCH, span), 0), STRETCH)
        bound = jnp.where(position < CACHE, tab[0, 4 + i], token + CACHE + 1)
        penalty = jnp.where(position < bound, 0.0, -1e30)
        tokens = pl.ds(i * STRETCH, STRETCH)

        def heads(c, carry):
            both = pl.ds(pl.multiple_of(c * 256, 256), 256)
            q = q_ref[i, :, both]
            q = jnp.concatenate([q[:, :HEAD_DIM], q[:, HEAD_DIM:]], axis=0)
            scores = lax.dot_general(
                q, all_k[i], (((1,), (1,)), ((), ())), preferred_element_type=jnp.float32
            )
            scores = scores * scale + penalty
            raised = jnp.exp(scores - jnp.max(scores, axis=1, keepdims=True))
            total = jnp.sum(raised, axis=1, keepdims=True)
            mixed = jnp.dot(
                raised.astype(jnp.bfloat16), all_v[i], preferred_element_type=jnp.float32
            )
            mixed = (mixed / total).astype(jnp.bfloat16)
            a_buf[core, tokens, both] = jnp.concatenate(
                [mixed[:STRETCH], mixed[STRETCH:]], axis=1
            )
            return carry

        lax.fori_loop(0, 4, heads, 0)
        exchange.append(
            remote(
                a_buf.at[core, tokens], a_buf.at[core, tokens],
                esem.at[0, i], esem.at[1, i], partner,
            )
        )
        exchange[-1].start()
        at_point("row%d" % i)

    def product(d, h, part):
        goal = lax.rem(z + d, 8)
        dy = lax.rem(y - goal // 2 + 4, 4)
        columns = []
        for k in range(2):
            dx = lax.rem(x - 2 * lax.rem(goal, 2) - k + 4, 4)
            columns.append(w_buf[part, dy * 4 + dx])
        return jnp.dot(
            a_buf[h], jnp.concatenate(columns, axis=1), preferred_element_type=jnp.float32
        )

    def finish(round_, owner, value):
        for k in range(2):
            columns = pl.ds(pl.multiple_of((2 * k + owner) * 256 + round_ * 128, 128), 128)
            out_ref[:, columns] = (
                skip_ref[:, columns].astype(jnp.float32)
                + value[:, k * 128 : k * 128 + 128].astype(jnp.float32)
            ).astype(jnp.bfloat16)
            pltpu.make_async_copy(
                out_ref.at[:, columns], out_hbm.at[:, columns], osem.at[round_, owner, k]
            ).start()

    def final(round_):
        def total_of(h):
            value = product(0, h, round_)
            for way, end in ((0, 3 - h), (1, 2 + h)):
                for u in range(2):
                    rows = pl.ds(u * 128, 128)
                    wait_for(
                        r_buf.at[end, round_, way, h, rows], rsem.at[end, round_, way, h, u]
                    )
                value += r_buf[end, round_, way, h].astype(jnp.float32)
            return value

        x_buf[0, round_] = total_of(1 - core).astype(jnp.bfloat16)
        remote(
            x_buf.at[0, round_], x_buf.at[1, round_], xsend.at[round_], xrecv.at[round_], partner
        ).start()
        finish(round_, core, total_of(core))

    def step(i, carry):
        round_ = i // 4
        s = lax.rem(i, 4)
        @pl.when(i == 6)
        def _():
            final(0)

        for turn in range(2):
            h = lax.rem(core + turn, 2)
            for (when, where), (stage, part) in SERVICES.items():
                if where == turn:

                    @pl.when(i == when)
                    def _():
                        weights(stage, part)

            if turn == 1:

                @pl.when(i == 0)
                def _():
                    for row in range(2):
                        rows = pl.ds(row * STRETCH, STRETCH)
                        wait_for(a_buf.at[1 - core, rows], esem.at[1, row])

            for way in range(2):
                d = 4 - s - h if way == 0 else 4 + s + 1 - h

                @pl.when((d > 0) & (d < 8))
                def _():
                    place = ((s * 2 + round_) * 2 + way) * 2 + h
                    t_buf[...] = product(d, h, round_)
                    for u in range(2):
                        rows = pl.ds(u * 128, 128)

                        @pl.when(s == 0)
                        def _():
                            s_buf[place, rows, :] = t_buf[rows, :].astype(jnp.bfloat16)

                        @pl.when(s > 0)
                        def _():
                            before = jnp.maximum(s - 1, 0)
                            wait_for(
                                r_buf.at[before, round_, way, h, rows],
                                rsem.at[before, round_, way, h, u],
                            )
                            s_buf[place, rows, :] = (
                                t_buf[rows, :]
                                + r_buf[before, round_, way, h, rows, :].astype(jnp.float32)
                            ).astype(jnp.bfloat16)

                        remote(
                            s_buf.at[place, rows], r_buf.at[s, round_, way, h, rows],
                            ssem, rsem.at[s, round_, way, h, u],
                            (dp, lax.rem(z + 1 + 6 * way, 8)),
                        ).start()
        return carry

    lax.fori_loop(0, 8, step, 0)

    def theirs(round_):
        wait_for(x_buf.at[1, round_], xrecv.at[round_])
        finish(round_, 1 - core, x_buf[1, round_])
        wait_for(x_buf.at[0, round_], xsend.at[round_])

    theirs(0)
    final(1)
    theirs(1)
    for round_ in range(2):
        for owner in range(2):
            for k in range(2):
                piece = pl.ds((2 * k + owner) * 256 + round_ * 128, 128)
                pltpu.make_async_copy(
                    out_ref.at[:, piece], out_hbm.at[:, piece], osem.at[round_, owner, k]
                ).wait()
    for each in started + exchange:
        each.wait_send()
    wait_for(s_buf.at[pl.ds(0, 28)], ssem)
    wait_for(all_of_them, tsem.at[0])
    beside_me.wait_send()
    for axis in range(2):
        for way in range(2):
            wait_for(w_buf.at[0, pl.ds(0, 15), pl.ds(0, 512)], wsend.at[axis, way])


def local(
    question_vectors,
    arriving_lookup_vectors,
    arriving_content_vectors,
    earlier_lookup_store,
    earlier_content_store,
    stored_extent,
    kept_parent,
    final_projection_matrix,
    skip_stream,
):
    dma = pltpu.SemaphoreType.DMA
    bf16 = jnp.bfloat16
    item = (256, 128)
    return pl.pallas_call(
        layer_kernel,
        out_shape=jax.ShapeDtypeStruct(skip_stream.shape, skip_stream.dtype),
        in_specs=[pl.BlockSpec(memory_space=pl.ANY)] * 9,
        out_specs=pl.BlockSpec(memory_space=pl.ANY),
        scratch_shapes=[
            pltpu.VMEM((32, 8, 128), jnp.int32),
            pltpu.VMEM((32, 128), jnp.int32),
            pltpu.SMEM((32, 128), jnp.int32),
            pltpu.VMEM((2, 16, 1024, 128), bf16),
            pltpu.VMEM(question_vectors.shape, bf16),
            pltpu.VMEM(arriving_lookup_vectors.shape, bf16),
            pltpu.VMEM(arriving_content_vectors.shape, bf16),
            pltpu.VMEM(earlier_lookup_store.shape, bf16),
            pltpu.VMEM(earlier_content_store.shape, bf16),
            pltpu.VMEM(skip_stream.shape, bf16),
            pltpu.SMEM(kept_parent.shape, jnp.int32),
            pltpu.SMEM(stored_extent.shape, jnp.int32),
            pltpu.VMEM(skip_stream.shape, bf16),
            dma((2, 2, 2)),
            pltpu.VMEM((2, 2, 512, 128), bf16),
            pltpu.VMEM((4, 4) + item, bf16),
            pltpu.VMEM((4, 4) + item, bf16),
            pltpu.VMEM((2, 2, 2) + item, bf16),
            pltpu.VMEM((2, 2, 2) + item, bf16),
            pltpu.VMEM((2, 2, 4) + item, bf16),
            pltpu.VMEM((2, 2, 4) + item, bf16),
            pltpu.VMEM((2, 4) + item, bf16),
            pltpu.VMEM((2, 2) + item, bf16),
            pltpu.VMEM((2, CACHE + STRETCH, HEAD_DIM), bf16),
            pltpu.VMEM((2, CACHE + STRETCH, HEAD_DIM), bf16),
            pltpu.VMEM((2, 256, 1024), bf16),
            pltpu.VMEM((32, 256, 256), bf16),
            pltpu.VMEM((4, 2, 2, 2, 256, 256), bf16),
            pltpu.VMEM((256, 256), jnp.float32),
            pltpu.VMEM((2, 2, 256, 256), bf16),
            dma((5,)), dma((10,)), dma((15, 2, 2)), dma((2, 2)),
            dma((2,)), dma((2,)),
            dma((2, 2, 2)), dma((2, 2, 2)),
            dma((2, 2)), dma((2, 2)),
            dma((2, 2)), dma((2, 2)),
            dma((2, 2, 2)), dma((2, 2, 2)),
            dma((2,)), dma((2,)),
            dma((4, 2, 2, 2, 2)), dma, dma((2, 2)), dma((2,)), dma((2,)),
        ],
        compiler_params=pltpu.CompilerParams(
            collective_id=1, has_side_effects=True, vmem_limit_bytes=60 * 1024 * 1024
        ),
        cost_estimate=pl.CostEstimate(
            flops=10 << 30, bytes_accessed=8 << 20, transcendentals=2 << 20
        ),
    )(
        kept_parent,
        stored_extent,
        question_vectors,
        arriving_lookup_vectors,
        arriving_content_vectors,
        earlier_lookup_store,
        earlier_content_store,
        final_projection_matrix,
        skip_stream,
    )


def solution(mesh):
    return jax.shard_map(
        local,
        mesh=mesh,
        in_specs=(
            P("dp", None, "tensor"),
            P("dp", None, "tensor"),
            P("dp", None, "tensor"),
            P("dp", None, "tensor"),
            P("dp", None, "tensor"),
            P("dp"),
            P("dp"),
            P("tensor", "dp"),
            P("dp", "tensor"),
        ),
        out_specs=P("dp", "tensor"),
        check_vma=False,
    )
```

```python
import math

import jax
import jax.numpy as jnp
from jax import lax
from jax.experimental import pallas as pl
from jax.experimental.pallas import tpu as pltpu
from jax.sharding import PartitionSpec as P

HEAD_DIM = 128
STRETCH = 128
CACHE = 512
MESH = pl.DeviceIdType.MESH


def spots():
    dp = lax.axis_index("dp")
    core = lax.rem(dp, 2)
    chip = dp // 2
    return dp, lax.axis_index("tensor"), core, lax.rem(chip, 4), chip // 4


def beside(axis, way):
    dp, z, core, x, y = spots()
    step = 1 + 2 * way
    nx = lax.rem(x + step, 4) if axis == 0 else x
    ny = y if axis == 0 else lax.rem(y + step, 4)
    return ((ny * 4 + nx) * 2 + core, z)


def remote(src, dst, send, recv, target):
    return pltpu.make_async_remote_copy(
        src_ref=src, dst_ref=dst, send_sem=send, recv_sem=recv,
        device_id=target, device_id_type=MESH,
    )


def wait_for(ref, sem):
    pltpu.make_async_copy(ref, ref, sem).wait()


def row_table(table, dp):
    lane = lax.broadcasted_iota(jnp.int32, (32, 128), 1)
    line = lax.broadcasted_iota(jnp.int32, (32, 128), 0)

    def column(k):
        return jnp.sum(jnp.where(lane == k, table, 0), axis=1, keepdims=True)

    parents = [column(0), column(1)]
    rows = [
        jnp.sum(jnp.where(lane == line, parent, 0), axis=0, keepdims=True) for parent in parents
    ]
    result = jnp.zeros((32, 128), jnp.int32)
    low = jnp.full((1, 1), 9, jnp.int32)
    high = jnp.full((1, 1), -1, jnp.int32)
    for i in range(2):
        before = jnp.zeros((32, 1), jnp.int32)
        for row in rows:
            same = jnp.right_shift(row, 2) == jnp.right_shift(parents[i], 2)
            hit = same & (row < parents[i]) & (lane < 32)
            before += jnp.sum(jnp.where(hit, 1, 0), axis=1, keepdims=True)
        code = jnp.right_shift(parents[i], 2) * 2 + before
        result = jnp.where(lane == i, code, result)
        here = jnp.right_shift(parents[i], 2) == dp
        slot = jnp.bitwise_and(parents[i], 3)
        low = jnp.minimum(low, jnp.min(jnp.where(here, slot, 9), axis=0, keepdims=True))
        high = jnp.maximum(high, jnp.max(jnp.where(here, slot, -1), axis=0, keepdims=True))
        wanted = jnp.sum(jnp.where(line[:, :1] == dp, parents[i], 0), axis=0, keepdims=True)
        found = (lane >= 2) & (lane < 6) & (line * 4 + lane - 2 == wanted)
        extent = jnp.sum(
            jnp.sum(jnp.where(found, table, 0), axis=0, keepdims=True), axis=1, keepdims=True
        )
        result = jnp.where(lane == 4 + i, extent, result)
    result = jnp.where(lane == 2, jnp.minimum(low, 3), result)
    return jnp.where(lane == 3, jnp.maximum(high, 0), result)


NEAR = [(1, 0), (3, 0), (0, 1), (0, 3)]
DIAGONAL = [(1, 1), (1, 3), (3, 1), (3, 3)]
FAR = [(2, 0), (0, 2), (2, 1), (2, 3), (1, 2), (3, 2), (2, 2)]
PLACES = {'start': [('own a', 0), ('own b', 0)], 'gather': [], 'forward': [('far', 0)], 'select': [('side', 0)], 'relay': [], 'own': [('far side', 0), ('diagonal', 0)], 'swap': [('corner', 0)], 'row0': [('own a', 1), ('own b', 1)], 'row1': [('done', 0)]}
SERVICES = {
    (0, 1): ("side", 1),
    (1, 0): ("far", 1),
    (2, 0): ("diagonal", 1),
    (2, 1): ("far side", 1),
    (3, 1): ("corner", 1),
    (4, 0): ("done", 1),
}


def layer_kernel(
    parent_hbm, extent_hbm, q_hbm, new_k_hbm, new_v_hbm, k_hbm, v_hbm, own_ref, skip_hbm, out_hbm,
    landing, tab_vmem, tab, w_buf, q_ref, new_k_ref, new_v_ref, k_ref, v_ref, skip_ref, parent_ref, extent_ref, out_ref, osem,
    picked, gk, gv, s1, r1, s2, r2, fin, xin, all_k, all_v,
    a_buf, s_buf, r_buf, t_buf, x_buf,
    tsem, lsem, wsem, wsend,
    psend, precv, asend, arecv, fsend, frecv, s1s, s1r, s2s, s2r, xs, xr,
    rsem, ssem, esem, xsend, xrecv,
):
    dp, z, core, x, y = spots()
    chip = dp // 2
    partner = (dp + 1 - 2 * core, z)
    barrier = pltpu.get_barrier_semaphore()

    def slot_of(place):
        return place[1] * 4 + place[0]

    def sem_of(place, half, part):
        return wsem.at[(NEAR + DIAGONAL + FAR).index(place), half, part]

    def push(source, to, first, count, axis, way, part):
        rows = pl.ds(first * 256, count * 256)
        remote(
            w_buf.at[part, slot_of(source), rows], w_buf.at[part, slot_of(to), rows],
            wsend.at[axis, way], sem_of(to, first // 2, part), beside(axis, way),
        ).start()

    def landed(place, half, part):
        wait_for(
            w_buf.at[part, slot_of(place), pl.ds(half * 512, 512)], sem_of(place, half, part)
        )

    def weights(stage, part):
        if stage == "own a":
            for way in range(2):
                push((0, 0), (1 + 2 * way, 0), 0, 2, 0, way, part)
                push((0, 0), (0, 1 + 2 * way), 2, 2, 1, way, part)
        if stage == "own b":
            for way in range(2):
                push((0, 0), (1 + 2 * way, 0), 2, 2, 0, way, part)
                push((0, 0), (0, 1 + 2 * way), 0, 2, 1, way, part)
        if stage == "side":
            for d in (1, 3):
                if part == 1:
                    landed((d, 0), 0, part)
                    landed((0, d), 1, part)
                for way in range(2):
                    push((d, 0), (d, 1 + 2 * way), 0, 2, 1, way, part)
                    push((0, d), (1 + 2 * way, d), 2, 2, 0, way, part)
        if stage == "far":
            for way in range(2):
                near = 1 + 2 * way
                if part == 0:
                    landed((near, 0), 0, part)
                    landed((0, near), 1, part)
                landed((near, 0), 1, part)
                landed((0, near), 0, part)
                push((near, 0), (2, 0), way, 1, 0, way, part)
                push((0, near), (0, 2), 2 + way, 1, 1, way, part)
                push((near, 0), (2, 0), 2 + way, 1, 0, way, part)
                push((0, near), (0, 2), way, 1, 1, way, part)
        if stage == "diagonal":
            for dx, dy in DIAGONAL:
                for half in range(2):
                    landed((dx, dy), half, part)
                push((dx, dy), (dx, 2), dy // 2, 1, 1, dy // 2, part)
                push((dx, dy), (2, dy), 2 + dx // 2, 1, 0, dx // 2, part)
        if stage == "far side":
            landed((2, 0), 0, part)
            landed((0, 2), 1, part)
            for way in range(2):
                push((2, 0), (2, 1 + 2 * way), 0, 2, 1, way, part)
                push((0, 2), (1 + 2 * way, 2), 2, 2, 0, way, part)
        if stage == "corner":
            for way in range(2):
                side = 1 + 2 * way
                landed((2, side), 0, part)
                push((2, side), (2, 2), way, 1, 1, way, part)
                landed((side, 2), 1, part)
                push((side, 2), (2, 2), 2 + way, 1, 0, way, part)
        if stage == "done":
            landed((2, 0), 1, part)
            landed((0, 2), 0, part)
            for way in range(2):
                side = 1 + 2 * way
                landed((2, side), 1, part)
                landed((side, 2), 0, part)
                landed((2, 2), way, part)

    def at_point(point):
        for stage, part in PLACES[point]:
            weights(stage, part)

    def same_core(step):
        return (lax.rem(dp + 2 * step, 32), z)

    def greet(step, carry):
        pl.semaphore_signal(barrier, inc=1, device_id=same_core(step), device_id_type=MESH)
        return carry

    for step in range(1, 16):
        greet(step, 0)
    for other in (partner, (dp, lax.rem(z + 1, 8)), (dp, lax.rem(z + 7, 8))):
        pl.semaphore_signal(barrier, inc=1, device_id=other, device_id_type=MESH)
    numbers_in = [
        pltpu.make_async_copy(parent_hbm, parent_ref, lsem.at[8]),
        pltpu.make_async_copy(extent_hbm, extent_ref, lsem.at[9]),
    ]
    for load in numbers_in:
        load.start()
    loads = [
        pltpu.make_async_copy(source, target, lsem.at[n])
        for n, (source, target) in enumerate(
            [
                (k_hbm, k_ref), (v_hbm, v_ref),
                (own_ref.at[:, pl.ds(0, 128)], w_buf.at[0, 0]),
                (own_ref.at[:, pl.ds(128, 128)], w_buf.at[1, 0]), (q_hbm, q_ref),
                (new_k_hbm, new_k_ref), (new_v_hbm, new_v_ref), (skip_hbm, skip_ref),
            ]
        )
    ]
    for load in loads:
        load.start()
    for load in numbers_in:
        load.wait()
    lane = lax.broadcasted_iota(jnp.int32, (8, 128), 1)
    numbers = jnp.zeros((8, 128), jnp.int32)
    for n in range(6):
        number = parent_ref[n] if n < 2 else extent_ref[n - 2]
        numbers = jnp.where(lane == n, number, numbers)
    landing[dp] = numbers
    loads[2].wait()
    loads[3].wait()
    pl.semaphore_wait(barrier, 18)

    beside_me = remote(landing.at[dp], landing.at[dp], tsem.at[3], tsem.at[4], partner)
    beside_me.start()
    beside_me.wait_recv()
    both_cores = landing.at[pl.ds(pl.multiple_of(chip * 2, 2), 2)]

    def share(step, carry):
        remote(both_cores, both_cores, tsem.at[0], tsem.at[1], same_core(step)).start()
        return carry

    for step in range(1, 16):
        share(step, 0)
    at_point("start")

    all_of_them = landing.at[pl.ds(0, 30)]
    wait_for(all_of_them, tsem.at[1])
    tab_vmem[...] = row_table(landing[:, 0, :], dp)
    to_scalar = pltpu.make_async_copy(tab_vmem, tab, tsem.at[2])
    to_scalar.start()
    to_scalar.wait()
    for load in loads[:2]:
        load.wait()

    stores = (k_ref, v_ref)
    gathered = (gk, gv)
    first_at = (x, y)
    second_at = (y, x)
    started = []

    def send(*args):
        started.append(remote(*args))
        started[-1].start()

    def at(kv, which, way):
        return beside(kv ^ which, way)

    mine_rows = pl.ds(pl.multiple_of(core * 256, 256), 256)
    other_rows = pl.ds(pl.multiple_of((1 - core) * 256, 256), 256)
    my_two = pl.ds(pl.multiple_of(core * 2, 2), 2)
    other_two = pl.ds(pl.multiple_of((1 - core) * 2, 2), 2)
    for kv in range(2):
        for i in range(2):
            picked[kv, i] = stores[kv][jnp.bitwise_and(tab[0, 2 + i], 3)]
            gathered[kv][first_at[kv], core * 2 + i] = picked[kv, i, mine_rows, :]
        send(
            picked.at[kv, pl.ds(0, 2), other_rows], gathered[kv].at[first_at[kv], my_two],
            psend.at[kv], precv.at[kv], partner,
        )

    def pair(kv, place, half):
        return gathered[kv].at[place, pl.ds(2 * half, 2)]

    for kv in range(2):
        wait_for(gathered[kv].at[first_at[kv], other_two], precv.at[kv])
        for turn in range(2):
            for way in range(2):
                half = turn ^ way
                block = pair(kv, first_at[kv], half)
                send(block, block, asend.at[kv, way, half], arecv.at[kv, way, half], at(kv, 0, way))
    at_point("gather")
    for kv in range(2):
        for way in range(2):
            block = pair(kv, lax.rem(first_at[kv] + (3 if way == 0 else 1), 4), way)
            wait_for(block, arecv.at[kv, way, way])
            send(block, block, fsend.at[kv, way], frecv.at[kv, way], at(kv, 0, way))
    at_point("forward")
    for kv in range(2):
        for way in range(2):
            place = lax.rem(first_at[kv] + (3 if way == 0 else 1), 4)
            wait_for(pair(kv, place, 1 - way), arecv.at[kv, way, 1 - way])
        for way in range(2):
            wait_for(pair(kv, lax.rem(first_at[kv] + 2, 4), way), frecv.at[kv, way])

    def candidate(kv, step, slot):
        to = lax.rem(second_at[kv] + step, 4)
        chip = to * 4 + x if kv == 0 else y * 4 + to
        code = tab[chip * 2 + slot // 2, slot % 2]
        rank = jnp.bitwise_and(code, 1)
        source_core = jnp.bitwise_and(jnp.right_shift(code, 1), 1)
        source_x = jnp.bitwise_and(jnp.right_shift(code, 2), 3)
        source_y = jnp.bitwise_and(jnp.right_shift(code, 4), 3)
        one, two = (source_x, source_y) if kv == 0 else (source_y, source_x)
        return gathered[kv][one, source_core * 2 + rank], two

    for kv in range(2):
        for way in range(2):
            for j in range(2):
                s1[kv, way, j] = candidate(kv, 2, 2 * way + j)[0]
            send(s1.at[kv, way], r1.at[kv, way], s1s.at[kv, way], s1r.at[kv, way], at(kv, 1, way))
    at_point("select")
    for turn in range(2):
        for kv in range(2):
            for way in range(2):
                half = 1 - way if turn == 0 else way
                if turn == 1:
                    wait_for(r1.at[kv, way], s1r.at[kv, way])
                for j in range(2):
                    slot = 2 * half + j
                    value, two = candidate(kv, 1 + 2 * way, slot)
                    if turn == 1:
                        value = jnp.where(two == second_at[kv], value, r1[kv, way, j])
                    s2[kv, way, slot] = value
                two_slots = pl.ds(2 * half, 2)
                send(
                    s2.at[kv, way, two_slots], r2.at[kv, way, two_slots],
                    s2s.at[kv, way, half], s2r.at[kv, way, half], at(kv, 1, way),
                )
        at_point("relay" if turn == 0 else "own")
    whole = (all_k, all_v)
    for load in loads[4:]:
        load.wait()
    for kv in range(2):
        for half in range(2):
            for way in range(2):
                wait_for(r2.at[kv, way, pl.ds(2 * half, 2)], s2r.at[kv, way, half])
            for j in range(2):
                slot = 2 * half + j
                value, two = candidate(kv, 0, slot)
                away = lax.rem(two - second_at[kv] + 4, 4)
                first = (away == 3) | (away == 2) if half == 0 else away == 3
                arrived = jnp.where(first, r2[kv, 0, slot], r2[kv, 1, slot])
                fin[kv, slot] = jnp.where(away == 0, value, arrived)
        send(fin.at[kv, other_two], xin.at[kv], xs.at[kv], xr.at[kv], partner)
        for i in range(2):
            whole[kv][i, mine_rows, :] = fin[kv, core * 2 + i]
            whole[kv][i, pl.ds(CACHE, STRETCH), :] = (new_k_ref, new_v_ref)[kv][i]
    at_point("swap")
    for kv in range(2):
        wait_for(xin.at[kv], xr.at[kv])
        for i in range(2):
            whole[kv][i, other_rows, :] = xin[kv, i]

    scale = 1.0 / math.sqrt(HEAD_DIM)
    span = CACHE + STRETCH
    exchange = []
    for i in range(2):
        position = lax.broadcasted_iota(jnp.int32, (2 * STRETCH, span), 1)
        token = lax.rem(lax.broadcasted_iota(jnp.int32, (2 * STRETCH, span), 0), STRETCH)
        bound = jnp.where(position < CACHE, tab[0, 4 + i], token + CACHE + 1)
        penalty = jnp.where(position < bound, 0.0, -1e30)
        tokens = pl.ds(i * STRETCH, STRETCH)

        def heads(c, carry):
            both = pl.ds(pl.multiple_of(c * 256, 256), 256)
            q = q_ref[i, :, both]
            q = jnp.concatenate([q[:, :HEAD_DIM], q[:, HEAD_DIM:]], axis=0)
            scores = lax.dot_general(
                q, all_k[i], (((1,), (1,)), ((), ())), preferred_element_type=jnp.float32
            )
            scores = scores * scale + penalty
            raised = jnp.exp(scores - jnp.max(scores, axis=1, keepdims=True))
            total = jnp.sum(raised, axis=1, keepdims=True)
            mixed = jnp.dot(
                raised.astype(jnp.bfloat16), all_v[i], preferred_element_type=jnp.float32
            )
            mixed = (mixed / total).astype(jnp.bfloat16)
            a_buf[core, tokens, both] = jnp.concatenate(
                [mixed[:STRETCH], mixed[STRETCH:]], axis=1
            )
            return carry

        lax.fori_loop(0, 4, heads, 0)
        exchange.append(
            remote(
                a_buf.at[core, tokens], a_buf.at[core, tokens],
                esem.at[0, i], esem.at[1, i], partner,
            )
        )
        exchange[-1].start()
        at_point("row%d" % i)

    def product(d, h, part):
        goal = lax.rem(z + d, 8)
        dy = lax.rem(y - goal // 2 + 4, 4)
        columns = []
        for k in range(2):
            dx = lax.rem(x - 2 * lax.rem(goal, 2) - k + 4, 4)
            columns.append(w_buf[part, dy * 4 + dx])
        return jnp.dot(
            a_buf[h], jnp.concatenate(columns, axis=1), preferred_element_type=jnp.float32
        )

    def finish(round_, owner, value):
        for k in range(2):
            columns = pl.ds(pl.multiple_of((2 * k + owner) * 256 + round_ * 128, 128), 128)
            out_ref[:, columns] = (
                skip_ref[:, columns].astype(jnp.float32)
                + value[:, k * 128 : k * 128 + 128].astype(jnp.float32)
            ).astype(jnp.bfloat16)
            pltpu.make_async_copy(
                out_ref.at[:, columns], out_hbm.at[:, columns], osem.at[round_, owner, k]
            ).start()

    def final(round_):
        def total_of(h):
            value = product(0, h, round_)
            for way, end in ((0, 3 - h), (1, 2 + h)):
                for u in range(2):
                    rows = pl.ds(u * 128, 128)
                    wait_for(
                        r_buf.at[end, round_, way, h, rows], rsem.at[end, round_, way, h, u]
                    )
                value += r_buf[end, round_, way, h].astype(jnp.float32)
            return value

        x_buf[0, round_] = total_of(1 - core).astype(jnp.bfloat16)
        remote(
            x_buf.at[0, round_], x_buf.at[1, round_], xsend.at[round_], xrecv.at[round_], partner
        ).start()
        finish(round_, core, total_of(core))

    def step(i, carry):
        round_ = i // 4
        s = lax.rem(i, 4)
        @pl.when(i == 6)
        def _():
            final(0)

        for turn in range(2):
            h = lax.rem(core + turn + round_, 2)
            for (when, where), (stage, part) in SERVICES.items():
                if where == turn:

                    @pl.when(i == when)
                    def _():
                        weights(stage, part)

            if turn == 1:

                @pl.when(i == 0)
                def _():
                    for row in range(2):
                        rows = pl.ds(row * STRETCH, STRETCH)
                        wait_for(a_buf.at[1 - core, rows], esem.at[1, row])

            for way in range(2):
                d = 4 - s - h if way == 0 else 4 + s + 1 - h

                @pl.when((d > 0) & (d < 8))
                def _():
                    place = ((s * 2 + round_) * 2 + way) * 2 + h
                    t_buf[...] = product(d, h, round_)
                    for u in range(2):
                        rows = pl.ds(u * 128, 128)

                        @pl.when(s == 0)
                        def _():
                            s_buf[place, rows, :] = t_buf[rows, :].astype(jnp.bfloat16)

                        @pl.when(s > 0)
                        def _():
                            before = jnp.maximum(s - 1, 0)
                            wait_for(
                                r_buf.at[before, round_, way, h, rows],
                                rsem.at[before, round_, way, h, u],
                            )
                            s_buf[place, rows, :] = (
                                t_buf[rows, :]
                                + r_buf[before, round_, way, h, rows, :].astype(jnp.float32)
                            ).astype(jnp.bfloat16)

                        remote(
                            s_buf.at[place, rows], r_buf.at[s, round_, way, h, rows],
                            ssem, rsem.at[s, round_, way, h, u],
                            (dp, lax.rem(z + 1 + 6 * way, 8)),
                        ).start()
        return carry

    lax.fori_loop(0, 8, step, 0)

    def theirs(round_):
        wait_for(x_buf.at[1, round_], xrecv.at[round_])
        finish(round_, 1 - core, x_buf[1, round_])
        wait_for(x_buf.at[0, round_], xsend.at[round_])

    theirs(0)
    final(1)
    theirs(1)
    for round_ in range(2):
        for owner in range(2):
            for k in range(2):
                piece = pl.ds((2 * k + owner) * 256 + round_ * 128, 128)
                pltpu.make_async_copy(
                    out_ref.at[:, piece], out_hbm.at[:, piece], osem.at[round_, owner, k]
                ).wait()
    for each in started + exchange:
        each.wait_send()
    wait_for(s_buf.at[pl.ds(0, 28)], ssem)
    wait_for(all_of_them, tsem.at[0])
    beside_me.wait_send()
    for axis in range(2):
        for way in range(2):
            wait_for(w_buf.at[0, pl.ds(0, 15), pl.ds(0, 512)], wsend.at[axis, way])


def local(
    question_vectors,
    arriving_lookup_vectors,
    arriving_content_vectors,
    earlier_lookup_store,
    earlier_content_store,
    stored_extent,
    kept_parent,
    final_projection_matrix,
    skip_stream,
):
    dma = pltpu.SemaphoreType.DMA
    bf16 = jnp.bfloat16
    item = (256, 128)
    return pl.pallas_call(
        layer_kernel,
        out_shape=jax.ShapeDtypeStruct(skip_stream.shape, skip_stream.dtype),
        in_specs=[pl.BlockSpec(memory_space=pl.ANY)] * 9,
        out_specs=pl.BlockSpec(memory_space=pl.ANY),
        scratch_shapes=[
            pltpu.VMEM((32, 8, 128), jnp.int32),
            pltpu.VMEM((32, 128), jnp.int32),
            pltpu.SMEM((32, 128), jnp.int32),
            pltpu.VMEM((2, 16, 1024, 128), bf16),
            pltpu.VMEM(question_vectors.shape, bf16),
            pltpu.VMEM(arriving_lookup_vectors.shape, bf16),
            pltpu.VMEM(arriving_content_vectors.shape, bf16),
            pltpu.VMEM(earlier_lookup_store.shape, bf16),
            pltpu.VMEM(earlier_content_store.shape, bf16),
            pltpu.VMEM(skip_stream.shape, bf16),
            pltpu.SMEM(kept_parent.shape, jnp.int32),
            pltpu.SMEM(stored_extent.shape, jnp.int32),
            pltpu.VMEM(skip_stream.shape, bf16),
            dma((2, 2, 2)),
            pltpu.VMEM((2, 2, 512, 128), bf16),
            pltpu.VMEM((4, 4) + item, bf16),
            pltpu.VMEM((4, 4) + item, bf16),
            pltpu.VMEM((2, 2, 2) + item, bf16),
            pltpu.VMEM((2, 2, 2) + item, bf16),
            pltpu.VMEM((2, 2, 4) + item, bf16),
            pltpu.VMEM((2, 2, 4) + item, bf16),
            pltpu.VMEM((2, 4) + item, bf16),
            pltpu.VMEM((2, 2) + item, bf16),
            pltpu.VMEM((2, CACHE + STRETCH, HEAD_DIM), bf16),
            pltpu.VMEM((2, CACHE + STRETCH, HEAD_DIM), bf16),
            pltpu.VMEM((2, 256, 1024), bf16),
            pltpu.VMEM((32, 256, 256), bf16),
            pltpu.VMEM((4, 2, 2, 2, 256, 256), bf16),
            pltpu.VMEM((256, 256), jnp.float32),
            pltpu.VMEM((2, 2, 256, 256), bf16),
            dma((5,)), dma((10,)), dma((15, 2, 2)), dma((2, 2)),
            dma((2,)), dma((2,)),
            dma((2, 2, 2)), dma((2, 2, 2)),
            dma((2, 2)), dma((2, 2)),
            dma((2, 2)), dma((2, 2)),
            dma((2, 2, 2)), dma((2, 2, 2)),
            dma((2,)), dma((2,)),
            dma((4, 2, 2, 2, 2)), dma, dma((2, 2)), dma((2,)), dma((2,)),
        ],
        compiler_params=pltpu.CompilerParams(
            collective_id=1, has_side_effects=True, vmem_limit_bytes=60 * 1024 * 1024
        ),
        cost_estimate=pl.CostEstimate(
            flops=10 << 30, bytes_accessed=8 << 20, transcendentals=2 << 20
        ),
    )(
        kept_parent,
        stored_extent,
        question_vectors,
        arriving_lookup_vectors,
        arriving_content_vectors,
        earlier_lookup_store,
        earlier_content_store,
        final_projection_matrix,
        skip_stream,
    )


def solution(mesh):
    return jax.shard_map(
        local,
        mesh=mesh,
        in_specs=(
            P("dp", None, "tensor"),
            P("dp", None, "tensor"),
            P("dp", None, "tensor"),
            P("dp", None, "tensor"),
            P("dp", None, "tensor"),
            P("dp"),
            P("dp"),
            P("tensor", "dp"),
            P("dp", "tensor"),
        ),
        out_specs=P("dp", "tensor"),
        check_vma=False,
    )
```

```python
import math

import jax
import jax.numpy as jnp
from jax import lax
from jax.experimental import pallas as pl
from jax.experimental.pallas import tpu as pltpu
from jax.sharding import PartitionSpec as P

HEAD_DIM = 128
STRETCH = 128
CACHE = 512
MESH = pl.DeviceIdType.MESH


def spots():
    dp = lax.axis_index("dp")
    core = lax.rem(dp, 2)
    chip = dp // 2
    return dp, lax.axis_index("tensor"), core, lax.rem(chip, 4), chip // 4


def beside(axis, way):
    dp, z, core, x, y = spots()
    step = 1 + 2 * way
    nx = lax.rem(x + step, 4) if axis == 0 else x
    ny = y if axis == 0 else lax.rem(y + step, 4)
    return ((ny * 4 + nx) * 2 + core, z)


def remote(src, dst, send, recv, target):
    return pltpu.make_async_remote_copy(
        src_ref=src, dst_ref=dst, send_sem=send, recv_sem=recv,
        device_id=target, device_id_type=MESH,
    )


def wait_for(ref, sem):
    pltpu.make_async_copy(ref, ref, sem).wait()


def row_length(table, dp, i):
    lane = lax.broadcasted_iota(jnp.int32, (32, 128), 1)
    line = lax.broadcasted_iota(jnp.int32, (32, 128), 0)
    wanted = jnp.where((line == dp) & (lane == i), table, 0)
    wanted = jnp.sum(jnp.sum(wanted, axis=0, keepdims=True), axis=1, keepdims=True)
    found = (lane >= 2) & (lane < 6) & (line * 4 + lane - 2 == wanted)
    found = jnp.sum(jnp.where(found, table, 0), axis=0, keepdims=True)
    return jnp.sum(found, axis=1, keepdims=True)


def row_table(table, dp):
    lane = lax.broadcasted_iota(jnp.int32, (32, 128), 1)
    line = lax.broadcasted_iota(jnp.int32, (32, 128), 0)

    def column(k):
        return jnp.sum(jnp.where(lane == k, table, 0), axis=1, keepdims=True)

    parents = [column(0), column(1)]
    rows = [
        jnp.sum(jnp.where(lane == line, parent, 0), axis=0, keepdims=True) for parent in parents
    ]
    result = jnp.zeros((32, 128), jnp.int32)
    low = jnp.full((1, 1), 9, jnp.int32)
    high = jnp.full((1, 1), -1, jnp.int32)
    for i in range(2):
        before = jnp.zeros((32, 1), jnp.int32)
        for row in rows:
            same = jnp.right_shift(row, 2) == jnp.right_shift(parents[i], 2)
            hit = same & (row < parents[i]) & (lane < 32)
            before += jnp.sum(jnp.where(hit, 1, 0), axis=1, keepdims=True)
        code = jnp.right_shift(parents[i], 2) * 2 + before
        result = jnp.where(lane == i, code, result)
        here = jnp.right_shift(parents[i], 2) == dp
        slot = jnp.bitwise_and(parents[i], 3)
        low = jnp.minimum(low, jnp.min(jnp.where(here, slot, 9), axis=0, keepdims=True))
        high = jnp.maximum(high, jnp.max(jnp.where(here, slot, -1), axis=0, keepdims=True))
    result = jnp.where(lane == 2, jnp.minimum(low, 3), result)
    return jnp.where(lane == 3, jnp.maximum(high, 0), result)


NEAR = [(1, 0), (3, 0), (0, 1), (0, 3)]
DIAGONAL = [(1, 1), (1, 3), (3, 1), (3, 3)]
FAR = [(2, 0), (0, 2), (2, 1), (2, 3), (1, 2), (3, 2), (2, 2)]
PLACES = {'start': [('own a', 0), ('own b', 0)], 'gather': [], 'forward': [('far', 0)], 'select': [('side', 0)], 'relay': [], 'own': [('far side', 0), ('diagonal', 0)], 'swap': [('corner', 0)], 'row0': [('own a', 1), ('own b', 1)], 'row1': [('done', 0)]}
SERVICES = {
    (0, 1): ("side", 1),
    (1, 0): ("far", 1),
    (2, 0): ("diagonal", 1),
    (2, 1): ("far side", 1),
    (3, 1): ("corner", 1),
    (4, 0): ("done", 1),
}


def layer_kernel(
    parent_hbm, extent_hbm, q_hbm, new_k_hbm, new_v_hbm, k_hbm, v_hbm, own_ref, skip_hbm, out_hbm,
    landing, tab_vmem, tab, w_buf, q_ref, new_k_ref, new_v_ref, k_ref, v_ref, skip_ref, parent_ref, extent_ref, out_ref, osem,
    picked, gk, gv, s1, r1, s2, r2, fin, xin, all_k, all_v,
    a_buf, s_buf, r_buf, t_buf, x_buf,
    tsem, lsem, wsem, wsend,
    psend, precv, asend, arecv, fsend, frecv, s1s, s1r, s2s, s2r, xs, xr,
    rsem, ssem, esem, xsend, xrecv,
):
    dp, z, core, x, y = spots()
    chip = dp // 2
    partner = (dp + 1 - 2 * core, z)
    barrier = pltpu.get_barrier_semaphore()

    def slot_of(place):
        return place[1] * 4 + place[0]

    def sem_of(place, half, part):
        return wsem.at[(NEAR + DIAGONAL + FAR).index(place), half, part]

    def push(source, to, first, count, axis, way, part):
        rows = pl.ds(first * 256, count * 256)
        remote(
            w_buf.at[part, slot_of(source), rows], w_buf.at[part, slot_of(to), rows],
            wsend.at[axis, way], sem_of(to, first // 2, part), beside(axis, way),
        ).start()

    def landed(place, half, part):
        wait_for(
            w_buf.at[part, slot_of(place), pl.ds(half * 512, 512)], sem_of(place, half, part)
        )

    def weights(stage, part):
        if stage == "own a":
            for way in range(2):
                push((0, 0), (1 + 2 * way, 0), 0, 2, 0, way, part)
                push((0, 0), (0, 1 + 2 * way), 2, 2, 1, way, part)
        if stage == "own b":
            for way in range(2):
                push((0, 0), (1 + 2 * way, 0), 2, 2, 0, way, part)
                push((0, 0), (0, 1 + 2 * way), 0, 2, 1, way, part)
        if stage == "side":
            for d in (1, 3):
                if part == 1:
                    landed((d, 0), 0, part)
                    landed((0, d), 1, part)
                for way in range(2):
                    push((d, 0), (d, 1 + 2 * way), 0, 2, 1, way, part)
                    push((0, d), (1 + 2 * way, d), 2, 2, 0, way, part)
        if stage == "far":
            for way in range(2):
                near = 1 + 2 * way
                if part == 0:
                    landed((near, 0), 0, part)
                    landed((0, near), 1, part)
                landed((near, 0), 1, part)
                landed((0, near), 0, part)
                push((near, 0), (2, 0), way, 1, 0, way, part)
                push((0, near), (0, 2), 2 + way, 1, 1, way, part)
                push((near, 0), (2, 0), 2 + way, 1, 0, way, part)
                push((0, near), (0, 2), way, 1, 1, way, part)
        if stage == "diagonal":
            for dx, dy in DIAGONAL:
                for half in range(2):
                    landed((dx, dy), half, part)
                push((dx, dy), (dx, 2), dy // 2, 1, 1, dy // 2, part)
                push((dx, dy), (2, dy), 2 + dx // 2, 1, 0, dx // 2, part)
        if stage == "far side":
            landed((2, 0), 0, part)
            landed((0, 2), 1, part)
            for way in range(2):
                push((2, 0), (2, 1 + 2 * way), 0, 2, 1, way, part)
                push((0, 2), (1 + 2 * way, 2), 2, 2, 0, way, part)
        if stage == "corner":
            for way in range(2):
                side = 1 + 2 * way
                landed((2, side), 0, part)
                push((2, side), (2, 2), way, 1, 1, way, part)
                landed((side, 2), 1, part)
                push((side, 2), (2, 2), 2 + way, 1, 0, way, part)
        if stage == "done":
            landed((2, 0), 1, part)
            landed((0, 2), 0, part)
            for way in range(2):
                side = 1 + 2 * way
                landed((2, side), 1, part)
                landed((side, 2), 0, part)
                landed((2, 2), way, part)

    def at_point(point):
        for stage, part in PLACES[point]:
            weights(stage, part)

    def same_core(step):
        return (lax.rem(dp + 2 * step, 32), z)

    def greet(step, carry):
        pl.semaphore_signal(barrier, inc=1, device_id=same_core(step), device_id_type=MESH)
        return carry

    lax.fori_loop(1, 16, greet, 0)
    for other in (partner, (dp, lax.rem(z + 1, 8)), (dp, lax.rem(z + 7, 8))):
        pl.semaphore_signal(barrier, inc=1, device_id=other, device_id_type=MESH)
    numbers_in = [
        pltpu.make_async_copy(parent_hbm, parent_ref, lsem.at[8]),
        pltpu.make_async_copy(extent_hbm, extent_ref, lsem.at[9]),
    ]
    for load in numbers_in:
        load.start()
    loads = [
        pltpu.make_async_copy(source, target, lsem.at[n])
        for n, (source, target) in enumerate(
            [
                (k_hbm, k_ref), (v_hbm, v_ref),
                (own_ref.at[:, pl.ds(0, 128)], w_buf.at[0, 0]),
                (own_ref.at[:, pl.ds(128, 128)], w_buf.at[1, 0]), (q_hbm, q_ref),
                (new_k_hbm, new_k_ref), (new_v_hbm, new_v_ref), (skip_hbm, skip_ref),
            ]
        )
    ]
    for load in loads:
        load.start()
    for load in numbers_in:
        load.wait()
    lane = lax.broadcasted_iota(jnp.int32, (8, 128), 1)
    numbers = jnp.zeros((8, 128), jnp.int32)
    for n in range(6):
        number = parent_ref[n] if n < 2 else extent_ref[n - 2]
        numbers = jnp.where(lane == n, number, numbers)
    landing[dp] = numbers
    loads[2].wait()
    loads[3].wait()
    pl.semaphore_wait(barrier, 18)

    beside_me = remote(landing.at[dp], landing.at[dp], tsem.at[3], tsem.at[4], partner)
    beside_me.start()
    beside_me.wait_recv()
    both_cores = landing.at[pl.ds(pl.multiple_of(chip * 2, 2), 2)]

    def share(step, carry):
        remote(both_cores, both_cores, tsem.at[0], tsem.at[1], same_core(step)).start()
        return carry

    lax.fori_loop(1, 16, share, 0)
    at_point("start")

    all_of_them = landing.at[pl.ds(0, 30)]
    wait_for(all_of_them, tsem.at[1])
    tab_vmem[...] = row_table(landing[:, 0, :], dp)
    to_scalar = pltpu.make_async_copy(tab_vmem, tab, tsem.at[2])
    to_scalar.start()
    to_scalar.wait()
    for load in loads[:2]:
        load.wait()

    stores = (k_ref, v_ref)
    gathered = (gk, gv)
    first_at = (x, y)
    second_at = (y, x)
    started = []

    def send(*args):
        started.append(remote(*args))
        started[-1].start()

    def at(kv, which, way):
        return beside(kv ^ which, way)

    mine_rows = pl.ds(pl.multiple_of(core * 256, 256), 256)
    other_rows = pl.ds(pl.multiple_of((1 - core) * 256, 256), 256)
    my_two = pl.ds(pl.multiple_of(core * 2, 2), 2)
    other_two = pl.ds(pl.multiple_of((1 - core) * 2, 2), 2)
    for kv in range(2):
        for i in range(2):
            picked[kv, i] = stores[kv][jnp.bitwise_and(tab[0, 2 + i], 3)]
            gathered[kv][first_at[kv], core * 2 + i] = picked[kv, i, mine_rows, :]
        send(
            picked.at[kv, pl.ds(0, 2), other_rows], gathered[kv].at[first_at[kv], my_two],
            psend.at[kv], precv.at[kv], partner,
        )

    def pair(kv, place, half):
        return gathered[kv].at[place, pl.ds(2 * half, 2)]

    for kv in range(2):
        wait_for(gathered[kv].at[first_at[kv], other_two], precv.at[kv])
        for turn in range(2):
            for way in range(2):
                half = turn ^ way
                block = pair(kv, first_at[kv], half)
                send(block, block, asend.at[kv, way, half], arecv.at[kv, way, half], at(kv, 0, way))
    at_point("gather")
    for kv in range(2):
        for way in range(2):
            block = pair(kv, lax.rem(first_at[kv] + (3 if way == 0 else 1), 4), way)
            wait_for(block, arecv.at[kv, way, way])
            send(block, block, fsend.at[kv, way], frecv.at[kv, way], at(kv, 0, way))
    at_point("forward")
    for kv in range(2):
        for way in range(2):
            place = lax.rem(first_at[kv] + (3 if way == 0 else 1), 4)
            wait_for(pair(kv, place, 1 - way), arecv.at[kv, way, 1 - way])
        for way in range(2):
            wait_for(pair(kv, lax.rem(first_at[kv] + 2, 4), way), frecv.at[kv, way])

    def candidate(kv, step, slot):
        to = lax.rem(second_at[kv] + step, 4)
        chip = to * 4 + x if kv == 0 else y * 4 + to
        code = tab[chip * 2 + slot // 2, slot % 2]
        rank = jnp.bitwise_and(code, 1)
        source_core = jnp.bitwise_and(jnp.right_shift(code, 1), 1)
        source_x = jnp.bitwise_and(jnp.right_shift(code, 2), 3)
        source_y = jnp.bitwise_and(jnp.right_shift(code, 4), 3)
        one, two = (source_x, source_y) if kv == 0 else (source_y, source_x)
        return gathered[kv][one, source_core * 2 + rank], two

    for kv in range(2):
        for way in range(2):
            for j in range(2):
                s1[kv, way, j] = candidate(kv, 2, 2 * way + j)[0]
            send(s1.at[kv, way], r1.at[kv, way], s1s.at[kv, way], s1r.at[kv, way], at(kv, 1, way))
    at_point("select")
    for turn in range(2):
        for kv in range(2):
            for way in range(2):
                half = 1 - way if turn == 0 else way
                if turn == 1:
                    wait_for(r1.at[kv, way], s1r.at[kv, way])
                for j in range(2):
                    slot = 2 * half + j
                    value, two = candidate(kv, 1 + 2 * way, slot)
                    if turn == 1:
                        value = jnp.where(two == second_at[kv], value, r1[kv, way, j])
                    s2[kv, way, slot] = value
                two_slots = pl.ds(2 * half, 2)
                send(
                    s2.at[kv, way, two_slots], r2.at[kv, way, two_slots],
                    s2s.at[kv, way, half], s2r.at[kv, way, half], at(kv, 1, way),
                )
        at_point("relay" if turn == 0 else "own")
    whole = (all_k, all_v)
    for load in loads[4:]:
        load.wait()
    for kv in range(2):
        for half in range(2):
            for way in range(2):
                wait_for(r2.at[kv, way, pl.ds(2 * half, 2)], s2r.at[kv, way, half])
            for j in range(2):
                slot = 2 * half + j
                value, two = candidate(kv, 0, slot)
                away = lax.rem(two - second_at[kv] + 4, 4)
                first = (away == 3) | (away == 2) if half == 0 else away == 3
                arrived = jnp.where(first, r2[kv, 0, slot], r2[kv, 1, slot])
                fin[kv, slot] = jnp.where(away == 0, value, arrived)
        send(fin.at[kv, other_two], xin.at[kv], xs.at[kv], xr.at[kv], partner)
        for i in range(2):
            whole[kv][i, mine_rows, :] = fin[kv, core * 2 + i]
            whole[kv][i, pl.ds(CACHE, STRETCH), :] = (new_k_ref, new_v_ref)[kv][i]
    at_point("swap")
    for kv in range(2):
        wait_for(xin.at[kv], xr.at[kv])
        for i in range(2):
            whole[kv][i, other_rows, :] = xin[kv, i]

    scale = 1.0 / math.sqrt(HEAD_DIM)
    span = CACHE + STRETCH
    exchange = []
    for i in range(2):
        position = lax.broadcasted_iota(jnp.int32, (2 * STRETCH, span), 1)
        token = lax.rem(lax.broadcasted_iota(jnp.int32, (2 * STRETCH, span), 0), STRETCH)
        bound = jnp.where(position < CACHE, row_length(landing[:, 0, :], dp, i), token + CACHE + 1)
        penalty = jnp.where(position < bound, 0.0, -1e30)
        tokens = pl.ds(i * STRETCH, STRETCH)

        def heads(c, carry):
            both = pl.ds(pl.multiple_of(c * 256, 256), 256)
            q = q_ref[i, :, both]
            q = jnp.concatenate([q[:, :HEAD_DIM], q[:, HEAD_DIM:]], axis=0)
            scores = lax.dot_general(
                q, all_k[i], (((1,), (1,)), ((), ())), preferred_element_type=jnp.float32
            )
            scores = scores * scale + penalty
            raised = jnp.exp(scores - jnp.max(scores, axis=1, keepdims=True))
            total = jnp.sum(raised, axis=1, keepdims=True)
            mixed = jnp.dot(
                raised.astype(jnp.bfloat16), all_v[i], preferred_element_type=jnp.float32
            )
            mixed = (mixed / total).astype(jnp.bfloat16)
            a_buf[core, tokens, both] = jnp.concatenate(
                [mixed[:STRETCH], mixed[STRETCH:]], axis=1
            )
            return carry

        lax.fori_loop(0, 4, heads, 0)
        exchange.append(
            remote(
                a_buf.at[core, tokens], a_buf.at[core, tokens],
                esem.at[0, i], esem.at[1, i], partner,
            )
        )
        exchange[-1].start()
        at_point("row%d" % i)

    def product(d, h, part):
        goal = lax.rem(z + d, 8)
        dy = lax.rem(y - goal // 2 + 4, 4)
        columns = []
        for k in range(2):
            dx = lax.rem(x - 2 * lax.rem(goal, 2) - k + 4, 4)
            columns.append(w_buf[part, dy * 4 + dx])
        return jnp.dot(
            a_buf[h], jnp.concatenate(columns, axis=1), preferred_element_type=jnp.float32
        )

    def finish(round_, owner, value):
        for k in range(2):
            columns = pl.ds(pl.multiple_of((2 * k + owner) * 256 + round_ * 128, 128), 128)
            out_ref[:, columns] = (
                skip_ref[:, columns].astype(jnp.float32)
                + value[:, k * 128 : k * 128 + 128].astype(jnp.float32)
            ).astype(jnp.bfloat16)
            pltpu.make_async_copy(
                out_ref.at[:, columns], out_hbm.at[:, columns], osem.at[round_, owner, k]
            ).start()

    def final(round_):
        def total_of(h):
            value = product(0, h, round_)
            for way, end in ((0, 3 - h), (1, 2 + h)):
                for u in range(2):
                    rows = pl.ds(u * 128, 128)
                    wait_for(
                        r_buf.at[end, round_, way, h, rows], rsem.at[end, round_, way, h, u]
                    )
                value += r_buf[end, round_, way, h].astype(jnp.float32)
            return value

        x_buf[0, round_] = total_of(1 - core).astype(jnp.bfloat16)
        remote(
            x_buf.at[0, round_], x_buf.at[1, round_], xsend.at[round_], xrecv.at[round_], partner
        ).start()
        finish(round_, core, total_of(core))

    def step(i, carry):
        round_ = i // 4
        s = lax.rem(i, 4)
        @pl.when(i == 6)
        def _():
            final(0)

        for turn in range(2):
            h = lax.rem(core + turn, 2)
            for (when, where), (stage, part) in SERVICES.items():
                if where == turn:

                    @pl.when(i == when)
                    def _():
                        weights(stage, part)

            if turn == 1:

                @pl.when(i == 0)
                def _():
                    for row in range(2):
                        rows = pl.ds(row * STRETCH, STRETCH)
                        wait_for(a_buf.at[1 - core, rows], esem.at[1, row])

            for way in range(2):
                d = 4 - s - h if way == 0 else 4 + s + 1 - h

                @pl.when((d > 0) & (d < 8))
                def _():
                    place = ((s * 2 + round_) * 2 + way) * 2 + h
                    t_buf[...] = product(d, h, round_)
                    for u in range(2):
                        rows = pl.ds(u * 128, 128)

                        @pl.when(s == 0)
                        def _():
                            s_buf[place, rows, :] = t_buf[rows, :].astype(jnp.bfloat16)

                        @pl.when(s > 0)
                        def _():
                            before = jnp.maximum(s - 1, 0)
                            wait_for(
                                r_buf.at[before, round_, way, h, rows],
                                rsem.at[before, round_, way, h, u],
                            )
                            s_buf[place, rows, :] = (
                                t_buf[rows, :]
                                + r_buf[before, round_, way, h, rows, :].astype(jnp.float32)
                            ).astype(jnp.bfloat16)

                        remote(
                            s_buf.at[place, rows], r_buf.at[s, round_, way, h, rows],
                            ssem, rsem.at[s, round_, way, h, u],
                            (dp, lax.rem(z + 1 + 6 * way, 8)),
                        ).start()
        return carry

    lax.fori_loop(0, 8, step, 0)

    def theirs(round_):
        wait_for(x_buf.at[1, round_], xrecv.at[round_])
        finish(round_, 1 - core, x_buf[1, round_])
        wait_for(x_buf.at[0, round_], xsend.at[round_])

    theirs(0)
    final(1)
    theirs(1)
    for round_ in range(2):
        for owner in range(2):
            for k in range(2):
                piece = pl.ds((2 * k + owner) * 256 + round_ * 128, 128)
                pltpu.make_async_copy(
                    out_ref.at[:, piece], out_hbm.at[:, piece], osem.at[round_, owner, k]
                ).wait()
    for each in started + exchange:
        each.wait_send()
    wait_for(s_buf.at[pl.ds(0, 28)], ssem)
    wait_for(all_of_them, tsem.at[0])
    beside_me.wait_send()
    for axis in range(2):
        for way in range(2):
            wait_for(w_buf.at[0, pl.ds(0, 15), pl.ds(0, 512)], wsend.at[axis, way])


def local(
    question_vectors,
    arriving_lookup_vectors,
    arriving_content_vectors,
    earlier_lookup_store,
    earlier_content_store,
    stored_extent,
    kept_parent,
    final_projection_matrix,
    skip_stream,
):
    dma = pltpu.SemaphoreType.DMA
    bf16 = jnp.bfloat16
    item = (256, 128)
    return pl.pallas_call(
        layer_kernel,
        out_shape=jax.ShapeDtypeStruct(skip_stream.shape, skip_stream.dtype),
        in_specs=[pl.BlockSpec(memory_space=pl.ANY)] * 9,
        out_specs=pl.BlockSpec(memory_space=pl.ANY),
        scratch_shapes=[
            pltpu.VMEM((32, 8, 128), jnp.int32),
            pltpu.VMEM((32, 128), jnp.int32),
            pltpu.SMEM((32, 128), jnp.int32),
            pltpu.VMEM((2, 16, 1024, 128), bf16),
            pltpu.VMEM(question_vectors.shape, bf16),
            pltpu.VMEM(arriving_lookup_vectors.shape, bf16),
            pltpu.VMEM(arriving_content_vectors.shape, bf16),
            pltpu.VMEM(earlier_lookup_store.shape, bf16),
            pltpu.VMEM(earlier_content_store.shape, bf16),
            pltpu.VMEM(skip_stream.shape, bf16),
            pltpu.SMEM(kept_parent.shape, jnp.int32),
            pltpu.SMEM(stored_extent.shape, jnp.int32),
            pltpu.VMEM(skip_stream.shape, bf16),
            dma((2, 2, 2)),
            pltpu.VMEM((2, 2, 512, 128), bf16),
            pltpu.VMEM((4, 4) + item, bf16),
            pltpu.VMEM((4, 4) + item, bf16),
            pltpu.VMEM((2, 2, 2) + item, bf16),
            pltpu.VMEM((2, 2, 2) + item, bf16),
            pltpu.VMEM((2, 2, 4) + item, bf16),
            pltpu.VMEM((2, 2, 4) + item, bf16),
            pltpu.VMEM((2, 4) + item, bf16),
            pltpu.VMEM((2, 2) + item, bf16),
            pltpu.VMEM((2, CACHE + STRETCH, HEAD_DIM), bf16),
            pltpu.VMEM((2, CACHE + STRETCH, HEAD_DIM), bf16),
            pltpu.VMEM((2, 256, 1024), bf16),
            pltpu.VMEM((32, 256, 256), bf16),
            pltpu.VMEM((4, 2, 2, 2, 256, 256), bf16),
            pltpu.VMEM((256, 256), jnp.float32),
            pltpu.VMEM((2, 2, 256, 256), bf16),
            dma((5,)), dma((10,)), dma((15, 2, 2)), dma((2, 2)),
            dma((2,)), dma((2,)),
            dma((2, 2, 2)), dma((2, 2, 2)),
            dma((2, 2)), dma((2, 2)),
            dma((2, 2)), dma((2, 2)),
            dma((2, 2, 2)), dma((2, 2, 2)),
            dma((2,)), dma((2,)),
            dma((4, 2, 2, 2, 2)), dma, dma((2, 2)), dma((2,)), dma((2,)),
        ],
        compiler_params=pltpu.CompilerParams(
            collective_id=1, has_side_effects=True, vmem_limit_bytes=60 * 1024 * 1024
        ),
        cost_estimate=pl.CostEstimate(
            flops=10 << 30, bytes_accessed=8 << 20, transcendentals=2 << 20
        ),
    )(
        kept_parent,
        stored_extent,
        question_vectors,
        arriving_lookup_vectors,
        arriving_content_vectors,
        earlier_lookup_store,
        earlier_content_store,
        final_projection_matrix,
        skip_stream,
    )


def solution(mesh):
    return jax.shard_map(
        local,
        mesh=mesh,
        in_specs=(
            P("dp", None, "tensor"),
            P("dp", None, "tensor"),
            P("dp", None, "tensor"),
            P("dp", None, "tensor"),
            P("dp", None, "tensor"),
            P("dp"),
            P("dp"),
            P("tensor", "dp"),
            P("dp", "tensor"),
        ),
        out_specs=P("dp", "tensor"),
        check_vma=False,
    )
```
